32 devices in a mesh: gx: 4 (over y, core), gy: 2 (over x), layer: 4 (over z).
Axes of the slice: x: 2, y: 2, z: 4, core: 2. Of those that a mesh axis runs over, the one named last changes fastest.
Arguments:
- source: float32 [3, 32, 32, 512], P(None, 'layer', 'gy', 'gx'), may hold values from -6 to 6
- active_cells: int32 [32, 32, 512], P('layer', 'gy', 'gx'), may hold values 0 or 1
- diag_blocks: float32 [9, 32, 32, 512], P(None, 'layer', 'gy', 'gx'), may hold values from -0.45 to 3, as said below
- frozen_inverses: float32 [9, 32, 32, 512], P(None, 'layer', 'gy', 'gx'), may hold values from -0.05 to 0.2, as said below
- transmissibility: float32 [3, 32, 32, 512], P(None, 'layer', 'gy', 'gx'), may hold values from 0.1 to 1
- pressure_weights: float32 [3, 32, 32, 512], P(None, 'layer', 'gy', 'gx'), may hold values from 1 to 4
- stencil_fine: float32 [7, 32, 32, 512], P(None, 'layer', 'gy', 'gx'), may hold values from -1 to 9, as said below
- coarse_one: float32 [7, 16, 16, 256], P(None, 'layer', 'gy', 'gx'), may hold values from -1 to 9, as said below
- coarse_two: float32 [7, 8, 8, 128], P(None, 'layer', 'gy', 'gx'), may hold values from -1 to 9, as said below
- coarse_three: float32 [7, 4, 4, 64], P(None, 'layer', 'gy', 'gx'), may hold values from -1 to 9, as said below
- pressure_state: float32 [32, 32, 512], P('layer', 'gy', 'gx'), may hold values from -6 to 6
- mobilities: float32 [3, 32, 32, 512], P(None, 'layer', 'gy', 'gx'), may hold values from 0.1 to 1
Outputs:
- adjoint: float32 [3, 32, 32, 512], P(None, 'layer', 'gy', 'gx')
- perm_grad: float32 [3, 32, 32, 512], P(None, 'layer', 'gy', 'gx')
The draws below stay inside these ranges and needn't reach their ends.
Inputs may be any that keep to these rules, and one draw needn't show every extreme that they name: `diag_blocks`: entries 0, 4 and 8 are the blocks' diagonals. `frozen_inverses`: entries 0, 4 and 8 are the blocks' diagonals. `stencil_fine`: coefficient 0 exceeds the sum of the magnitudes of the other six. `coarse_one`: coefficient 0 exceeds the sum of the magnitudes of the other six. `coarse_two`: coefficient 0 exceeds the sum of the magnitudes of the other six. `coarse_three`: coefficient 0 exceeds the sum of the magnitudes of the other six.
All inputs are finite; a program needn't handle non-finite values. No bound on the sum of `active_cells` on one device may be relied on, other than what follows from the above.
Results may differ from the reference program's by a relative error of at most 0.00002.
Values sent between devices are 32-bit elements; how exact they have to be, the bound alone decides.
No kernel may reach another device: no remote copies, remote signals or barrier semaphores. Data moves between devices by JAX's collectives and lax.ppermute only.
A program may use at most 64 MiB of HBM per device.

```python
import math
import jax
import jax.numpy as jnp

SWEEPS = 3
LEVELS = 3
COARSE_SWEEPS = 4
NX = 512
NY = 32
NZ = 32


def block_draw(key, diag_low, diag_span, coupling_most, coupling_scale):
    extent = (9, NZ, NY, NX)
    first, second = jax.random.split(jax.random.fold_in(key, 11))
    on_diag = (jnp.arange(9) % 4 == 0).reshape(9, 1, 1, 1)
    diagonal = diag_low + diag_span * jax.random.uniform(first, extent, jnp.float32)
    coupling = jnp.clip(coupling_scale * jax.random.normal(second, extent, jnp.float32), -coupling_most, coupling_most)
    return jnp.where(on_diag, diagonal, coupling)


def draw_diag_blocks(key, part):
    return block_draw(key, 1.0, 2.0, 0.45, 0.15)


def draw_frozen_inverses(key, part):
    return block_draw(key, 0.1, 0.1, 0.05, 0.02)


def stencil_draw(key, extent):
    first, second = jax.random.split(jax.random.fold_in(key, 23))
    center_draw = jax.random.uniform(first, (1,) + extent, jnp.float32)
    coupling_draw = jax.random.uniform(second, (6,) + extent, jnp.float32)
    center = 6.5 + 2.5 * center_draw
    coupling = -(0.2 + 0.8 * coupling_draw)
    return jnp.concatenate([center, coupling])


def draw_stencil_fine(key, part):
    return stencil_draw(key, (NZ, NY, NX))


def draw_coarse_one(key, part):
    return stencil_draw(key, (NZ // 2, NY // 2, NX // 2))


def draw_coarse_two(key, part):
    return stencil_draw(key, (NZ // 4, NY // 4, NX // 4))


def draw_coarse_three(key, part):
    return stencil_draw(key, (NZ // 8, NY // 8, NX // 8))


def plant(drawn, stream_key, smallest, largest):
    dims = drawn.shape
    place = [jax.random.randint(jax.random.fold_in(stream_key, axis), (), 0, dims[axis]) for axis in range(len(dims))]
    drawn = drawn.at[tuple(place)].set(smallest)
    longest = dims.index(max(dims))
    place[longest] = (place[longest] + 1) % dims[longest]
    return drawn.at[tuple(place)].set(largest)


def levels(rng, shape, cuts, smallest, high):
    level, own = 1.0, jax.random.fold_in(rng, 6)
    for axis_at, blocks in cuts:
        steps = jnp.exp(jax.random.uniform(jax.random.fold_in(own, axis_at), (blocks,), jnp.float32, smallest / len(cuts), high / len(cuts)))
        level = level * jnp.repeat(steps, shape[axis_at] // blocks).reshape([-1 if axis == axis_at else 1 for axis in range(len(shape))])
    return level


def bell_draw(key, shape, spread, most, cuts=(), dtype=jnp.bfloat16):
    factor_of = levels(key, shape, cuts, -0.22, 0.18) if cuts else 1.0
    drawn = jax.random.normal(key, shape, jnp.float32) * spread * factor_of
    return jnp.minimum(jnp.maximum(drawn, -most), most).astype(dtype)


def setup_inputs(seed: int = 0) -> dict:
    keys = jax.random.split(jax.random.key(seed), 13)
    return {
        "source": bell_draw(keys[0], (3, NZ, NY, NX), 1.0, 6.0, ((1, 4), (2, 2), (3, 4)), jnp.float32),
        "active_cells": plant((jax.random.randint(keys[1], (NZ, NY, NX), 0, 10) < 9).astype(jnp.int32), jax.random.fold_in(keys[1], 1), 0, 1),
        "diag_blocks": draw_diag_blocks(jax.random.fold_in(keys[12], 71), 0),
        "frozen_inverses": draw_frozen_inverses(jax.random.fold_in(keys[12], 71), 0),
        "transmissibility": jnp.clip(jnp.exp(math.log(1.0) - 2.3025851 * jax.random.uniform(keys[4], (3, NZ, NY, NX), jnp.float32) ** levels(keys[4], (3, NZ, NY, NX), ((1, 4), (2, 2), (3, 4)), -0.2, 0.2)), 0.1, 1.0),
        "pressure_weights": jnp.clip(1.0 + 3.0 * jax.random.uniform(keys[5], (3, NZ, NY, NX), jnp.float32) ** levels(keys[5], (3, NZ, NY, NX), ((1, 4), (2, 2), (3, 4)), -0.2, 0.2), 1.0, 4.0),
        "stencil_fine": draw_stencil_fine(jax.random.fold_in(keys[12], 71), 0),
        "coarse_one": draw_coarse_one(jax.random.fold_in(keys[12], 71), 0),
        "coarse_two": draw_coarse_two(jax.random.fold_in(keys[12], 71), 0),
        "coarse_three": draw_coarse_three(jax.random.fold_in(keys[12], 71), 0),
        "pressure_state": bell_draw(keys[10], (NZ, NY, NX), 1.0, 6.0, ((0, 4), (1, 2), (2, 4)), jnp.float32),
        "mobilities": jnp.clip(jnp.exp(math.log(1.0) - 2.3025851 * jax.random.uniform(keys[11], (3, NZ, NY, NX), jnp.float32) ** levels(keys[11], (3, NZ, NY, NX), ((1, 4), (2, 2), (3, 4)), -0.2, 0.2)), 0.1, 1.0),
    }


OMEGA = 0.8


def leading(field):
    return (slice(None),) * (field.ndim - 3)


def padded_zero(field):
    widths = [(0, 0)] * (field.ndim - 3) + [(1, 1)] * 3
    return jnp.pad(field, widths)


def interior(padded):
    return padded[leading(padded) + (slice(1, -1), slice(1, -1), slice(1, -1))]


def neighbour(padded, direction, lower):
    window = [slice(1, -1), slice(1, -1), slice(1, -1)]
    window[direction] = slice(0, -2) if lower else slice(2, None)
    return padded[leading(padded) + tuple(window)]


def system_row(channel, values, padded_channel, trans_pad, blocks):
    total = blocks[channel] * values[0] + blocks[3 + channel] * values[1] + blocks[6 + channel] * values[2]
    center = interior(padded_channel)
    for direction in range(3):
        here = interior(trans_pad[direction])
        before = neighbour(trans_pad[direction], direction, True)
        total = total + here * (center - neighbour(padded_channel, direction, False))
        total = total + before * (center - neighbour(padded_channel, direction, True))
    return total


def system_apply(values, padded_values, trans_pad, blocks):
    return jnp.stack([system_row(channel, values, padded_values[channel], trans_pad, blocks) for channel in range(3)])


def frozen_apply(inverses, residual):
    return jnp.stack([inverses[channel] * residual[0] + inverses[3 + channel] * residual[1] + inverses[6 + channel] * residual[2] for channel in range(3)])


def stencil_apply(field, padded_field, center, off_pad):
    total = center * field
    for direction in range(3):
        upper_coef = off_pad[2 * direction + 1]
        lower_coef = off_pad[2 * direction]
        total = total + neighbour(upper_coef, direction, True) * neighbour(padded_field, direction, True)
        total = total + neighbour(lower_coef, direction, False) * neighbour(padded_field, direction, False)
    return total


def restrict(field):
    depth, height, width = field.shape
    return field.reshape(depth // 2, 2, height // 2, 2, width // 2, 2).sum(axis=(1, 3, 5))


def prolong(field):
    return jnp.repeat(jnp.repeat(jnp.repeat(field, 2, 0), 2, 1), 2, 2)


def coarsest_solve(rhs, stencil):
    center = stencil[0]
    off_pad = padded_zero(stencil[1:])
    field = OMEGA * rhs / center
    for sweep in range(COARSE_SWEEPS - 1):
        field = field + OMEGA * (rhs - stencil_apply(field, padded_zero(field), center, off_pad)) / center
    return field


def vcycle(rhs, stencils, level):
    if level == LEVELS:
        return coarsest_solve(rhs, stencils[level])
    stencil = stencils[level]
    center = stencil[0]
    off_pad = padded_zero(stencil[1:])
    field = OMEGA * rhs / center
    residual = rhs - stencil_apply(field, padded_zero(field), center, off_pad)
    field = field + prolong(vcycle(restrict(residual), stencils, level + 1))
    field = field + OMEGA * (rhs - stencil_apply(field, padded_zero(field), center, off_pad)) / center
    return field


def face_term(coef, lam_a, lam_b, mob_a, mob_b, pres_a, pres_b):
    total = (lam_a[0] - lam_b[0]) * (0.5 * (mob_a[0] + mob_b[0]))
    for channel in (1, 2):
        total = total + (lam_a[channel] - lam_b[channel]) * (0.5 * (mob_a[channel] + mob_b[channel]))
    return coef * total * (pres_a - pres_b)


def reference(source, active_cells, diag_blocks, frozen_inverses, transmissibility, pressure_weights, stencil_fine, coarse_one, coarse_two, coarse_three, pressure_state, mobilities):
    mask = active_cells.astype(jnp.float32)
    rhs = source * mask
    trans_pad = padded_zero(transmissibility)
    iterate = frozen_apply(frozen_inverses, rhs)
    for sweep in range(SWEEPS - 1):
        iterate = iterate + frozen_apply(frozen_inverses, rhs - system_apply(iterate, padded_zero(iterate), trans_pad, diag_blocks))
    row = system_row(0, iterate, padded_zero(iterate[0]), trans_pad, diag_blocks)
    pressure_rhs = rhs[0] - row
    correction = vcycle(pressure_rhs, (stencil_fine, coarse_one, coarse_two, coarse_three), 0)
    adjoint = mask * (iterate + pressure_weights * correction[None])
    states = jnp.concatenate([adjoint, mobilities, pressure_state[None]])
    states_pad = padded_zero(states)
    gradients = []
    for direction in range(3):
        above = neighbour(states_pad, direction, False)
        here_term = face_term(transmissibility[direction], adjoint, above[0:3], mobilities, above[3:6], pressure_state, above[6])
        below_term = neighbour(padded_zero(here_term), direction, True)
        gradients.append(0.5 * (here_term + below_term))
    return adjoint, jnp.stack(gradients)
```

```python
import itertools

import jax
import jax.numpy as jnp
from jax import lax
from jax.sharding import PartitionSpec as P

SWEEPS = 3
LEVELS = 3
COARSE_SWEEPS = 4
OMEGA = 0.8
AXES = ("gx", "gy", "layer")
DIMS = (("layer", 0), ("gy", 1), ("gx", 2))
HIGHEST = lax.Precision.HIGHEST


def pair_route(axis, phase):
    sizes = [lax.axis_size(name) for name in AXES]
    k = AXES.index(axis)
    n = sizes[k]
    route = []
    for index in itertools.product(*[range(size) for size in sizes]):
        target = list(index)
        if phase == 0:
            target[k] = index[k] ^ 1
        elif 0 < index[k] < n - 1 or k == 0:
            target[k] = (((index[k] + 1) % n ^ 1) - 1) % n
        else:
            target[0] = index[0] ^ 1 if sizes[0] % 2 == 0 else index[0]
        flat = [(i[0] * sizes[1] + i[1]) * sizes[2] + i[2] for i in (index, target)]
        route.append(tuple(flat))
    return route


def swap(axis, first, last):
    n, me = lax.axis_size(axis), lax.axis_index(axis)
    if n == 1:
        return jnp.zeros_like(last), jnp.zeros_like(first)
    if n % 2:
        before = lax.ppermute(last, axis, [(i, (i + 1) % n) for i in range(n)])
        after = lax.ppermute(first, axis, [(i, (i - 1) % n) for i in range(n)])
    else:
        even = me % 2 == 0
        one = lax.ppermute(jnp.where(even, last, first), AXES, pair_route(axis, 0))
        if n == 2:
            return jnp.where(even, 0.0, one), jnp.where(even, one, 0.0)
        two = lax.ppermute(jnp.where(even, first, last), AXES, pair_route(axis, 1))
        before, after = jnp.where(even, two, one), jnp.where(even, one, two)
    return jnp.where(me > 0, before, 0.0), jnp.where(me < n - 1, after, 0.0)


def face(field, dim, last):
    axis = field.ndim - 3 + dim
    size = field.shape[axis]
    return lax.slice_in_dim(field, size - 1, size, axis=axis) if last else lax.slice_in_dim(field, 0, 1, axis=axis)


def previous(field, before, dim):
    axis = field.ndim - 3 + dim
    return jnp.concatenate([before, lax.slice_in_dim(field, 0, field.shape[axis] - 1, axis=axis)], axis=axis)


def following(field, after, dim):
    axis = field.ndim - 3 + dim
    return jnp.concatenate([lax.slice_in_dim(field, 1, field.shape[axis], axis=axis), after], axis=axis)


def exchange(firsts, lasts):
    return [swap(axis, firsts[dim], lasts[dim]) for axis, dim in DIMS]


def faces(field):
    return [face(field, dim, False) for dim in range(3)], [face(field, dim, True) for dim in range(3)]


def block_apply(blocks, values):
    return jnp.stack([blocks[c] * values[0] + blocks[3 + c] * values[1] + blocks[6 + c] * values[2] for c in range(3)])


def laplacian(field, halos, trans, trans_before):
    total = 0.0
    for dim in range(3):
        before, after = halos[dim]
        flux = trans[dim] * (field - following(field, after, dim))
        rim = trans_before[dim] * (before - face(field, dim, False))
        total = total + flux - previous(flux, jnp.broadcast_to(rim, before.shape), dim)
    return total


def product_faces(stencil, field):
    firsts = [face(stencil[1 + 2 * dim], dim, False) * face(field, dim, False) for dim in range(3)]
    lasts = [face(stencil[2 + 2 * dim], dim, True) * face(field, dim, True) for dim in range(3)]
    return firsts, lasts


def off_apply(stencil, field, halos):
    total = 0.0
    for dim in range(3):
        before, after = halos[dim]
        total = total + previous(stencil[2 + 2 * dim] * field, before, dim)
        total = total + following(stencil[1 + 2 * dim] * field, after, dim)
    return total


def pool_matrix(size):
    return (jnp.arange(size)[:, None] // 2 == jnp.arange(size // 2)[None, :]).astype(jnp.float32)


def restrict(field):
    depth, height, width = field.shape
    field = field.reshape(depth // 2, 2, height // 2, 2, width).sum(axis=(1, 3))
    return jnp.einsum("lyx,xX->lyX", field, pool_matrix(width), precision=HIGHEST)


def prolong_x(field):
    return jnp.einsum("...X,xX->...x", field, pool_matrix(2 * field.shape[-1]), precision=HIGHEST)


def prolong(field):
    return jnp.repeat(jnp.repeat(prolong_x(field), 2, 1), 2, 0)


def zero_halos(field):
    return [(jnp.zeros_like(face(field, dim, False)),) * 2 for dim in range(3)]


def apply_whole(stencil, field):
    return stencil[0] * field + off_apply(stencil, field, zero_halos(field))


def cycle_whole(rhs, stencils, level):
    stencil = stencils[level]
    scale = OMEGA / stencil[0]
    field = rhs * scale
    if level == LEVELS:
        for sweep in range(COARSE_SWEEPS - 1):
            field = field + (rhs - apply_whole(stencil, field)) * scale
        return field
    residual = rhs - apply_whole(stencil, field)
    field = field + prolong(cycle_whole(restrict(residual), stencils, level + 1))
    return field + (rhs - apply_whole(stencil, field)) * scale


def gather_whole(arrays):
    sizes = [lax.axis_size(name) for name in AXES]
    count = sizes[0] * sizes[1] * sizes[2]
    flat = jnp.concatenate([array.reshape(-1) for array in arrays])
    width = flat.shape[0]
    rows = -(-width // 128)
    flat = jnp.pad(flat, (0, rows * 128 - width)).reshape(rows, 128)
    sent = jnp.broadcast_to(flat[None], (count,) + flat.shape)
    got = lax.all_to_all(sent, AXES, 0, 0).reshape(sizes[0], sizes[1], sizes[2], rows * 128)
    wholes, start = [], 0
    for array in arrays:
        part = got[..., start : start + array.size]
        start += array.size
        lead = array.shape[:-3]
        d, h, w = array.shape[-3:]
        part = part.reshape(sizes + [-1, d, h, w])
        part = part.transpose(3, 2, 4, 1, 5, 0, 6)
        wholes.append(part.reshape(lead + (sizes[2] * d, sizes[1] * h, sizes[0] * w)))
    return wholes


def level_one(rhs, stencil, coarse_two, coarse_three):
    scale = OMEGA / stencil[0]
    field = rhs * scale
    product_firsts, product_lasts = product_faces(stencil, field)
    firsts = [jnp.stack([product_firsts[dim], face(stencil[1 + 2 * dim], dim, False)]) for dim in range(3)]
    lasts = [jnp.stack([product_lasts[dim], face(stencil[2 + 2 * dim], dim, True)]) for dim in range(3)]
    halos = exchange(firsts, lasts)
    off = off_apply(stencil, field, [(b[0], a[0]) for b, a in halos])
    residual = (1.0 - OMEGA) * rhs - off
    next_rhs = restrict(residual)
    d, h, w = next_rhs.shape
    rhs_two, whole_two, whole_three = gather_whole([next_rhs, coarse_two, coarse_three])
    coarse = cycle_whole(rhs_two, [None, None, whole_two, whole_three], 2)
    wide = jnp.pad(coarse, 1)
    starts = [lax.axis_index(axis) * size for axis, size in zip(("layer", "gy", "gx"), (d, h, w))]
    box = lax.dynamic_slice(wide, starts, (d + 2, h + 2, w + 2))
    addition = prolong(box[1:-1, 1:-1, 1:-1])
    rims = []
    for dim in range(3):
        pair = []
        for last in (False, True):
            window = [slice(1, -1)] * 3
            window[dim] = slice(-1, None) if last else slice(0, 1)
            rim = box[tuple(window)]
            for other in range(3):
                if other != dim:
                    rim = prolong_x(rim) if other == 2 else jnp.repeat(rim, 2, other)
            pair.append(rim)
        rims.append(pair)
    add_halos = [(halos[dim][0][1] * rims[dim][0], halos[dim][1][1] * rims[dim][1]) for dim in range(3)]
    off = off + off_apply(stencil, addition, add_halos)
    field = field + addition
    return field + (rhs - stencil[0] * field - off) * scale


def local(
    source,
    active_cells,
    diag_blocks,
    frozen_inverses,
    transmissibility,
    pressure_weights,
    stencil_fine,
    coarse_one,
    coarse_two,
    coarse_three,
    pressure_state,
    mobilities,
):
    mask = active_cells.astype(jnp.float32)
    rhs = source * mask
    iterate = block_apply(frozen_inverses, rhs)
    trans_before = None
    for sweep in range(SWEEPS - 1):
        if sweep == 0:
            extra = [transmissibility[dim][None] for dim in range(3)]
        elif sweep == 1:
            extra = [jnp.concatenate([mobilities, pressure_state[None]])] * 3
        else:
            extra = [iterate[:0]] * 3
        firsts = [jnp.concatenate([face(iterate, dim, False), face(extra[dim], dim, False)]) for dim in range(3)]
        lasts = [jnp.concatenate([face(iterate, dim, True), face(extra[dim], dim, True)]) for dim in range(3)]
        halos = exchange(firsts, lasts)
        if sweep == 0:
            trans_before = [before[3] for before, after in halos]
        elif sweep == 1:
            state_halos = [(before[3:7], after[3:7]) for before, after in halos]
        halos = [(before[0:3], after[0:3]) for before, after in halos]
        applied = block_apply(diag_blocks, iterate) + laplacian(iterate, halos, transmissibility, trans_before)
        iterate = iterate + block_apply(frozen_inverses, rhs - applied)
    halos = exchange(*faces(iterate[0]))
    row = (
        diag_blocks[0] * iterate[0]
        + diag_blocks[3] * iterate[1]
        + diag_blocks[6] * iterate[2]
        + laplacian(iterate[0], halos, transmissibility, trans_before)
    )
    pressure_rhs = rhs[0] - row
    scale = OMEGA / stencil_fine[0]
    field = pressure_rhs * scale
    halos = exchange(*product_faces(stencil_fine, field))
    residual = (1.0 - OMEGA) * pressure_rhs - off_apply(stencil_fine, field, halos)
    field = field + prolong(level_one(restrict(residual), coarse_one, coarse_two, coarse_three))
    halos = exchange(*product_faces(stencil_fine, field))
    correction = (1.0 - OMEGA) * field + (pressure_rhs - off_apply(stencil_fine, field, halos)) * scale
    adjoint = mask * (iterate + pressure_weights * correction[None])
    halos = exchange(*faces(adjoint))
    gradients = []
    for dim in range(3):
        (adj_b, adj_a), (sta_b, sta_a) = halos[dim], state_halos[dim]
        mean = 0.5 * (mobilities + following(mobilities, sta_a[0:3], dim))
        drop = adjoint - following(adjoint, adj_a, dim)
        total = drop[0] * mean[0] + drop[1] * mean[1] + drop[2] * mean[2]
        here = transmissibility[dim] * total * (pressure_state - following(pressure_state, sta_a[3], dim))
        mean = 0.5 * (sta_b[0:3] + face(mobilities, dim, False))
        drop = adj_b - face(adjoint, dim, False)
        total = drop[0] * mean[0] + drop[1] * mean[1] + drop[2] * mean[2]
        rim = trans_before[dim] * total * (sta_b[3] - face(pressure_state, dim, False))
        gradients.append(0.5 * (here + previous(here, rim, dim)))
    return (adjoint, jnp.stack(gradients))


def solution(mesh):
    cells = P("layer", "gy", "gx")
    fields = P(None, "layer", "gy", "gx")
    return jax.shard_map(
        local,
        mesh=mesh,
        in_specs=(
            fields,
            cells,
            fields,
            fields,
            fields,
            fields,
            fields,
            fields,
            fields,
            fields,
            cells,
            fields,
        ),
        out_specs=(fields, fields),
        check_vma=False,
    )
```

```python
import itertools

import jax
import jax.numpy as jnp
from jax import lax
from jax.experimental import pallas as pl
from jax.experimental.pallas import tpu as pltpu
from jax.sharding import PartitionSpec as P

SWEEPS = 3
LEVELS = 3
COARSE_SWEEPS = 4
OMEGA = 0.8
LANES = 128
AXES = ("gx", "gy", "layer")
BY_DIM = ("layer", "gy", "gx")
ORDER = ((0, 1), (0, 0), (1, 1), (1, 0), (2, 1), (2, 0))
HIGHEST = lax.Precision.HIGHEST
F32 = jnp.float32


def pair_route(axis, phase):
    sizes = [lax.axis_size(name) for name in AXES]
    k = AXES.index(axis)
    n = sizes[k]
    route = []
    for index in itertools.product(*[range(size) for size in sizes]):
        target = list(index)
        if phase == 0:
            target[k] = index[k] ^ 1
        elif 0 < index[k] < n - 1 or k == 0:
            target[k] = (((index[k] + 1) % n ^ 1) - 1) % n
        else:
            target[0] = index[0] ^ 1
        flat = [(i[0] * sizes[1] + i[1]) * sizes[2] + i[2] for i in (index, target)]
        route.append(tuple(flat))
    return route


def phases(dim):
    return min(lax.axis_size(BY_DIM[dim]), 3) - 1


def sends():
    return [(dim, phase) for dim, phase in ORDER if phase < phases(dim)]


def swap(buffers):
    return [lax.ppermute(b, AXES, pair_route(BY_DIM[dim], phase)) for b, (dim, phase) in zip(buffers, sends())]


class Grid:
    def __init__(self, depth, height, dup):
        self.depth, self.height, self.dup = depth, height, dup
        self.rows = depth * height

    def buffers(self, channels):
        shapes = ((channels, self.height, LANES), (channels, self.depth, LANES), (8, LANES))
        return [jax.ShapeDtypeStruct(shapes[dim], F32) for dim, phase in sends()]

    def emit(self, channels, out):
        out = dict(zip(sends(), out))
        lane = lax.broadcasted_iota(jnp.int32, (8, LANES), 1)
        for dim in range(3):
            if phases(dim) == 0:
                continue
            even = lax.axis_index(BY_DIM[dim]) % 2 == 0
            if dim == 2:
                firsts, lasts = jnp.zeros((8, LANES), F32), jnp.zeros((8, LANES), F32)
                for c, (first, last) in enumerate(channels[dim]):
                    for k in range(self.rows // 8):
                        at = 8 * k + self.dup * c
                        here = (lane >= at) & (lane < at + self.dup)
                        rows = slice(8 * k, 8 * k + 8)
                        firsts = jnp.where(here, roll(first(rows), at, 1), firsts)
                        lasts = jnp.where(here, roll(last(rows), at + self.dup, 1), lasts)
                pairs = [(slice(None), firsts, lasts)]
            else:
                if dim == 0:
                    low, high = slice(0, self.height), slice(self.rows - self.height, self.rows)
                else:
                    low, high = (pl.ds(s, self.depth, stride=self.height) for s in (0, self.height - 1))
                pairs = [(c, first(low), last(high)) for c, (first, last) in enumerate(channels[dim])]
            for c, first, last in pairs:
                out[dim, 0][c] = jnp.where(even, last, first)
                if phases(dim) == 2:
                    out[dim, 1][c] = jnp.where(even, first, last)

    def halos(self, got, count, scratch):
        got = dict(zip(sends(), got))
        result = [[None] * 3 for _ in range(count)]
        for dim in range(3):
            me, n = lax.axis_index(BY_DIM[dim]), lax.axis_size(BY_DIM[dim])
            even = me % 2 == 0
            for c in range(count if dim < 2 else 1):
                key = c if dim < 2 else slice(None)
                if phases(dim) == 0:
                    before = after = jnp.zeros((self.height, self.depth, 8)[dim : dim + 1] + (LANES,), F32)
                elif phases(dim) == 1:
                    one = got[dim, 0][key]
                    before, after = jnp.where(even, 0.0, one), jnp.where(even, one, 0.0)
                else:
                    one, two = got[dim, 0][key], got[dim, 1][key]
                    before, after = jnp.where(even, two, one), jnp.where(even, one, two)
                    before, after = jnp.where(me > 0, before, 0.0), jnp.where(me < n - 1, after, 0.0)
                if dim < 2:
                    result[c][dim] = (before, after)
                else:
                    for ch in range(count):
                        parts = []
                        for side, start in ((before, 0), (after, LANES - self.dup)):
                            pieces = [roll(side, start - 8 * k - self.dup * ch, 1) for k in range(self.rows // 8)]
                            parts.append(jnp.concatenate(pieces))
                        result[ch][dim] = tuple(parts)
        return [Rim(self, r, scratch, c) for c, r in enumerate(result)]


class Rim:
    def __init__(self, grid, faces, scratch, c):
        self.grid, self.faces = grid, faces
        ends = scratch.at[c]
        ends[pl.ds(0, grid.depth, stride=grid.height), :] = faces[1][0]
        ends[pl.ds(grid.height - 1, grid.depth, stride=grid.height), :] = faces[1][1]
        self.y_ends = ends[...]

    def previous(self, value, dim):
        g = self.grid
        if dim == 0:
            return jnp.concatenate([self.faces[0][0], value[: g.rows - g.height]])
        if dim == 1:
            return jnp.where(row_y(value, g.height) == 0, self.y_ends, roll(value, 1, 0))
        return jnp.where(lane_of(value) < g.dup, self.faces[2][0], roll(value, g.dup, 1))

    def following(self, value, dim):
        g = self.grid
        if dim == 0:
            return jnp.concatenate([value[g.height :], self.faces[0][1]])
        if dim == 1:
            return jnp.where(row_y(value, g.height) == g.height - 1, self.y_ends, roll(value, -1, 0))
        return jnp.where(lane_of(value) >= value.shape[1] - g.dup, self.faces[2][1], roll(value, -g.dup, 1))


class Closed:
    def __init__(self, height, dup):
        self.height, self.dup = height, dup

    def previous(self, value, dim):
        if dim == 0:
            return jnp.concatenate([jnp.zeros_like(value[: self.height]), value[: -self.height]])
        if dim == 1:
            return jnp.where(row_y(value, self.height) == 0, 0.0, roll(value, 1, 0))
        return jnp.where(lane_of(value) < self.dup, 0.0, roll(value, self.dup, 1))

    def following(self, value, dim):
        if dim == 0:
            return jnp.concatenate([value[self.height :], jnp.zeros_like(value[: self.height])])
        if dim == 1:
            return jnp.where(row_y(value, self.height) == self.height - 1, 0.0, roll(value, -1, 0))
        return jnp.where(lane_of(value) >= value.shape[1] - self.dup, 0.0, roll(value, -self.dup, 1))


def roll(value, shift, axis):
    shift %= value.shape[axis]
    return pltpu.roll(value, shift, axis) if shift else value


def row_y(value, height):
    return lax.broadcasted_iota(jnp.int32, value.shape, 0) % height


def lane_of(value):
    return lax.broadcasted_iota(jnp.int32, value.shape, 1)


def loader(ref, c):
    return lambda rows: ref[c, rows, :]


def product(coefs, k, ref):
    return lambda rows: coefs[k, rows, :] * ref[rows, :]


def off_apply(stencil, field, rim):
    total = 0.0
    for dim in range(3):
        total = total + rim.previous(stencil[2 + 2 * dim] * field, dim)
        total = total + rim.following(stencil[1 + 2 * dim] * field, dim)
    return total


def block_row(blocks, c, values):
    return blocks[c] * values[0] + blocks[3 + c] * values[1] + blocks[6 + c] * values[2]


def system_row(c, values, rim, blocks, trans, trans_before):
    total = block_row(blocks, c, values)
    v = values[c]
    for dim in range(3):
        total = total + trans[dim] * (v - rim.following(v, dim))
        total = total + trans_before[dim] * (v - rim.previous(v, dim))
    return total


def pair_sum_x(value, dup):
    odd = (lane_of(value) // dup) % 2 == 1
    return value + jnp.where(odd, roll(value, dup, 1), roll(value, -dup, 1))


def pair_sum_rows(value, depth, height, scratch):
    half = depth // 2
    parts = [value[2 * a * height : (2 * a + 1) * height] + value[(2 * a + 1) * height : (2 * a + 2) * height] for a in range(half)]
    whole = jnp.concatenate(parts)
    count = half * height // 2
    sums = []
    for at in range(0, whole.shape[1], LANES):
        scratch[: half * height, :] = whole[:, at : at + LANES]
        sums.append(scratch[pl.ds(0, count, stride=2), :] + scratch[pl.ds(1, count, stride=2), :])
    return jnp.concatenate(sums, axis=1)


def spread_rows(value, depth, height, scratch):
    count = depth * height
    tiles = []
    for at in range(0, value.shape[1], LANES):
        scratch[pl.ds(0, count, stride=2), :] = value[:, at : at + LANES]
        scratch[pl.ds(1, count, stride=2), :] = value[:, at : at + LANES]
        wide = scratch[: 2 * count, :]
        tiles.append(jnp.concatenate([wide[2 * height * (a // 2) : 2 * height * (a // 2 + 1)] for a in range(2 * depth)]))
    return jnp.concatenate(tiles, axis=1)


def one_hot(shape, hit):
    return jnp.where(hit(lax.broadcasted_iota(jnp.int32, shape, 0), lax.broadcasted_iota(jnp.int32, shape, 1)), 1.0, 0.0).astype(F32)


def matmul(a, b):
    return jnp.dot(a, b, precision=HIGHEST, preferred_element_type=F32)


def call(kernel, inputs, outputs, scratch=()):
    return pl.pallas_call(
        kernel,
        out_shape=list(outputs),
        scratch_shapes=[pltpu.VMEM(shape, F32) for shape in scratch],
        compiler_params=pltpu.CompilerParams(vmem_limit_bytes=40 * 2**20),
    )(*inputs)


def local(
    source,
    active_cells,
    diag_blocks,
    frozen_inverses,
    transmissibility,
    pressure_weights,
    stencil_fine,
    coarse_one,
    coarse_two,
    coarse_three,
    pressure_state,
    mobilities,
):
    depth, height, width = active_cells.shape
    fine, mid = Grid(depth, height, 1), Grid(depth // 2, height // 2, 2)
    sizes = [lax.axis_size(name) for name in AXES]
    count = sizes[0] * sizes[1] * sizes[2]
    swaps = len(sends())
    rows = fine.rows

    def flat(array):
        return array.reshape(array.shape[:-3] + (rows, width))

    def out(*shape):
        return jax.ShapeDtypeStruct(shape, F32)

    source, active, diag, frozen, trans, weights, stencil, pressure, mobility = (
        flat(a)
        for a in (
            source,
            active_cells,
            diag_blocks,
            frozen_inverses,
            transmissibility,
            pressure_weights,
            stencil_fine,
            pressure_state,
            mobilities,
        )
    )
    pressure = pressure[None]

    def start_kernel(source, active, frozen, trans, rhs_out, it_out, *buffers):
        mask = active[...].astype(F32)
        rhs = [source[c] * mask for c in range(3)]
        for c in range(3):
            rhs_out[c] = rhs[c]
            it_out[c] = block_row(frozen, c, rhs)
        its = [(loader(it_out, c),) * 2 for c in range(3)]
        fine.emit([its + [(loader(trans, dim),) * 2] for dim in range(3)], buffers)

    rhs, iterate, *buffers = call(
        start_kernel, (source, active, frozen, trans), [out(3, rows, LANES)] * 2 + fine.buffers(4)
    )
    got = swap(buffers)

    def sweep_one(rhs, it, frozen, diag, trans, mobility, pressure, *rest):
        got, (it_out, before_out), buffers, (ends,) = rest[:swaps], rest[swaps : swaps + 2], rest[swaps + 2 : -1], rest[-1:]
        rims = fine.halos(got, 4, ends)
        trans_before = [rims[3].previous(trans[dim], dim) for dim in range(3)]
        values = [it[c] for c in range(3)]
        rest = [rhs[c] - system_row(c, values, rims[c], diag, trans, trans_before) for c in range(3)]
        for c in range(3):
            before_out[c] = trans_before[c]
            it_out[c] = values[c] + block_row(frozen, c, rest)
        channels = [(loader(it_out, c),) * 2 for c in range(3)]
        channels += [(loader(mobility, c),) * 2 for c in range(3)] + [(loader(pressure, 0),) * 2]
        fine.emit([channels] * 3, buffers)

    iterate, trans_before, *buffers = call(
        sweep_one,
        (rhs, iterate, frozen, diag, trans, mobility, pressure, *got),
        [out(3, rows, LANES)] * 2 + fine.buffers(7),
        [(4, rows, LANES)],
    )
    state_got = got = swap(buffers)

    def sweep_two(rhs, it, frozen, diag, trans, trans_before, *rest):
        got, it_out, buffers, ends = rest[:swaps], rest[swaps], rest[swaps + 1 : -1], rest[-1]
        rims = fine.halos(got, 3, ends)
        values = [it[c] for c in range(3)]
        rest = [rhs[c] - system_row(c, values, rims[c], diag, trans, trans_before) for c in range(3)]
        for c in range(3):
            it_out[c] = values[c] + block_row(frozen, c, rest)
        fine.emit([[(loader(it_out, 0),) * 2]] * 3, buffers)

    iterate, *buffers = call(
        sweep_two,
        (rhs, iterate, frozen, diag, trans, trans_before, *got),
        [out(3, rows, LANES)] + fine.buffers(1),
        [(3, rows, LANES)],
    )
    got = swap(buffers)

    def emit_products(grid, coefs, field, buffers, with_coefs=False):
        channels = []
        for dim in range(3):
            pairs = [(product(coefs, 1 + 2 * dim, field), product(coefs, 2 + 2 * dim, field))]
            if with_coefs:
                pairs.append((loader(coefs, 1 + 2 * dim), loader(coefs, 2 + 2 * dim)))
            channels.append(pairs)
        grid.emit(channels, buffers)

    def pressure_kernel(rhs, it, diag, trans, trans_before, stencil, *rest):
        got, (b_out, x_out), buffers, ends = rest[:swaps], rest[swaps : swaps + 2], rest[swaps + 2 : -1], rest[-1]
        (rim,) = fine.halos(got, 1, ends)
        b = rhs[0] - system_row(0, [it[c] for c in range(3)], rim, diag, trans, trans_before)
        b_out[...] = b
        x_out[...] = b * (OMEGA / stencil[0])
        emit_products(fine, stencil, x_out, buffers)

    b_fine, x_fine, *buffers = call(
        pressure_kernel,
        (rhs, iterate, diag, trans, trans_before, stencil, *got),
        [out(rows, LANES)] * 2 + fine.buffers(1),
        [(1, rows, LANES)],
    )
    got = swap(buffers)

    one = coarse_one.reshape(7, mid.rows, width // 2)
    one = jnp.repeat(one, 2, axis=2)
    low_depth, low_height, low_width = coarse_two.shape[1:]
    groups = LANES // low_width

    def pack(array, channels, dup):
        lead = array.shape[1] * array.shape[2]
        array = jnp.repeat(array, dup, axis=3) if dup > 1 else array
        array = jnp.pad(array, ((0, channels - array.shape[0]), (0, 0), (0, 0), (0, 0)))
        array = array.reshape(groups, channels // groups, lead, low_width).transpose(1, 2, 0, 3)
        return array.reshape(channels // groups * lead, LANES)

    packed = jnp.concatenate([pack(coarse_two, 8, 1), pack(coarse_three, 8, 2)])
    block = packed.shape[0]
    low_rows = low_depth * low_height

    def residual_kernel(b, x, stencil, one, *rest):
        got, (b_out, x_out), buffers, (ends, temp) = rest[:swaps], rest[swaps : swaps + 2], rest[swaps + 2 : -2], rest[-2:]
        (rim,) = fine.halos(got, 1, ends)
        residual = (1.0 - OMEGA) * b[...] - off_apply(stencil, x[...], rim)
        coarse = pair_sum_rows(pair_sum_x(residual, 1), depth, height, temp)
        b_out[...] = coarse
        x_out[...] = coarse * (OMEGA / one[0])
        emit_products(mid, one, x_out, buffers, True)

    b_mid, x_mid, *buffers = call(
        residual_kernel,
        (b_fine, x_fine, stencil, one, *got),
        [out(mid.rows, LANES)] * 2 + mid.buffers(2),
        [(1, rows, LANES), (rows // 2, LANES)],
    )
    mid_got = got = swap(buffers)

    def low_kernel(b, x, one, packed, *rest):
        got, (off_out, sent), (ends, temp) = rest[:swaps], rest[swaps : swaps + 2], rest[-2:]
        rim, _ = mid.halos(got, 2, ends)
        off = off_apply(one, x[...], rim)
        off_out[...] = off
        residual = (1.0 - OMEGA) * b[...] - off
        coarse = pair_sum_rows(residual, mid.depth, mid.height, temp)
        first = LANES - low_width
        place = one_hot((LANES, LANES), lambda i, j: (i // 4 == j - first) & (i % 2 == 0))
        filled = jnp.concatenate([packed[:low_rows], packed[low_rows : 2 * low_rows] + matmul(coarse, place), packed[2 * low_rows :]])
        sent[...] = jnp.broadcast_to(filled[None], (count, block, LANES))

    off_mid, sent = call(
        low_kernel,
        (b_mid, x_mid, one, packed, *got),
        [out(mid.rows, LANES), out(count, block, LANES)],
        [(2, mid.rows, LANES), (mid.rows // 2, LANES)],
    )
    everyone = lax.all_to_all(sent, AXES, 0, 0)

    two_rows, two_width = sizes[2] * low_depth * sizes[1] * low_height, sizes[0] * low_width
    two_height = sizes[1] * low_height
    three_height = two_height // 2
    three_rows = two_rows // 4

    def assemble(everyone, two, three):
        per = sizes[1] * sizes[2]
        for tile in range(two_width // LANES):
            parts = [everyone[(tile * groups + g) * per : (tile * groups + g + 1) * per].reshape(per * block, LANES) for g in range(groups)]
            lane = lane_of(parts[0])
            for q in range(groups):
                value = parts[0] if q == 0 else roll(parts[0], -low_width * q, 1)
                for g in range(1, groups):
                    value = jnp.where(lane // low_width == g, roll(parts[g], low_width * (g - q), 1), value)
                value = value.reshape(per, block, LANES)
                lanes = slice(tile * LANES, (tile + 1) * LANES)
                for y in range(sizes[1]):
                    for z in range(sizes[2]):
                        for half in range(8 // groups):
                            c = q * (8 // groups) + half
                            mine = value[y * sizes[2] + z]
                            for a in range(low_depth):
                                at = (z * low_depth + a) * two_height + y * low_height
                                start = (half * low_depth + a) * low_height
                                two[c, at : at + low_height, lanes] = mine[start : start + low_height]
                            low = low_height // 2
                            for a in range(low_depth // 2):
                                at = (z * (low_depth // 2) + a) * three_height + y * low
                                start = 8 // groups * low_rows + (half * (low_depth // 2) + a) * low
                                three[c, at : at + low, lanes] = mine[start : start + low]

    def solve_low(two, three, temp):
        closed = Closed(two_height, 1)
        b = two[7]
        scale = OMEGA / two[0]
        x = b * scale
        residual = (1.0 - OMEGA) * b - off_apply(two, x, closed)
        coarse = pair_sum_rows(pair_sum_x(residual, 1), sizes[2] * low_depth, two_height, temp)
        inner = Closed(three_height, 2)
        inner_scale = OMEGA / three[0]
        field = start = coarse * inner_scale
        for sweep in range(COARSE_SWEEPS - 1):
            field = start + (1.0 - OMEGA) * field - off_apply(three, field, inner) * inner_scale
        x = x + spread_rows(field, sizes[2] * low_depth // 2, three_height, temp)
        return (1.0 - OMEGA) * x + (b - off_apply(two, x, closed)) * scale

    def up_kernel(everyone, b, x, off, one, x_fine, stencil, *rest):
        got, field_out, buffers = rest[:swaps], rest[swaps], rest[swaps + 1 : -5]
        ends, two, three, low_temp, temp = rest[-5:]
        assemble(everyone, two, three)
        low = solve_low(two, three, low_temp)
        gx, gy, gz = (lax.axis_index(name) for name in AXES)
        h, d = mid.height, mid.depth
        own = one_hot((two_width, LANES), lambda i, j: i == gx * low_width + j // 4)
        beside = one_hot(
            (two_width, LANES),
            lambda i, j: ((j < 2) & (i == gx * low_width - 1)) | ((j >= LANES - 2) & (i == (gx + 1) * low_width)),
        )

        def picked(n, layer, y):
            def hit(i, j):
                return j == (gz * low_depth + layer(i)) * two_height + gy * low_height + y(i)

            return one_hot((n, two_rows), hit)

        picks = jnp.concatenate(
            [
                picked(d * h, lambda i: i // h // 2, lambda i: i % h // 2),
                picked(h, lambda i: -1, lambda i: i // 2),
                picked(h, lambda i: low_depth, lambda i: i // 2),
                picked(8, lambda i: i % d // 2, lambda i: jnp.where(i < d, -1, low_height)),
            ]
        )
        chosen = matmul(picks, low)
        around = matmul(chosen, own)
        add = around[: d * h]
        add_x = matmul(chosen[: d * h], beside)
        _, coefs = mid.halos(got, 2, ends)
        starts = d * h
        faces = [
            (coefs.faces[0][0] * around[starts : starts + h], coefs.faces[0][1] * around[starts + h : starts + 2 * h]),
            (
                coefs.faces[1][0] * around[starts + 2 * h : starts + 2 * h + d],
                coefs.faces[1][1] * around[starts + 2 * h + d : starts + 2 * h + 2 * d],
            ),
            (coefs.faces[2][0] * add_x, coefs.faces[2][1] * add_x),
        ]
        off_all = off[...] + off_apply(one, add, Rim(mid, faces, ends, 0))
        field = (1.0 - OMEGA) * (x[...] + add) + (b[...] - off_all) * (OMEGA / one[0])
        field_out[...] = x_fine[...] + spread_rows(field, d, h, temp)
        emit_products(fine, stencil, field_out, buffers)

    field, *buffers = call(
        up_kernel,
        (everyone, b_mid, x_mid, off_mid, one, x_fine, stencil, *got),
        [out(rows, LANES)] + fine.buffers(1),
        [(2, mid.rows, LANES), (8, two_rows, two_width), (8, three_rows, two_width), (two_rows, LANES), (rows // 2, LANES)],
    )
    got = swap(buffers)

    def adjoint_kernel(field, b, stencil, it, active, weights, *rest):
        got, adj_out, buffers, ends = rest[:swaps], rest[swaps], rest[swaps + 1 : -1], rest[-1]
        (rim,) = fine.halos(got, 1, ends)
        value = field[...]
        correction = (1.0 - OMEGA) * value + (b[...] - off_apply(stencil, value, rim)) * (OMEGA / stencil[0])
        mask = active[...].astype(F32)
        for c in range(3):
            adj_out[c] = mask * (it[c] + weights[c] * correction)
        fine.emit([[(loader(adj_out, c),) * 2 for c in range(3)]] * 3, buffers)

    adjoint, *buffers = call(
        adjoint_kernel,
        (field, b_fine, stencil, iterate, active, weights, *got),
        [out(3, rows, LANES)] + fine.buffers(3),
        [(1, rows, LANES)],
    )
    got = swap(buffers)

    def gradient_kernel(adj, mobility, pressure, trans, trans_before, *rest):
        got, state_got, grad_out, (ends, state_ends) = rest[:swaps], rest[swaps : 2 * swaps], rest[2 * swaps], rest[-2:]
        adj_rims = fine.halos(got, 3, ends)
        state_rims = fine.halos(state_got, 7, state_ends)[3:]
        values = [adj[c] for c in range(3)]
        for dim in range(3):

            def term(trans, shift):
                total = 0.0
                for c in range(3):
                    mean = 0.5 * (mobility[c] + shift(state_rims[c], mobility[c]))
                    total = total + (values[c] - shift(adj_rims[c], values[c])) * mean
                return trans * total * (pressure[0] - shift(state_rims[3], pressure[0]))

            here = term(trans[dim], lambda rim, v: rim.following(v, dim))
            below = term(trans_before[dim], lambda rim, v: rim.previous(v, dim))
            grad_out[dim] = 0.5 * (here + below)

    (gradient,) = call(
        gradient_kernel,
        (adjoint, mobility, pressure, trans, trans_before, *got, *state_got),
        [out(3, rows, LANES)],
        [(3, rows, LANES), (7, rows, LANES)],
    )
    shape = (3, depth, height, width)
    return adjoint.reshape(shape), gradient.reshape(shape)


def solution(mesh):
    cells = P("layer", "gy", "gx")
    fields = P(None, "layer", "gy", "gx")
    return jax.shard_map(
        local,
        mesh=mesh,
        in_specs=(
            fields,
            cells,
            fields,
            fields,
            fields,
            fields,
            fields,
            fields,
            fields,
            fields,
            cells,
            fields,
        ),
        out_specs=(fields, fields),
        check_vma=False,
    )
```

```python
import itertools

import jax
import jax.numpy as jnp
from jax import lax
from jax.experimental import pallas as pl
from jax.experimental.pallas import tpu as pltpu
from jax.sharding import PartitionSpec as P

SWEEPS = 3
LEVELS = 3
COARSE_SWEEPS = 4
OMEGA = 0.8
LANES = 128
AXES = ("gx", "gy", "layer")
BY_DIM = ("layer", "gy", "gx")
ORDER = ((0, 1), (0, 0), (1, 1), (1, 0), (2, 1), (2, 0))
HIGHEST = lax.Precision.HIGHEST
F32 = jnp.float32


def pair_route(axis, phase):
    sizes = [lax.axis_size(name) for name in AXES]
    k = AXES.index(axis)
    n = sizes[k]
    route = []
    for index in itertools.product(*[range(size) for size in sizes]):
        target = list(index)
        if phase == 0:
            target[k] = index[k] ^ 1
        elif 0 < index[k] < n - 1 or k == 0:
            target[k] = (((index[k] + 1) % n ^ 1) - 1) % n
        else:
            target[0] = index[0] ^ 1
        flat = [(i[0] * sizes[1] + i[1]) * sizes[2] + i[2] for i in (index, target)]
        route.append(tuple(flat))
    return route


def phases(dim):
    return min(lax.axis_size(BY_DIM[dim]), 3) - 1


def sends():
    return [(dim, phase) for dim, phase in ORDER if phase < phases(dim)]


def swap(buffers):
    return [lax.ppermute(b, AXES, pair_route(BY_DIM[dim], phase)) for b, (dim, phase) in zip(buffers, sends())]


class Grid:
    def __init__(self, depth, height, dup):
        self.depth, self.height, self.dup = depth, height, dup
        self.rows = depth * height

    def buffers(self, channels):
        shapes = ((channels, self.height, LANES), (channels, self.depth, LANES), (8, LANES))
        return [jax.ShapeDtypeStruct(shapes[dim], F32) for dim, phase in sends()]

    def emit(self, channels, out):
        out = dict(zip(sends(), out))
        lane = lax.broadcasted_iota(jnp.int32, (8, LANES), 1)
        for dim in range(3):
            if phases(dim) == 0:
                continue
            even = lax.axis_index(BY_DIM[dim]) % 2 == 0
            if dim == 2:
                firsts, lasts = jnp.zeros((8, LANES), F32), jnp.zeros((8, LANES), F32)
                for c, (first, last) in enumerate(channels[dim]):
                    for k in range(self.rows // 8):
                        at = 8 * k + self.dup * c
                        here = (lane >= at) & (lane < at + self.dup)
                        rows = slice(8 * k, 8 * k + 8)
                        firsts = jnp.where(here, roll(first(rows), at, 1), firsts)
                        lasts = jnp.where(here, roll(last(rows), at + self.dup, 1), lasts)
                pairs = [(slice(None), firsts, lasts)]
            else:
                if dim == 0:
                    low, high = slice(0, self.height), slice(self.rows - self.height, self.rows)
                else:
                    low, high = (pl.ds(s, self.depth, stride=self.height) for s in (0, self.height - 1))
                pairs = [(c, first(low), last(high)) for c, (first, last) in enumerate(channels[dim])]
            for c, first, last in pairs:
                out[dim, 0][c] = jnp.where(even, last, first)
                if phases(dim) == 2:
                    out[dim, 1][c] = jnp.where(even, first, last)

    def halos(self, got, count, scratch):
        got = dict(zip(sends(), got))
        result = [[None] * 3 for _ in range(count)]
        for dim in range(3):
            me, n = lax.axis_index(BY_DIM[dim]), lax.axis_size(BY_DIM[dim])
            even = me % 2 == 0
            for c in range(count if dim < 2 else 1):
                key = c if dim < 2 else slice(None)
                if phases(dim) == 0:
                    before = after = jnp.zeros((self.height, self.depth, 8)[dim : dim + 1] + (LANES,), F32)
                elif phases(dim) == 1:
                    one = got[dim, 0][key]
                    before, after = jnp.where(even, 0.0, one), jnp.where(even, one, 0.0)
                else:
                    one, two = got[dim, 0][key], got[dim, 1][key]
                    before, after = jnp.where(even, two, one), jnp.where(even, one, two)
                    before, after = jnp.where(me > 0, before, 0.0), jnp.where(me < n - 1, after, 0.0)
                if dim < 2:
                    result[c][dim] = (before, after)
                else:
                    for ch in range(count):
                        parts = []
                        for side, start in ((before, 0), (after, LANES - self.dup)):
                            pieces = [roll(side, start - 8 * k - self.dup * ch, 1) for k in range(self.rows // 8)]
                            parts.append(jnp.concatenate(pieces))
                        result[ch][dim] = tuple(parts)
        return [Rim(self, r, scratch, c) for c, r in enumerate(result)]


class Rim:
    def __init__(self, grid, faces, scratch, c):
        self.grid, self.faces = grid, faces
        ends = scratch.at[c]
        ends[pl.ds(0, grid.depth, stride=grid.height), :] = faces[1][0]
        ends[pl.ds(grid.height - 1, grid.depth, stride=grid.height), :] = faces[1][1]
        self.y_ends = ends[...]

    def previous(self, value, dim):
        g = self.grid
        if dim == 0:
            return jnp.concatenate([self.faces[0][0], value[: g.rows - g.height]])
        if dim == 1:
            return jnp.where(row_y(value, g.height) == 0, self.y_ends, roll(value, 1, 0))
        return jnp.where(lane_of(value) < g.dup, self.faces[2][0], roll(value, g.dup, 1))

    def following(self, value, dim):
        g = self.grid
        if dim == 0:
            return jnp.concatenate([value[g.height :], self.faces[0][1]])
        if dim == 1:
            return jnp.where(row_y(value, g.height) == g.height - 1, self.y_ends, roll(value, -1, 0))
        return jnp.where(lane_of(value) >= value.shape[1] - g.dup, self.faces[2][1], roll(value, -g.dup, 1))


class Closed:
    def __init__(self, height, dup):
        self.height, self.dup = height, dup

    def previous(self, value, dim):
        if dim == 0:
            return jnp.concatenate([jnp.zeros_like(value[: self.height]), value[: -self.height]])
        if dim == 1:
            return jnp.where(row_y(value, self.height) == 0, 0.0, roll(value, 1, 0))
        return jnp.where(lane_of(value) < self.dup, 0.0, roll(value, self.dup, 1))

    def following(self, value, dim):
        if dim == 0:
            return jnp.concatenate([value[self.height :], jnp.zeros_like(value[: self.height])])
        if dim == 1:
            return jnp.where(row_y(value, self.height) == self.height - 1, 0.0, roll(value, -1, 0))
        return jnp.where(lane_of(value) >= value.shape[1] - self.dup, 0.0, roll(value, -self.dup, 1))


def roll(value, shift, axis):
    shift %= value.shape[axis]
    return pltpu.roll(value, shift, axis) if shift else value


def row_y(value, height):
    return lax.broadcasted_iota(jnp.int32, value.shape, 0) % height


def lane_of(value):
    return lax.broadcasted_iota(jnp.int32, value.shape, 1)


def loader(ref, c):
    return lambda rows: ref[c, rows, :]


def product(coefs, k, ref):
    return lambda rows: coefs[k, rows, :] * ref[rows, :]


def off_apply(stencil, field, rim):
    total = 0.0
    for dim in range(3):
        total = total + rim.previous(stencil[2 + 2 * dim] * field, dim)
        total = total + rim.following(stencil[1 + 2 * dim] * field, dim)
    return total


def block_row(blocks, c, values):
    return blocks[c] * values[0] + blocks[3 + c] * values[1] + blocks[6 + c] * values[2]


def system_row(c, values, rim, blocks, trans, trans_before):
    total = block_row(blocks, c, values)
    v = values[c]
    for dim in range(3):
        total = total + trans[dim] * (v - rim.following(v, dim))
        total = total + trans_before[dim] * (v - rim.previous(v, dim))
    return total


def pair_sum_x(value, dup):
    odd = (lane_of(value) // dup) % 2 == 1
    return value + jnp.where(odd, roll(value, dup, 1), roll(value, -dup, 1))


def pair_sum_rows(value, depth, height, scratch):
    half = depth // 2
    parts = [value[2 * a * height : (2 * a + 1) * height] + value[(2 * a + 1) * height : (2 * a + 2) * height] for a in range(half)]
    whole = jnp.concatenate(parts)
    count = half * height // 2
    sums = []
    for at in range(0, whole.shape[1], LANES):
        scratch[: half * height, :] = whole[:, at : at + LANES]
        sums.append(scratch[pl.ds(0, count, stride=2), :] + scratch[pl.ds(1, count, stride=2), :])
    return jnp.concatenate(sums, axis=1)


def spread_rows(value, depth, height, scratch):
    count = depth * height
    tiles = []
    for at in range(0, value.shape[1], LANES):
        scratch[pl.ds(0, count, stride=2), :] = value[:, at : at + LANES]
        scratch[pl.ds(1, count, stride=2), :] = value[:, at : at + LANES]
        wide = scratch[: 2 * count, :]
        tiles.append(jnp.concatenate([wide[2 * height * (a // 2) : 2 * height * (a // 2 + 1)] for a in range(2 * depth)]))
    return jnp.concatenate(tiles, axis=1)


def one_hot(shape, hit):
    return jnp.where(hit(lax.broadcasted_iota(jnp.int32, shape, 0), lax.broadcasted_iota(jnp.int32, shape, 1)), 1.0, 0.0).astype(F32)


def matmul(a, b):
    return jnp.dot(a, b, precision=HIGHEST, preferred_element_type=F32)


def call(kernel, inputs, outputs, scratch=(), far_inputs=0, far_outputs=0):
    inputs = list(inputs)
    for i in range(far_inputs):
        inputs[i] = pltpu.with_memory_space_constraint(inputs[i], pltpu.HBM)

    def specs(count, far):
        return [pl.BlockSpec(memory_space=pltpu.HBM if i < far else pltpu.VMEM) for i in range(count)]

    return pl.pallas_call(
        kernel,
        out_shape=list(outputs),
        in_specs=specs(len(inputs), far_inputs),
        out_specs=specs(len(outputs), far_outputs),
        scratch_shapes=[pltpu.VMEM(shape, F32) if isinstance(shape, tuple) else shape for shape in scratch],
        compiler_params=pltpu.CompilerParams(vmem_limit_bytes=24 * 2**20),
    )(*inputs)


def local(
    source,
    active_cells,
    diag_blocks,
    frozen_inverses,
    transmissibility,
    pressure_weights,
    stencil_fine,
    coarse_one,
    coarse_two,
    coarse_three,
    pressure_state,
    mobilities,
):
    depth, height, width = active_cells.shape
    fine, mid = Grid(depth, height, 1), Grid(depth // 2, height // 2, 2)
    sizes = [lax.axis_size(name) for name in AXES]
    count = sizes[0] * sizes[1] * sizes[2]
    swaps = len(sends())
    rows = fine.rows

    def flat(array):
        return array.reshape(array.shape[:-3] + (rows, width))

    def out(*shape):
        return jax.ShapeDtypeStruct(shape, F32)

    source, active, diag, frozen, trans, weights, stencil, pressure, mobility = (
        flat(a)
        for a in (
            source,
            active_cells,
            diag_blocks,
            frozen_inverses,
            transmissibility,
            pressure_weights,
            stencil_fine,
            pressure_state,
            mobilities,
        )
    )
    pressure = pressure[None]

    def start_kernel(source, active, frozen, trans, rhs_out, it_out, frozen_out, trans_out, *rest):
        buffers, (source_in, active_in, sems) = rest[:-3], rest[-3:]
        order = [k for c in range(3) for k in (c, 3 + c, 6 + c)]
        pairs = [(active, active_in), (source, source_in)] + [(frozen.at[k], frozen_out.at[k]) for k in order]
        pairs.append((trans, trans_out))
        copies = [pltpu.make_async_copy(a, b, sems.at[i]) for i, (a, b) in enumerate(pairs)]
        for copy in copies:
            copy.start()
        copies[0].wait()
        mask = active_in[...].astype(F32)
        copies[1].wait()
        rhs = [source_in[c] * mask for c in range(3)]
        for c in range(3):
            rhs_out[c] = rhs[c]
        for c in range(3):
            for copy in copies[2 + 3 * c : 5 + 3 * c]:
                copy.wait()
            it_out[c] = block_row(frozen_out, c, rhs)
        copies[-1].wait()
        its = [(loader(it_out, c),) * 2 for c in range(3)]
        fine.emit([its + [(loader(trans_out, dim),) * 2] for dim in range(3)], buffers)

    rhs, iterate, frozen, trans, *buffers = call(
        start_kernel,
        (source, active, frozen, trans),
        [out(3, rows, LANES)] * 2 + [out(9, rows, LANES), out(3, rows, LANES)] + fine.buffers(4),
        [(3, rows, LANES), pltpu.VMEM((rows, LANES), jnp.int32), pltpu.SemaphoreType.DMA((12,))],
        far_inputs=4,
    )
    got = swap(buffers)

    def sweep_one(rhs, it, frozen, diag, trans, mobility, pressure, *rest):
        got, (it_out, before_out), buffers, (ends,) = rest[:swaps], rest[swaps : swaps + 2], rest[swaps + 2 : -1], rest[-1:]
        rims = fine.halos(got, 4, ends)
        trans_before = [rims[3].previous(trans[dim], dim) for dim in range(3)]
        values = [it[c] for c in range(3)]
        rest = [rhs[c] - system_row(c, values, rims[c], diag, trans, trans_before) for c in range(3)]
        for c in range(3):
            before_out[c] = trans_before[c]
            it_out[c] = values[c] + block_row(frozen, c, rest)
        channels = [(loader(it_out, c),) * 2 for c in range(3)]
        channels += [(loader(mobility, c),) * 2 for c in range(3)] + [(loader(pressure, 0),) * 2]
        fine.emit([channels] * 3, buffers)

    iterate, trans_before, *buffers = call(
        sweep_one,
        (rhs, iterate, frozen, diag, trans, mobility, pressure, *got),
        [out(3, rows, LANES)] * 2 + fine.buffers(7),
        [(4, rows, LANES)],
    )
    state_got = got = swap(buffers)

    def sweep_two(rhs, it, frozen, diag, trans, trans_before, *rest):
        got, it_out, buffers, ends = rest[:swaps], rest[swaps], rest[swaps + 1 : -1], rest[-1]
        rims = fine.halos(got, 3, ends)
        values = [it[c] for c in range(3)]
        rest = [rhs[c] - system_row(c, values, rims[c], diag, trans, trans_before) for c in range(3)]
        for c in range(3):
            it_out[c] = values[c] + block_row(frozen, c, rest)
        fine.emit([[(loader(it_out, 0),) * 2]] * 3, buffers)

    iterate, *buffers = call(
        sweep_two,
        (rhs, iterate, frozen, diag, trans, trans_before, *got),
        [out(3, rows, LANES)] + fine.buffers(1),
        [(3, rows, LANES)],
    )
    got = swap(buffers)

    def emit_products(grid, coefs, field, buffers, with_coefs=False):
        channels = []
        for dim in range(3):
            pairs = [(product(coefs, 1 + 2 * dim, field), product(coefs, 2 + 2 * dim, field))]
            if with_coefs:
                pairs.append((loader(coefs, 1 + 2 * dim), loader(coefs, 2 + 2 * dim)))
            channels.append(pairs)
        grid.emit(channels, buffers)

    def pressure_kernel(rhs, it, diag, trans, trans_before, stencil, *rest):
        got, (b_out, x_out), buffers, ends = rest[:swaps], rest[swaps : swaps + 2], rest[swaps + 2 : -1], rest[-1]
        (rim,) = fine.halos(got, 1, ends)
        b = rhs[0] - system_row(0, [it[c] for c in range(3)], rim, diag, trans, trans_before)
        b_out[...] = b
        x_out[...] = b * (OMEGA / stencil[0])
        emit_products(fine, stencil, x_out, buffers)

    b_fine, x_fine, *buffers = call(
        pressure_kernel,
        (rhs, iterate, diag, trans, trans_before, stencil, *got),
        [out(rows, LANES)] * 2 + fine.buffers(1),
        [(1, rows, LANES)],
    )
    got = swap(buffers)

    one = coarse_one.reshape(7, mid.rows, width // 2)
    one = jnp.repeat(one, 2, axis=2)
    low_depth, low_height, low_width = coarse_two.shape[1:]
    groups = LANES // low_width

    def pack(array, channels, dup):
        lead = array.shape[1] * array.shape[2]
        array = jnp.repeat(array, dup, axis=3) if dup > 1 else array
        array = jnp.pad(array, ((0, channels - array.shape[0]), (0, 0), (0, 0), (0, 0)))
        array = array.reshape(groups, channels // groups, lead, low_width).transpose(1, 2, 0, 3)
        return array.reshape(channels // groups * lead, LANES)

    packed = jnp.concatenate([pack(coarse_two, 8, 1), pack(coarse_three, 8, 2)])
    block = packed.shape[0]
    low_rows = low_depth * low_height

    def residual_kernel(b, x, stencil, one, *rest):
        got, (b_out, x_out), buffers, (ends, temp) = rest[:swaps], rest[swaps : swaps + 2], rest[swaps + 2 : -2], rest[-2:]
        (rim,) = fine.halos(got, 1, ends)
        residual = (1.0 - OMEGA) * b[...] - off_apply(stencil, x[...], rim)
        coarse = pair_sum_rows(pair_sum_x(residual, 1), depth, height, temp)
        b_out[...] = coarse
        x_out[...] = coarse * (OMEGA / one[0])
        emit_products(mid, one, x_out, buffers, True)

    b_mid, x_mid, *buffers = call(
        residual_kernel,
        (b_fine, x_fine, stencil, one, *got),
        [out(mid.rows, LANES)] * 2 + mid.buffers(2),
        [(1, rows, LANES), (rows // 2, LANES)],
    )
    mid_got = got = swap(buffers)

    def low_kernel(b, x, one, packed, *rest):
        got, (off_out, sent), (ends, temp) = rest[:swaps], rest[swaps : swaps + 2], rest[-2:]
        rim, _ = mid.halos(got, 2, ends)
        off = off_apply(one, x[...], rim)
        off_out[...] = off
        residual = (1.0 - OMEGA) * b[...] - off
        coarse = pair_sum_rows(residual, mid.depth, mid.height, temp)
        first = LANES - low_width
        place = one_hot((LANES, LANES), lambda i, j: (i // 4 == j - first) & (i % 2 == 0))
        filled = jnp.concatenate([packed[:low_rows], packed[low_rows : 2 * low_rows] + matmul(coarse, place), packed[2 * low_rows :]])
        sent[...] = jnp.broadcast_to(filled[None], (count, block, LANES))

    off_mid, sent = call(
        low_kernel,
        (b_mid, x_mid, one, packed, *got),
        [out(mid.rows, LANES), out(count, block, LANES)],
        [(2, mid.rows, LANES), (mid.rows // 2, LANES)],
    )
    everyone = lax.all_to_all(sent, AXES, 0, 0)

    two_rows, two_width = sizes[2] * low_depth * sizes[1] * low_height, sizes[0] * low_width
    two_height = sizes[1] * low_height
    three_height = two_height // 2
    three_rows = two_rows // 4

    def assemble(everyone, two, three):
        per = sizes[1] * sizes[2]
        for tile in range(two_width // LANES):
            parts = [everyone[(tile * groups + g) * per : (tile * groups + g + 1) * per].reshape(per * block, LANES) for g in range(groups)]
            lane = lane_of(parts[0])
            for q in range(groups):
                value = parts[0] if q == 0 else roll(parts[0], -low_width * q, 1)
                for g in range(1, groups):
                    value = jnp.where(lane // low_width == g, roll(parts[g], low_width * (g - q), 1), value)
                value = value.reshape(per, block, LANES)
                lanes = slice(tile * LANES, (tile + 1) * LANES)
                for y in range(sizes[1]):
                    for z in range(sizes[2]):
                        for half in range(8 // groups):
                            c = q * (8 // groups) + half
                            mine = value[y * sizes[2] + z]
                            for a in range(low_depth):
                                at = (z * low_depth + a) * two_height + y * low_height
                                start = (half * low_depth + a) * low_height
                                two[c, at : at + low_height, lanes] = mine[start : start + low_height]
                            low = low_height // 2
                            for a in range(low_depth // 2):
                                at = (z * (low_depth // 2) + a) * three_height + y * low
                                start = 8 // groups * low_rows + (half * (low_depth // 2) + a) * low
                                three[c, at : at + low, lanes] = mine[start : start + low]

    def solve_low(two, three, temp):
        closed = Closed(two_height, 1)
        b = two[7]
        scale = OMEGA / two[0]
        x = b * scale
        residual = (1.0 - OMEGA) * b - off_apply(two, x, closed)
        coarse = pair_sum_rows(pair_sum_x(residual, 1), sizes[2] * low_depth, two_height, temp)
        inner = Closed(three_height, 2)
        inner_scale = OMEGA / three[0]
        field = start = coarse * inner_scale
        for sweep in range(COARSE_SWEEPS - 1):
            field = start + (1.0 - OMEGA) * field - off_apply(three, field, inner) * inner_scale
        x = x + spread_rows(field, sizes[2] * low_depth // 2, three_height, temp)
        return (1.0 - OMEGA) * x + (b - off_apply(two, x, closed)) * scale

    def up_kernel(everyone, b, x, off, one, x_fine, stencil, *rest):
        got, field_out, buffers = rest[:swaps], rest[swaps], rest[swaps + 1 : -5]
        ends, two, three, low_temp, temp = rest[-5:]
        assemble(everyone, two, three)
        low = solve_low(two, three, low_temp)
        gx, gy, gz = (lax.axis_index(name) for name in AXES)
        h, d = mid.height, mid.depth
        own = one_hot((two_width, LANES), lambda i, j: i == gx * low_width + j // 4)
        beside = one_hot(
            (two_width, LANES),
            lambda i, j: ((j < 2) & (i == gx * low_width - 1)) | ((j >= LANES - 2) & (i == (gx + 1) * low_width)),
        )

        def picked(n, layer, y):
            def hit(i, j):
                return j == (gz * low_depth + layer(i)) * two_height + gy * low_height + y(i)

            return one_hot((n, two_rows), hit)

        picks = jnp.concatenate(
            [
                picked(d * h, lambda i: i // h // 2, lambda i: i % h // 2),
                picked(h, lambda i: -1, lambda i: i // 2),
                picked(h, lambda i: low_depth, lambda i: i // 2),
                picked(8, lambda i: i % d // 2, lambda i: jnp.where(i < d, -1, low_height)),
            ]
        )
        chosen = matmul(picks, low)
        around = matmul(chosen, own)
        add = around[: d * h]
        add_x = matmul(chosen[: d * h], beside)
        _, coefs = mid.halos(got, 2, ends)
        starts = d * h
        faces = [
            (coefs.faces[0][0] * around[starts : starts + h], coefs.faces[0][1] * around[starts + h : starts + 2 * h]),
            (
                coefs.faces[1][0] * around[starts + 2 * h : starts + 2 * h + d],
                coefs.faces[1][1] * around[starts + 2 * h + d : starts + 2 * h + 2 * d],
            ),
            (coefs.faces[2][0] * add_x, coefs.faces[2][1] * add_x),
        ]
        off_all = off[...] + off_apply(one, add, Rim(mid, faces, ends, 0))
        field = (1.0 - OMEGA) * (x[...] + add) + (b[...] - off_all) * (OMEGA / one[0])
        field_out[...] = x_fine[...] + spread_rows(field, d, h, temp)
        emit_products(fine, stencil, field_out, buffers)

    field, *buffers = call(
        up_kernel,
        (everyone, b_mid, x_mid, off_mid, one, x_fine, stencil, *got),
        [out(rows, LANES)] + fine.buffers(1),
        [(2, mid.rows, LANES), (8, two_rows, two_width), (8, three_rows, two_width), (two_rows, LANES), (rows // 2, LANES)],
    )
    got = swap(buffers)

    def adjoint_kernel(field, b, stencil, it, active, weights, *rest):
        got, adj_out, buffers, ends = rest[:swaps], rest[swaps], rest[swaps + 1 : -1], rest[-1]
        (rim,) = fine.halos(got, 1, ends)
        value = field[...]
        correction = (1.0 - OMEGA) * value + (b[...] - off_apply(stencil, value, rim)) * (OMEGA / stencil[0])
        mask = active[...].astype(F32)
        for c in range(3):
            adj_out[c] = mask * (it[c] + weights[c] * correction)
        fine.emit([[(loader(adj_out, c),) * 2 for c in range(3)]] * 3, buffers)

    adjoint, *buffers = call(
        adjoint_kernel,
        (field, b_fine, stencil, iterate, active, weights, *got),
        [out(3, rows, LANES)] + fine.buffers(3),
        [(1, rows, LANES)],
    )
    got = swap(buffers)

    def gradient_kernel(adj, mobility, pressure, trans, trans_before, *rest):
        got, state_got, (adj_out, grad_out) = rest[:swaps], rest[swaps : 2 * swaps], rest[2 * swaps : 2 * swaps + 2]
        ends, state_ends, grad, sems = rest[-4:]
        copies = [pltpu.make_async_copy(adj, adj_out, sems.at[3])]
        copies[0].start()
        adj_rims = fine.halos(got, 3, ends)
        state_rims = fine.halos(state_got, 7, state_ends)[3:]
        values = [adj[c] for c in range(3)]
        for dim in range(3):

            def term(trans, shift):
                total = 0.0
                for c in range(3):
                    mean = 0.5 * (mobility[c] + shift(state_rims[c], mobility[c]))
                    total = total + (values[c] - shift(adj_rims[c], values[c])) * mean
                return trans * total * (pressure[0] - shift(state_rims[3], pressure[0]))

            here = term(trans[dim], lambda rim, v: rim.following(v, dim))
            below = term(trans_before[dim], lambda rim, v: rim.previous(v, dim))
            grad[dim] = 0.5 * (here + below)
            copies.append(pltpu.make_async_copy(grad.at[dim], grad_out.at[dim], sems.at[dim]))
            copies[-1].start()
        for copy in copies:
            copy.wait()

    adjoint, gradient = call(
        gradient_kernel,
        (adjoint, mobility, pressure, trans, trans_before, *got, *state_got),
        [out(3, rows, LANES)] * 2,
        [(3, rows, LANES), (7, rows, LANES), (3, rows, LANES), pltpu.SemaphoreType.DMA((4,))],
        far_outputs=2,
    )
    shape = (3, depth, height, width)
    return adjoint.reshape(shape), gradient.reshape(shape)


def solution(mesh):
    cells = P("layer", "gy", "gx")
    fields = P(None, "layer", "gy", "gx")
    return jax.shard_map(
        local,
        mesh=mesh,
        in_specs=(
            fields,
            cells,
            fields,
            fields,
            fields,
            fields,
            fields,
            fields,
            fields,
            fields,
            cells,
            fields,
        ),
        out_specs=(fields, fields),
        check_vma=False,
    )
```

```python
import itertools

import jax
import jax.numpy as jnp
from jax import lax
from jax.experimental import pallas as pl
from jax.experimental.pallas import tpu as pltpu
from jax.sharding import PartitionSpec as P

SWEEPS = 3
LEVELS = 3
COARSE_SWEEPS = 4
OMEGA = 0.8
LANES = 128
AXES = ("gx", "gy", "layer")
BY_DIM = ("layer", "gy", "gx")
ORDER = ((0, 1), (0, 0), (1, 1), (1, 0), (2, 1), (2, 0))
HIGHEST = lax.Precision.HIGHEST
F32 = jnp.float32


def pair_route(axis, phase):
    sizes = [lax.axis_size(name) for name in AXES]
    k = AXES.index(axis)
    n = sizes[k]
    route = []
    for index in itertools.product(*[range(size) for size in sizes]):
        target = list(index)
        if phase == 0:
            target[k] = index[k] ^ 1
        elif 0 < index[k] < n - 1 or k == 0:
            target[k] = (((index[k] + 1) % n ^ 1) - 1) % n
        else:
            target[0] = index[0] ^ 1
        flat = [(i[0] * sizes[1] + i[1]) * sizes[2] + i[2] for i in (index, target)]
        route.append(tuple(flat))
    return route


def phases(dim):
    return min(lax.axis_size(BY_DIM[dim]), 3) - 1


def sends():
    return [(dim, phase) for dim, phase in ORDER if phase < phases(dim)]


def swap(buffers):
    return [lax.ppermute(b, AXES, pair_route(BY_DIM[dim], phase)) for b, (dim, phase) in zip(buffers, sends())]


class Grid:
    def __init__(self, depth, height, dup):
        self.depth, self.height, self.dup = depth, height, dup
        self.rows = depth * height
        self.groups = self.rows // 8
        self.stride = LANES // self.groups

    def lines(self, dim):
        return (self.height, self.depth)[dim]


class Message:
    def __init__(self, *parts):
        self.parts = parts

    def start(self, part, dim):
        return sum(8 if dim == 2 else count * grid.lines(dim) for grid, count in self.parts[:part])

    def buffers(self):
        return [jax.ShapeDtypeStruct((self.start(len(self.parts), dim), LANES), F32) for dim, phase in sends()]

    def emit(self, part, channels, out):
        out = dict(zip(sends(), out))
        grid, count = self.parts[part]
        lane = lax.broadcasted_iota(jnp.int32, (8, LANES), 1)
        for dim in range(3):
            if phases(dim) == 0:
                continue
            even = lax.axis_index(BY_DIM[dim]) % 2 == 0
            start = self.start(part, dim)
            if dim == 2:
                firsts, lasts = jnp.zeros((8, LANES), F32), jnp.zeros((8, LANES), F32)
                for c, (first, last) in enumerate(channels[dim]):
                    for k in range(grid.groups):
                        at = grid.stride * k + grid.dup * c
                        here = (lane >= at) & (lane < at + grid.dup)
                        rows = slice(8 * k, 8 * k + 8)
                        firsts = jnp.where(here, roll(first(rows), at, 1), firsts)
                        lasts = jnp.where(here, roll(last(rows), at + grid.dup, 1), lasts)
                pairs = [(slice(start, start + 8), firsts, lasts)]
            else:
                if dim == 0:
                    low, high = slice(0, grid.height), slice(grid.rows - grid.height, grid.rows)
                else:
                    low, high = (pl.ds(s, grid.depth, stride=grid.height) for s in (0, grid.height - 1))
                n = grid.lines(dim)
                pairs = [
                    (slice(start + c * n, start + (c + 1) * n), first(low), last(high))
                    for c, (first, last) in enumerate(channels[dim])
                ]
            for rows, first, last in pairs:
                out[dim, 0][rows] = jnp.where(even, last, first)
                if phases(dim) == 2:
                    out[dim, 1][rows] = jnp.where(even, first, last)

    def faces(self, part, got, channels=None):
        got = dict(zip(sends(), got))
        grid, count = self.parts[part]
        channels = range(count) if channels is None else channels
        result = [[None] * 3 for _ in channels]
        for dim in range(3):
            me, n = lax.axis_index(BY_DIM[dim]), lax.axis_size(BY_DIM[dim])
            even = me % 2 == 0
            start = self.start(part, dim)

            def both(rows):
                if phases(dim) == 0:
                    return (jnp.zeros((rows.stop - rows.start, LANES), F32),) * 2
                one = got[dim, 0][rows]
                if phases(dim) == 1:
                    return jnp.where(even, 0.0, one), jnp.where(even, one, 0.0)
                two = got[dim, 1][rows]
                before, after = jnp.where(even, two, one), jnp.where(even, one, two)
                return jnp.where(me > 0, before, 0.0), jnp.where(me < n - 1, after, 0.0)

            if dim == 2:
                sides = both(slice(start, start + 8))
                for i, c in enumerate(channels):
                    parts = []
                    for side, lane in zip(sides, (0, LANES - grid.dup)):
                        pieces = [roll(side, lane - grid.stride * k - grid.dup * c, 1) for k in range(grid.groups)]
                        parts.append(jnp.concatenate(pieces))
                    result[i][dim] = tuple(parts)
            else:
                size = grid.lines(dim)
                for i, c in enumerate(channels):
                    result[i][dim] = both(slice(start + c * size, start + (c + 1) * size))
        return result

    def halos(self, part, got, scratch, channels=None):
        return [Rim(self.parts[part][0], r, scratch, c) for c, r in enumerate(self.faces(part, got, channels))]


class Rim:
    def __init__(self, grid, faces, scratch, c):
        self.grid, self.faces = grid, faces
        ends = scratch.at[c]
        ends[pl.ds(0, grid.depth, stride=grid.height), :] = faces[1][0]
        ends[pl.ds(grid.height - 1, grid.depth, stride=grid.height), :] = faces[1][1]
        self.y_ends = ends[...]

    def previous(self, value, dim):
        g = self.grid
        if dim == 0:
            return jnp.concatenate([self.faces[0][0], value[: g.rows - g.height]])
        if dim == 1:
            return jnp.where(row_y(value, g.height) == 0, self.y_ends, roll(value, 1, 0))
        return jnp.where(lane_of(value) < g.dup, self.faces[2][0], roll(value, g.dup, 1))

    def following(self, value, dim):
        g = self.grid
        if dim == 0:
            return jnp.concatenate([value[g.height :], self.faces[0][1]])
        if dim == 1:
            return jnp.where(row_y(value, g.height) == g.height - 1, self.y_ends, roll(value, -1, 0))
        return jnp.where(lane_of(value) >= value.shape[1] - g.dup, self.faces[2][1], roll(value, -g.dup, 1))


class Closed:
    def __init__(self, height, dup):
        self.height, self.dup = height, dup

    def previous(self, value, dim):
        if dim == 0:
            return jnp.concatenate([jnp.zeros_like(value[: self.height]), value[: -self.height]])
        if dim == 1:
            return jnp.where(row_y(value, self.height) == 0, 0.0, roll(value, 1, 0))
        return jnp.where(lane_of(value) < self.dup, 0.0, roll(value, self.dup, 1))

    def following(self, value, dim):
        if dim == 0:
            return jnp.concatenate([value[self.height :], jnp.zeros_like(value[: self.height])])
        if dim == 1:
            return jnp.where(row_y(value, self.height) == self.height - 1, 0.0, roll(value, -1, 0))
        return jnp.where(lane_of(value) >= value.shape[1] - self.dup, 0.0, roll(value, -self.dup, 1))


def roll(value, shift, axis):
    shift %= value.shape[axis]
    return pltpu.roll(value, shift, axis) if shift else value


def row_y(value, height):
    return lax.broadcasted_iota(jnp.int32, value.shape, 0) % height


def lane_of(value):
    return lax.broadcasted_iota(jnp.int32, value.shape, 1)


def loader(ref, c):
    return lambda rows: ref[c, rows, :]


def product(coefs, k, ref):
    return lambda rows: coefs[k, rows, :] * ref[rows, :]


def off_apply(stencil, field, rim):
    total = 0.0
    for dim in range(3):
        total = total + rim.previous(stencil[2 + 2 * dim] * field, dim)
        total = total + rim.following(stencil[1 + 2 * dim] * field, dim)
    return total


def block_row(blocks, c, values):
    return blocks[c] * values[0] + blocks[3 + c] * values[1] + blocks[6 + c] * values[2]


def system_row(c, values, rim, blocks, trans, trans_before):
    total = block_row(blocks, c, values)
    v = values[c]
    for dim in range(3):
        total = total + trans[dim] * (v - rim.following(v, dim))
        total = total + trans_before[dim] * (v - rim.previous(v, dim))
    return total


def pair_sum_x(value, dup):
    odd = (lane_of(value) // dup) % 2 == 1
    return value + jnp.where(odd, roll(value, dup, 1), roll(value, -dup, 1))


def pair_sum_rows(value, depth, height, scratch):
    half = depth // 2
    parts = [value[2 * a * height : (2 * a + 1) * height] + value[(2 * a + 1) * height : (2 * a + 2) * height] for a in range(half)]
    whole = jnp.concatenate(parts)
    count = half * height // 2
    sums = []
    for at in range(0, whole.shape[1], LANES):
        scratch[: half * height, :] = whole[:, at : at + LANES]
        sums.append(scratch[pl.ds(0, count, stride=2), :] + scratch[pl.ds(1, count, stride=2), :])
    return jnp.concatenate(sums, axis=1)


def spread_rows(value, depth, height, scratch):
    count = depth * height
    tiles = []
    for at in range(0, value.shape[1], LANES):
        scratch[pl.ds(0, count, stride=2), :] = value[:, at : at + LANES]
        scratch[pl.ds(1, count, stride=2), :] = value[:, at : at + LANES]
        wide = scratch[: 2 * count, :]
        tiles.append(jnp.concatenate([wide[2 * height * (a // 2) : 2 * height * (a // 2 + 1)] for a in range(2 * depth)]))
    return jnp.concatenate(tiles, axis=1)


def spread_lines(value, scratch):
    count = value.shape[0]
    scratch[pl.ds(0, count, stride=2), :] = value
    scratch[pl.ds(1, count, stride=2), :] = value
    return scratch[: 2 * count, :]


def fold(value):
    half = value.shape[0] // 2
    return jnp.where(lane_of(value[:half]) % 2 == 0, value[:half], value[half:])


def unfold(value):
    even = lane_of(value) % 2 == 0
    return jnp.concatenate([jnp.where(even, value, roll(value, 1, 1)), jnp.where(even, roll(value, -1, 1), value)])


def one_hot(shape, hit):
    return jnp.where(hit(lax.broadcasted_iota(jnp.int32, shape, 0), lax.broadcasted_iota(jnp.int32, shape, 1)), 1.0, 0.0).astype(F32)


def matmul(a, b):
    return jnp.dot(a, b, precision=HIGHEST, preferred_element_type=F32)


def call(kernel, inputs, outputs, scratch=(), far_inputs=0, far_outputs=0):
    inputs = list(inputs)
    for i in range(far_inputs):
        inputs[i] = pltpu.with_memory_space_constraint(inputs[i], pltpu.HBM)

    def specs(count, far):
        return [pl.BlockSpec(memory_space=pltpu.HBM if i < far else pltpu.VMEM) for i in range(count)]

    return pl.pallas_call(
        kernel,
        out_shape=list(outputs),
        in_specs=specs(len(inputs), far_inputs),
        out_specs=specs(len(outputs), far_outputs),
        scratch_shapes=[pltpu.VMEM(shape, F32) if isinstance(shape, tuple) else shape for shape in scratch],
        compiler_params=pltpu.CompilerParams(vmem_limit_bytes=24 * 2**20),
    )(*inputs)


def local(
    source,
    active_cells,
    diag_blocks,
    frozen_inverses,
    transmissibility,
    pressure_weights,
    stencil_fine,
    coarse_one,
    coarse_two,
    coarse_three,
    pressure_state,
    mobilities,
):
    depth, height, width = active_cells.shape
    fine, mid = Grid(depth, height, 1), Grid(depth // 2, height // 2, 2)
    sizes = [lax.axis_size(name) for name in AXES]
    count = sizes[0] * sizes[1] * sizes[2]
    swaps = len(sends())
    first_round = Message((fine, 4))
    second_round = Message((fine, 8), (mid, 1))
    third_round = Message((fine, 1))
    fourth_round = Message((fine, 1), (mid, 6))
    fifth_round = Message((mid, 1))
    last_round = Message((fine, 3))
    rows = fine.rows

    def flat(array):
        return array.reshape(array.shape[:-3] + (rows, width))

    def out(*shape):
        return jax.ShapeDtypeStruct(shape, F32)

    source, active, diag, frozen, trans, weights, stencil, pressure, mobility = (
        flat(a)
        for a in (
            source,
            active_cells,
            diag_blocks,
            frozen_inverses,
            transmissibility,
            pressure_weights,
            stencil_fine,
            pressure_state,
            mobilities,
        )
    )
    pressure = pressure[None]

    def start_kernel(source, active, frozen, trans, rhs_out, it_out, frozen_out, trans_out, *rest):
        buffers, (source_in, active_in, sems) = rest[:-3], rest[-3:]
        order = [k for c in range(3) for k in (c, 3 + c, 6 + c)]
        pairs = [(active, active_in), (source, source_in)] + [(frozen.at[k], frozen_out.at[k]) for k in order]
        pairs.append((trans, trans_out))
        copies = [pltpu.make_async_copy(a, b, sems.at[i]) for i, (a, b) in enumerate(pairs)]
        for copy in copies:
            copy.start()
        copies[0].wait()
        mask = active_in[...].astype(F32)
        copies[1].wait()
        rhs = [source_in[c] * mask for c in range(3)]
        for c in range(3):
            rhs_out[c] = rhs[c]
        for c in range(3):
            for copy in copies[2 + 3 * c : 5 + 3 * c]:
                copy.wait()
            it_out[c] = block_row(frozen_out, c, rhs)
        copies[-1].wait()
        its = [(loader(it_out, c),) * 2 for c in range(3)]
        first_round.emit(0, [its + [(loader(trans_out, dim),) * 2] for dim in range(3)], buffers)

    rhs, iterate, frozen, trans, *buffers = call(
        start_kernel,
        (source, active, frozen, trans),
        [out(3, rows, LANES)] * 2 + [out(9, rows, LANES), out(3, rows, LANES)] + first_round.buffers(),
        [(3, rows, LANES), pltpu.VMEM((rows, LANES), jnp.int32), pltpu.SemaphoreType.DMA((12,))],
        far_inputs=4,
    )
    got = swap(buffers)

    one = jnp.repeat(coarse_one.reshape(7, mid.rows, width // 2), 2, axis=2)

    def coupling_faces(coefs):
        return [[(loader(coefs, 1 + 2 * dim), loader(coefs, 2 + 2 * dim))] for dim in range(3)]

    def sweep_one(rhs, it, frozen, diag, trans, mobility, pressure, stencil, one, *rest):
        got, (it_out, before_out), buffers, ends = rest[:swaps], rest[swaps : swaps + 2], rest[swaps + 2 : -1], rest[-1]
        rims = first_round.halos(0, got, ends)
        trans_before = [rims[3].previous(trans[dim], dim) for dim in range(3)]
        values = [it[c] for c in range(3)]
        rest = [rhs[c] - system_row(c, values, rims[c], diag, trans, trans_before) for c in range(3)]
        for c in range(3):
            before_out[c] = trans_before[c]
            it_out[c] = values[c] + block_row(frozen, c, rest)
        channels = [(loader(it_out, c),) * 2 for c in range(3)]
        channels += [(loader(mobility, c),) * 2 for c in range(3)] + [(loader(pressure, 0),) * 2]
        second_round.emit(0, [channels + faces for faces in coupling_faces(stencil)], buffers)
        second_round.emit(1, coupling_faces(one), buffers)

    iterate, trans_before, *buffers = call(
        sweep_one,
        (rhs, iterate, frozen, diag, trans, mobility, pressure, stencil, one, *got),
        [out(3, rows, LANES)] * 2 + second_round.buffers(),
        [(4, rows, LANES)],
    )
    second_got = swap(buffers)

    def couplings_kernel(stencil, one, *rest):
        got, outs, scratch = rest[:swaps], rest[swaps : swaps + 2], rest[swaps + 2 :]
        for part, channel, coefs, coupling, ends in ((0, 7, stencil, outs[0], scratch[0]), (1, 0, one, outs[1], scratch[1])):
            (rim,) = second_round.halos(part, got, ends, [channel])
            scale = OMEGA / coefs[0]
            for dim in range(3):
                coupling[2 * dim] = scale * rim.previous(coefs[2 + 2 * dim], dim)
                coupling[2 * dim + 1] = scale * rim.following(coefs[1 + 2 * dim], dim)

    fine_couplings, mid_couplings = call(
        couplings_kernel,
        (stencil, one, *second_got),
        [out(6, rows, LANES), out(6, mid.rows, LANES)],
        [(1, rows, LANES), (1, mid.rows, LANES)],
    )

    def sweep_two(rhs, it, frozen, diag, trans, trans_before, *rest):
        got, it_out, buffers, ends = rest[:swaps], rest[swaps], rest[swaps + 1 : -1], rest[-1]
        rims = second_round.halos(0, got, ends, range(3))
        values = [it[c] for c in range(3)]
        rest = [rhs[c] - system_row(c, values, rims[c], diag, trans, trans_before) for c in range(3)]
        for c in range(3):
            it_out[c] = values[c] + block_row(frozen, c, rest)
        third_round.emit(0, [[(loader(it_out, 0),) * 2]] * 3, buffers)

    iterate, *buffers = call(
        sweep_two,
        (rhs, iterate, frozen, diag, trans, trans_before, *second_got),
        [out(3, rows, LANES)] + third_round.buffers(),
        [(3, rows, LANES)],
    )
    got = swap(buffers)

    def products(coefs, field):
        return [[(product(coefs, 1 + 2 * dim, field), product(coefs, 2 + 2 * dim, field))] for dim in range(3)]

    def pressure_kernel(rhs, it, diag, trans, trans_before, stencil, mid_couplings, *rest):
        got, (b_out, x_out), buffers, ends = rest[:swaps], rest[swaps : swaps + 2], rest[swaps + 2 : -1], rest[-1]
        (rim,) = third_round.halos(0, got, ends)
        b = rhs[0] - system_row(0, [it[c] for c in range(3)], rim, diag, trans, trans_before)
        b_out[...] = b
        x_out[...] = b * (OMEGA / stencil[0])
        fourth_round.emit(0, products(stencil, x_out), buffers)
        fourth_round.emit(1, [[(loader(mid_couplings, c),) * 2 for c in range(6)]] * 3, buffers)

    b_fine, x_fine, *buffers = call(
        pressure_kernel,
        (rhs, iterate, diag, trans, trans_before, stencil, mid_couplings, *got),
        [out(rows, LANES)] * 2 + fourth_round.buffers(),
        [(1, rows, LANES)],
    )
    fourth_got = swap(buffers)

    low_depth, low_height, low_width = coarse_two.shape[1:]
    groups = LANES // low_width

    def pack(array, channels, dup):
        lead = array.shape[1] * array.shape[2]
        array = jnp.repeat(array, dup, axis=3) if dup > 1 else array
        array = jnp.pad(array, ((0, channels - array.shape[0]), (0, 0), (0, 0), (0, 0)))
        array = array.reshape(groups, channels // groups, lead, low_width).transpose(1, 2, 0, 3)
        return array.reshape(channels // groups * lead, LANES)

    packed = jnp.concatenate([pack(coarse_two, 8, 1), pack(coarse_three, 8, 2)])
    own_lines = mid.height // 2
    face_at = packed.shape[0]
    block = face_at + own_lines
    low_rows = low_depth * low_height

    def residual_kernel(b, x, stencil, one, *rest):
        got, (b_out, x_out, q_out), buffers = rest[:swaps], rest[swaps : swaps + 3], rest[swaps + 3 : -2]
        ends, temp = rest[-2:]
        (rim,) = fourth_round.halos(0, got, ends, [0])
        off = off_apply(stencil, x[...], rim)
        residual = (1.0 - OMEGA) * b[...] - off
        q_out[...] = (1.0 - OMEGA) * x[...] + (b[...] - off) * (OMEGA / stencil[0])
        coarse = pair_sum_rows(pair_sum_x(residual, 1), depth, height, temp)
        b_out[...] = coarse
        x_out[...] = coarse * (OMEGA / one[0])
        fifth_round.emit(0, products(one, x_out), buffers)

    b_mid, x_mid, q_fine, *buffers = call(
        residual_kernel,
        (b_fine, x_fine, stencil, one, *fourth_got),
        [out(mid.rows, LANES)] * 2 + [out(rows, LANES)] + fifth_round.buffers(),
        [(1, rows, LANES), (rows // 2, LANES)],
    )
    got = swap(buffers)

    rim_y = 4
    line = mid.height + 2 * rim_y
    window = (mid.depth + 4) * line

    def fill_window(ref, own, faces):
        for a in range(mid.depth):
            at = (a + 2) * line + rim_y
            ref[at : at + mid.height, :] = own[a * mid.height : (a + 1) * mid.height]
        if faces is not None:
            for a, value in ((1, faces[0][0]), (mid.depth + 2, faces[0][1])):
                ref[a * line + rim_y : a * line + rim_y + mid.height, :] = value
            for y, value in ((rim_y - 1, faces[1][0]), (rim_y + mid.height, faces[1][1])):
                ref[pl.ds(2 * line + y, mid.depth, stride=line), :] = value

    def beside_of(faces):
        return jnp.where(lane_of(faces[0]) < LANES // 2, faces[0], faces[1])

    def window_kernel(couplings, *rest):
        got, (around, beside) = rest[:swaps], rest[swaps:]
        around[...] = jnp.zeros(around.shape, F32)
        beside[...] = jnp.zeros(beside.shape, F32)
        for c, faces in enumerate(fourth_round.faces(1, got)):
            fill_window(around.at[c], couplings[c], faces)
            fill_window(beside.at[c], beside_of(faces[2]), None)

    around_couplings, beside_couplings = call(
        window_kernel, (mid_couplings, *fourth_got), [out(6, window, LANES)] * 2
    )

    def device(*steps):
        at = [lax.axis_index(name) for name in AXES]
        inside, flat = True, 0
        for position, size, step in zip(at, sizes, steps):
            inside = inside & (position + step >= 0) & (position + step < size)
        for position, size, step in zip(at, sizes, steps):
            flat = flat * size + jnp.where(inside, position + step, position)
        return flat

    steps = {(dim, sign): tuple(sign if name == BY_DIM[dim] else 0 for name in AXES) for dim in range(3) for sign in (-1, 1)}
    x_step = mid.stride

    def low_kernel(b, x, one, packed, *rest):
        got, (q_out, sent), (ends, temp) = rest[:swaps], rest[swaps : swaps + 2], rest[-2:]
        (rim,) = fifth_round.halos(0, got, ends, [0])
        off = off_apply(one, x[...], rim)
        residual = (1.0 - OMEGA) * b[...] - off
        q = (1.0 - OMEGA) * x[...] + (b[...] - off) * (OMEGA / one[0])
        q_out[...] = q
        coarse = pair_sum_rows(residual, mid.depth, mid.height, temp)
        first = LANES - low_width
        place = one_hot((LANES, LANES), lambda i, j: (i // 4 == j - first) & (i % 2 == 0))
        filled = jnp.concatenate(
            [
                packed[:low_rows],
                packed[low_rows : 2 * low_rows] + matmul(coarse, place),
                packed[2 * low_rows :],
                jnp.zeros((own_lines, LANES), F32),
            ]
        )
        sent[...] = jnp.broadcast_to(filled[None], (count, block, LANES))
        lane = lax.broadcasted_iota(jnp.int32, (8, LANES), 1)
        for sign in (-1, 1):
            value = fold(q[: mid.height] if sign < 0 else q[mid.rows - mid.height :])
            sent[device(*steps[0, sign]), face_at : face_at + own_lines, :] = value
            value = q_out[pl.ds(0 if sign < 0 else mid.height - 1, mid.depth, stride=mid.height), :]
            sent[device(*steps[1, sign]), face_at : face_at + mid.depth, :] = value
            value = jnp.zeros((8, LANES), F32)
            for k in range(mid.groups):
                at = x_step * k
                here = (lane >= at) & (lane < at + 2)
                value = jnp.where(here, roll(q[8 * k : 8 * k + 8], at if sign < 0 else at + 2, 1), value)
            sent[device(*steps[2, sign]), face_at : face_at + 4, :] = value[:4] + roll(value[4:], 2, 1)

    q_mid, sent = call(
        low_kernel,
        (b_mid, x_mid, one, packed, *got),
        [out(mid.rows, LANES), out(count, block, LANES)],
        [(1, mid.rows, LANES), (mid.rows // 2, LANES)],
    )
    everyone = lax.all_to_all(sent, AXES, 0, 0)

    two_rows, two_width = sizes[2] * low_depth * sizes[1] * low_height, sizes[0] * low_width
    two_height = sizes[1] * low_height
    three_height = two_height // 2
    three_rows = two_rows // 4

    def assemble(everyone, two, three):
        per = sizes[1] * sizes[2]
        for tile in range(two_width // LANES):
            parts = [everyone[(tile * groups + g) * per : (tile * groups + g + 1) * per].reshape(per * block, LANES) for g in range(groups)]
            lane = lane_of(parts[0])
            for q in range(groups):
                value = parts[0] if q == 0 else roll(parts[0], -low_width * q, 1)
                for g in range(1, groups):
                    value = jnp.where(lane // low_width == g, roll(parts[g], low_width * (g - q), 1), value)
                value = value.reshape(per, block, LANES)
                lanes = slice(tile * LANES, (tile + 1) * LANES)
                for y in range(sizes[1]):
                    for z in range(sizes[2]):
                        for half in range(8 // groups):
                            c = q * (8 // groups) + half
                            mine = value[y * sizes[2] + z]
                            for a in range(low_depth):
                                at = (z * low_depth + a) * two_height + y * low_height
                                start = (half * low_depth + a) * low_height
                                two[c, at : at + low_height, lanes] = mine[start : start + low_height]
                            low = low_height // 2
                            for a in range(low_depth // 2):
                                at = (z * (low_depth // 2) + a) * three_height + y * low
                                start = 8 // groups * low_rows + (half * (low_depth // 2) + a) * low
                                three[c, at : at + low, lanes] = mine[start : start + low]

    def solve_low(two, three, temp):
        closed = Closed(two_height, 1)
        b = two[7]
        scale = OMEGA / two[0]
        x = b * scale
        residual = (1.0 - OMEGA) * b - off_apply(two, x, closed)
        coarse = pair_sum_rows(pair_sum_x(residual, 1), sizes[2] * low_depth, two_height, temp)
        inner = Closed(three_height, 2)
        inner_scale = OMEGA / three[0]
        field = start = coarse * inner_scale
        for sweep in range(COARSE_SWEEPS - 1):
            field = start + (1.0 - OMEGA) * field - off_apply(three, field, inner) * inner_scale
        x = x + spread_rows(field, sizes[2] * low_depth // 2, three_height, temp)
        return (1.0 - OMEGA) * x + (b - off_apply(two, x, closed)) * scale

    def smooth_mid(low, everyone, q, around_couplings, beside_couplings, q_around, q_beside):
        gx, gy, gz = (lax.axis_index(name) for name in AXES)
        q_around[...] = jnp.zeros((window, LANES), F32)
        q_beside[...] = jnp.zeros((window, LANES), F32)
        got = {key: everyone[device(*step), face_at : face_at + own_lines, :] for key, step in steps.items()}
        layers = [unfold(got[0, sign]) for sign in (-1, 1)]
        lines = [got[1, sign][: mid.depth] for sign in (-1, 1)]
        sides = []
        for sign, start in ((-1, 0), (1, LANES - 2)):
            pieces = [roll(got[2, sign], start - x_step * k - 2 * half, 1) for k in range(mid.groups) for half in range(2)]
            sides.append(jnp.concatenate(pieces))
        fill_window(q_around, q, (layers, lines))
        fill_window(q_beside, beside_of(sides), None)

        def picked(i, j):
            layer, y = i // (2 * line) - 1, i % line // 2 - rim_y // 2
            return j == (gz * low_depth + layer) * two_height + gy * low_height + y

        def columns(i, j):
            own = (j < LANES) & (i == gx * low_width + j // 4)
            before = (j >= LANES) & (j < LANES + 2) & (i == gx * low_width - 1)
            after = (j >= 2 * LANES - 2) & (i == (gx + 1) * low_width)
            return own | before | after

        chosen = matmul(one_hot((window, two_rows), picked), low)
        both = matmul(chosen, one_hot((two_width, 2 * LANES), columns))
        around, beside = both[:, :LANES], both[:, LANES:]
        lane = lane_of(around)
        none = jnp.zeros((line, LANES), F32)
        results = []
        for value, q, couplings in ((around, q_around, around_couplings), (beside, q_beside, beside_couplings)):
            if value is around:
                shifts = [jnp.where(lane < 2, beside, roll(around, 2, 1)), jnp.where(lane >= LANES - 2, beside, roll(around, -2, 1))]
            else:
                shifts = [jnp.where(lane < LANES // 2, beside, around), jnp.where(lane < LANES // 2, around, beside)]
            shifts = [roll(value, 1, 0), roll(value, -1, 0)] + shifts
            shifts = [jnp.concatenate([none, value[:-line]]), jnp.concatenate([value[line:], none])] + shifts
            total = q[...] + (1.0 - OMEGA) * value
            for k in range(6):
                total = total - couplings[k] * shifts[k]
            results.append(total)
        return results

    def correct_fine(around, beside, q, couplings, ends, temp):
        def own(ref):
            lines = [ref[(a + 2) * line + rim_y : (a + 2) * line + rim_y + mid.height, :] for a in range(mid.depth)]
            return spread_rows(jnp.concatenate(lines), mid.depth, mid.height, temp)

        def layer(ref, a):
            return spread_lines(ref[a * line + rim_y : a * line + rim_y + mid.height, :], temp)

        def row(ref, y):
            return spread_lines(ref[pl.ds(2 * line + y, mid.depth, stride=line), :], temp)

        value, side = own(around), own(beside)
        faces = [
            (layer(around, 1), layer(around, mid.depth + 2)),
            (row(around, rim_y - 1), row(around, rim_y + mid.height)),
            (side, side),
        ]
        rim = Rim(fine, faces, ends, 0)
        total = q + (1.0 - OMEGA) * value
        for dim in range(3):
            total = total - couplings[2 * dim] * rim.previous(value, dim)
            total = total - couplings[2 * dim + 1] * rim.following(value, dim)
        return total

    def up_kernel(everyone, q_mid, around_couplings, beside_couplings, q_fine, fine_couplings, it, active, weights, *rest):
        adj_out, buffers = rest[0], rest[1:-7]
        ends, two, three, low_temp, temp, first, second = rest[-7:]
        assemble(everyone, two, three)
        low = solve_low(two, three, low_temp)
        around, beside = smooth_mid(low, everyone, q_mid[...], around_couplings, beside_couplings, first, second)
        first[...] = around
        second[...] = beside
        correction = correct_fine(first, second, q_fine[...], fine_couplings, ends, temp)
        mask = active[...].astype(F32)
        for c in range(3):
            adj_out[c] = mask * (it[c] + weights[c] * correction)
        last_round.emit(0, [[(loader(adj_out, c),) * 2 for c in range(3)]] * 3, buffers)

    adjoint, *buffers = call(
        up_kernel,
        (everyone, q_mid, around_couplings, beside_couplings, q_fine, fine_couplings, iterate, active, weights),
        [out(3, rows, LANES)] + last_round.buffers(),
        [
            (1, rows, LANES),
            (8, two_rows, two_width),
            (8, three_rows, two_width),
            (two_rows, LANES),
            (rows // 2, LANES),
            (window, LANES),
            (window, LANES),
        ],
    )
    got = swap(buffers)

    def gradient_kernel(adj, mobility, pressure, trans, trans_before, *rest):
        got, state_got, (adj_out, grad_out) = rest[:swaps], rest[swaps : 2 * swaps], rest[2 * swaps : 2 * swaps + 2]
        ends, state_ends, grad, sems = rest[-4:]
        copies = [pltpu.make_async_copy(adj, adj_out, sems.at[3])]
        copies[0].start()
        adj_rims = last_round.halos(0, got, ends)
        state_rims = second_round.halos(0, state_got, state_ends, range(3, 7))
        values = [adj[c] for c in range(3)]
        for dim in range(3):

            def term(trans, shift):
                total = 0.0
                for c in range(3):
                    mean = 0.5 * (mobility[c] + shift(state_rims[c], mobility[c]))
                    total = total + (values[c] - shift(adj_rims[c], values[c])) * mean
                return trans * total * (pressure[0] - shift(state_rims[3], pressure[0]))

            here = term(trans[dim], lambda rim, v: rim.following(v, dim))
            below = term(trans_before[dim], lambda rim, v: rim.previous(v, dim))
            grad[dim] = 0.5 * (here + below)
            copies.append(pltpu.make_async_copy(grad.at[dim], grad_out.at[dim], sems.at[dim]))
            copies[-1].start()
        for copy in copies:
            copy.wait()

    adjoint, gradient = call(
        gradient_kernel,
        (adjoint, mobility, pressure, trans, trans_before, *got, *second_got),
        [out(3, rows, LANES)] * 2,
        [(3, rows, LANES), (4, rows, LANES), (3, rows, LANES), pltpu.SemaphoreType.DMA((4,))],
        far_outputs=2,
    )
    shape = (3, depth, height, width)
    return adjoint.reshape(shape), gradient.reshape(shape)


def solution(mesh):
    cells = P("layer", "gy", "gx")
    fields = P(None, "layer", "gy", "gx")
    return jax.shard_map(
        local,
        mesh=mesh,
        in_specs=(
            fields,
            cells,
            fields,
            fields,
            fields,
            fields,
            fields,
            fields,
            fields,
            fields,
            cells,
            fields,
        ),
        out_specs=(fields, fields),
        check_vma=False,
    )
```

```python
import itertools

import jax
import jax.numpy as jnp
from jax import lax
from jax.experimental import pallas as pl
from jax.experimental.pallas import tpu as pltpu
from jax.sharding import PartitionSpec as P

SWEEPS = 3
LEVELS = 3
COARSE_SWEEPS = 4
OMEGA = 0.8
LANES = 128
AXES = ("gx", "gy", "layer")
BY_DIM = ("layer", "gy", "gx")
ORDER = ((0, 1), (0, 0), (1, 1), (1, 0), (2, 1), (2, 0))
HIGHEST = lax.Precision.HIGHEST
F32 = jnp.float32


def pair_route(axis, phase):
    sizes = [lax.axis_size(name) for name in AXES]
    k = AXES.index(axis)
    n = sizes[k]
    route = []
    for index in itertools.product(*[range(size) for size in sizes]):
        target = list(index)
        if phase == 0:
            target[k] = index[k] ^ 1
        elif 0 < index[k] < n - 1 or k == 0:
            target[k] = (((index[k] + 1) % n ^ 1) - 1) % n
        else:
            target[0] = index[0] ^ 1
        flat = [(i[0] * sizes[1] + i[1]) * sizes[2] + i[2] for i in (index, target)]
        route.append(tuple(flat))
    return route


def phases(dim):
    return min(lax.axis_size(BY_DIM[dim]), 3) - 1


def sends():
    return [(dim, phase) for dim, phase in ORDER if phase < phases(dim)]


def swap(buffers):
    return [lax.ppermute(b, AXES, pair_route(BY_DIM[dim], phase)) for b, (dim, phase) in zip(buffers, sends())]


class Grid:
    def __init__(self, depth, height, dup):
        self.depth, self.height, self.dup = depth, height, dup
        self.rows = depth * height
        self.width = LANES // dup
        self.groups = self.rows // 8
        self.stride = LANES // self.groups

    def lines(self, dim):
        return (self.height, self.depth)[dim]


class Message:
    def __init__(self, *parts):
        self.parts = parts

    def size(self, part, dim):
        part = self.parts[part]
        if isinstance(part, dict):
            return part.get(dim, 0)
        if dim not in part[2:] and len(part) > 2:
            return 0
        return 8 if dim == 2 else part[1] * part[0].lines(dim)

    def start(self, part, dim):
        return sum(self.size(i, dim) for i in range(part))

    def buffers(self):
        return [jax.ShapeDtypeStruct((self.start(len(self.parts), dim), LANES), F32) for dim, phase in sends()]

    def put(self, dim, rows, first, last, out):
        if phases(dim) == 0:
            return
        out = dict(zip(sends(), out))
        even = lax.axis_index(BY_DIM[dim]) % 2 == 0
        out[dim, 0][rows] = jnp.where(even, last, first)
        if phases(dim) == 2:
            out[dim, 1][rows] = jnp.where(even, first, last)

    def put_rows(self, part, dim, first, last, out):
        start = self.start(part, dim)
        self.put(dim, slice(start, start + self.size(part, dim)), first, last, out)

    def emit(self, part, channels, out):
        grid = self.parts[part][0]
        lane = lax.broadcasted_iota(jnp.int32, (8, LANES), 1)
        for dim in range(3):
            if self.size(part, dim) == 0:
                continue
            start = self.start(part, dim)
            if dim == 2:
                firsts, lasts = jnp.zeros((8, LANES), F32), jnp.zeros((8, LANES), F32)
                for c, (first, last) in enumerate(channels[dim]):
                    for k in range(grid.groups):
                        at = grid.stride * k + grid.dup * c
                        here = (lane >= at) & (lane < at + grid.dup)
                        rows = slice(8 * k, 8 * k + 8)
                        firsts = jnp.where(here, roll(first(rows), at, 1), firsts)
                        lasts = jnp.where(here, roll(last(rows), at + grid.dup, 1), lasts)
                self.put(dim, slice(start, start + 8), firsts, lasts, out)
                continue
            if dim == 0:
                low, high = slice(0, grid.height), slice(grid.rows - grid.height, grid.rows)
            else:
                low, high = (pl.ds(s, grid.depth, stride=grid.height) for s in (0, grid.height - 1))
            n = grid.lines(dim)
            for c, (first, last) in enumerate(channels[dim]):
                self.put(dim, slice(start + c * n, start + (c + 1) * n), first(low), last(high), out)

    def both(self, dim, rows, got):
        if phases(dim) == 0:
            return (jnp.zeros((rows.stop - rows.start, LANES), F32),) * 2
        got = dict(zip(sends(), got))
        me, n = lax.axis_index(BY_DIM[dim]), lax.axis_size(BY_DIM[dim])
        even = me % 2 == 0
        one = got[dim, 0][rows]
        if phases(dim) == 1:
            return jnp.where(even, 0.0, one), jnp.where(even, one, 0.0)
        two = got[dim, 1][rows]
        before, after = jnp.where(even, two, one), jnp.where(even, one, two)
        return jnp.where(me > 0, before, 0.0), jnp.where(me < n - 1, after, 0.0)

    def rows(self, part, dim, got):
        start = self.start(part, dim)
        return self.both(dim, slice(start, start + self.size(part, dim)), got)

    def faces(self, part, got, channels=None):
        grid, count = self.parts[part][:2]
        channels = range(count) if channels is None else channels
        result = [[None] * 3 for _ in channels]
        for dim in range(3):
            if self.size(part, dim) == 0:
                continue
            start = self.start(part, dim)
            if dim == 2:
                sides = self.both(dim, slice(start, start + 8), got)
                for i, c in enumerate(channels):
                    parts = []
                    for side, lane in zip(sides, (0, LANES - grid.dup)):
                        pieces = [roll(side, lane - grid.stride * k - grid.dup * c, 1) for k in range(grid.groups)]
                        parts.append(jnp.concatenate(pieces))
                    result[i][dim] = tuple(parts)
            else:
                size = grid.lines(dim)
                for i, c in enumerate(channels):
                    result[i][dim] = self.both(dim, slice(start + c * size, start + (c + 1) * size), got)
        return result

    def halos(self, part, got, scratch, channels=None):
        return [Rim(self.parts[part][0], r, scratch, c) for c, r in enumerate(self.faces(part, got, channels))]


class Window:
    def __init__(self, grid, rim):
        self.grid, self.rim = grid, rim
        self.line = grid.height + 2 * rim
        self.rows = (grid.depth + 4) * self.line

    def at(self, layer, y):
        return (layer + 2) * self.line + self.rim + y

    def layer(self, layer):
        return slice(self.at(layer, 0), self.at(layer, self.grid.height))

    def row(self, y):
        return pl.ds(self.at(0, y), self.grid.depth, stride=self.line)

    def fill(self, ref, own):
        height = self.grid.height
        for a in range(self.grid.depth):
            ref[self.layer(a), :] = own[a * height : (a + 1) * height]


class Rim:
    def __init__(self, grid, faces, scratch, c):
        self.grid, self.faces = grid, faces
        ends = scratch.at[c]
        ends[pl.ds(0, grid.depth, stride=grid.height), :] = faces[1][0]
        ends[pl.ds(grid.height - 1, grid.depth, stride=grid.height), :] = faces[1][1]
        self.y_ends = ends[...]

    def previous(self, value, dim):
        g = self.grid
        if dim == 0:
            return jnp.concatenate([self.faces[0][0], value[: g.rows - g.height]])
        if dim == 1:
            return jnp.where(row_y(value, g.height) == 0, self.y_ends, roll(value, 1, 0))
        return jnp.where(lane_of(value) < g.dup, self.faces[2][0], roll(value, g.dup, 1))

    def following(self, value, dim):
        g = self.grid
        if dim == 0:
            return jnp.concatenate([value[g.height :], self.faces[0][1]])
        if dim == 1:
            return jnp.where(row_y(value, g.height) == g.height - 1, self.y_ends, roll(value, -1, 0))
        return jnp.where(lane_of(value) >= value.shape[1] - g.dup, self.faces[2][1], roll(value, -g.dup, 1))


class Closed:
    def __init__(self, height, dup):
        self.height, self.dup = height, dup

    def previous(self, value, dim):
        if dim == 0:
            return jnp.concatenate([jnp.zeros_like(value[: self.height]), value[: -self.height]])
        if dim == 1:
            return jnp.where(row_y(value, self.height) == 0, 0.0, roll(value, 1, 0))
        return jnp.where(lane_of(value) < self.dup, 0.0, roll(value, self.dup, 1))

    def following(self, value, dim):
        if dim == 0:
            return jnp.concatenate([value[self.height :], jnp.zeros_like(value[: self.height])])
        if dim == 1:
            return jnp.where(row_y(value, self.height) == self.height - 1, 0.0, roll(value, -1, 0))
        return jnp.where(lane_of(value) >= value.shape[1] - self.dup, 0.0, roll(value, -self.dup, 1))


def roll(value, shift, axis):
    shift %= value.shape[axis]
    return pltpu.roll(value, shift, axis) if shift else value


def row_y(value, height):
    return lax.broadcasted_iota(jnp.int32, value.shape, 0) % height


def lane_of(value):
    return lax.broadcasted_iota(jnp.int32, value.shape, 1)


def loader(ref, c):
    return lambda rows: ref[c, rows, :]


def product(coefs, k, ref):
    return lambda rows: coefs[k, rows, :] * ref[rows, :]


def off_apply(stencil, field, rim):
    total = 0.0
    for dim in range(3):
        total = total + rim.previous(stencil[2 + 2 * dim] * field, dim)
        total = total + rim.following(stencil[1 + 2 * dim] * field, dim)
    return total


def block_row(blocks, c, values):
    return blocks[c] * values[0] + blocks[3 + c] * values[1] + blocks[6 + c] * values[2]


def system_row(c, values, rim, blocks, trans, trans_before):
    total = block_row(blocks, c, values)
    v = values[c]
    for dim in range(3):
        total = total + trans[dim] * (v - rim.following(v, dim))
        total = total + trans_before[dim] * (v - rim.previous(v, dim))
    return total


def pair_sum_x(value, dup):
    odd = (lane_of(value) // dup) % 2 == 1
    return value + jnp.where(odd, roll(value, dup, 1), roll(value, -dup, 1))


def pair_sum_rows(value, depth, height, scratch):
    half = depth // 2
    parts = [value[2 * a * height : (2 * a + 1) * height] + value[(2 * a + 1) * height : (2 * a + 2) * height] for a in range(half)]
    whole = jnp.concatenate(parts)
    count = half * height // 2
    sums = []
    for at in range(0, whole.shape[1], LANES):
        scratch[: half * height, :] = whole[:, at : at + LANES]
        sums.append(scratch[pl.ds(0, count, stride=2), :] + scratch[pl.ds(1, count, stride=2), :])
    return jnp.concatenate(sums, axis=1)


def spread_rows(value, depth, height, scratch):
    count = depth * height
    tiles = []
    for at in range(0, value.shape[1], LANES):
        scratch[pl.ds(0, count, stride=2), :] = value[:, at : at + LANES]
        scratch[pl.ds(1, count, stride=2), :] = value[:, at : at + LANES]
        wide = scratch[: 2 * count, :]
        tiles.append(jnp.concatenate([wide[2 * height * (a // 2) : 2 * height * (a // 2 + 1)] for a in range(2 * depth)]))
    return jnp.concatenate(tiles, axis=1)


def spread_lines(value, scratch):
    count = value.shape[0]
    scratch[pl.ds(0, count, stride=2), :] = value
    scratch[pl.ds(1, count, stride=2), :] = value
    return scratch[: 2 * count, :]


def fold(value):
    half = value.shape[0] // 2
    return jnp.where(lane_of(value[:half]) % 2 == 0, value[:half], value[half:])


def unfold(value):
    even = lane_of(value) % 2 == 0
    return jnp.concatenate([jnp.where(even, value, roll(value, 1, 1)), jnp.where(even, roll(value, -1, 1), value)])


def beside_of(before, after):
    return jnp.where(lane_of(before) < LANES // 2, before, after)


def pack_sides(values, dup):
    total = jnp.zeros_like(values[0])
    lane = lane_of(total)
    for c, value in enumerate(values):
        total = jnp.where((lane >= dup * c) & (lane < dup * (c + 1)), roll(value, dup * c, 1), total)
        high = LANES - dup * c
        total = jnp.where((lane >= high - dup) & (lane < high), roll(value, -dup * c, 1), total)
    return total


def unpack_side(value, c, dup):
    return beside_of(roll(value, -dup * c, 1), roll(value, dup * c, 1))


def moved(rows, by):
    if isinstance(rows, slice):
        return slice(rows.start + by, rows.stop + by)
    return pl.ds(rows.start + by, rows.size, stride=rows.stride)


def shifts_of(value, inner, outer, line, dup, beside):
    none = jnp.zeros((line, LANES), F32)
    lane = lane_of(value)
    if beside:
        low, high = jnp.where(lane < LANES // 2, outer, inner), jnp.where(lane < LANES // 2, inner, outer)
    else:
        low, high = jnp.where(lane < dup, outer, roll(value, dup, 1)), jnp.where(lane >= LANES - dup, outer, roll(value, -dup, 1))
    return [
        jnp.concatenate([none, value[:-line]]),
        jnp.concatenate([value[line:], none]),
        roll(value, 1, 0),
        roll(value, -1, 0),
        low,
        high,
    ]


def smooth(x, added, couplings, line, dup):
    around, beside, second = x[0] + added[0], x[1] + added[1], x[2] + added[1]
    results = []
    for k, (value, shifts) in enumerate(
        (
            (around, shifts_of(around, None, beside, line, dup, False)),
            (beside, shifts_of(beside, around, second, line, dup, True)),
        )
    ):
        total = x[k] + (1.0 - OMEGA) * value
        for c in range(6):
            total = total - couplings[k](c) * shifts[c]
        results.append(total)
    return results


def one_hot(shape, hit):
    return jnp.where(hit(lax.broadcasted_iota(jnp.int32, shape, 0), lax.broadcasted_iota(jnp.int32, shape, 1)), 1.0, 0.0).astype(F32)


def matmul(a, b):
    return jnp.dot(a, b, precision=HIGHEST, preferred_element_type=F32)


def call(kernel, inputs, outputs, scratch=(), far_inputs=0, far_outputs=0):
    inputs = list(inputs)
    for i in range(far_inputs):
        inputs[i] = pltpu.with_memory_space_constraint(inputs[i], pltpu.HBM)

    def specs(count, far):
        return [pl.BlockSpec(memory_space=pltpu.HBM if i < far else pltpu.VMEM) for i in range(count)]

    return pl.pallas_call(
        kernel,
        out_shape=list(outputs),
        in_specs=specs(len(inputs), far_inputs),
        out_specs=specs(len(outputs), far_outputs),
        scratch_shapes=[pltpu.VMEM(shape, F32) if isinstance(shape, tuple) else shape for shape in scratch],
        compiler_params=pltpu.CompilerParams(vmem_limit_bytes=24 * 2**20),
    )(*inputs)


def local(
    source,
    active_cells,
    diag_blocks,
    frozen_inverses,
    transmissibility,
    pressure_weights,
    stencil_fine,
    coarse_one,
    coarse_two,
    coarse_three,
    pressure_state,
    mobilities,
):
    depth, height, width = active_cells.shape
    low_depth, low_height, low_width = coarse_two.shape[1:]
    last_height, last_width = coarse_three.shape[2:]
    fine = Grid(depth, height, 1)
    mid = Grid(depth // 2, height // 2, 2)
    low = Grid(low_depth, low_height, 4)
    mid_window, low_window = Window(mid, 4), Window(low, 2)
    sizes = [lax.axis_size(name) for name in AXES]
    count = sizes[0] * sizes[1] * sizes[2]
    swaps = len(sends())
    rows = fine.rows
    first_round = Message((fine, 4), (mid, 1), (low, 1))
    second_round = Message((fine, 8))
    third_round = Message((fine, 4), (mid, 6, 2), (low, 6, 2))
    fourth_round = Message((fine, 7), {1: 7 * mid.depth}, {1: 7 * low.depth})
    fifth_round = Message((fine, 3), (mid, 2), {0: 4 * mid_window.line}, {0: 4 * low_window.line})

    def flat(array):
        return array.reshape(array.shape[:-3] + (rows, width))

    def out(*shape):
        return jax.ShapeDtypeStruct(shape, F32)

    source, active, diag, frozen, trans, weights, stencil, pressure, mobility = (
        flat(a)
        for a in (
            source,
            active_cells,
            diag_blocks,
            frozen_inverses,
            transmissibility,
            pressure_weights,
            stencil_fine,
            pressure_state,
            mobilities,
        )
    )
    pressure = pressure[None]

    def coupling_faces(coefs):
        return [[(loader(coefs, 1 + 2 * dim), loader(coefs, 2 + 2 * dim))] for dim in range(3)]

    def widen(values, dup):
        wide = matmul(values, one_hot((values.shape[1], LANES), lambda i, j: i == j // dup))
        return wide.reshape(7, wide.shape[0] // 7, LANES)

    def start_kernel(source, active, frozen, trans, one, two, rhs_out, it_out, frozen_out, trans_out, one_out, two_out, *rest):
        buffers, (source_in, active_in, one_in, two_in, two_flat, sems) = rest[:-6], rest[-6:]
        order = [k for c in range(3) for k in (c, 3 + c, 6 + c)]
        pairs = [(active, active_in), (source, source_in)] + [(frozen.at[k], frozen_out.at[k]) for k in order]
        pairs += [(trans, trans_out), (one, one_in), (two, two_in)]
        copies = [pltpu.make_async_copy(a, b, sems.at[i]) for i, (a, b) in enumerate(pairs)]
        for copy in copies[-2:] + copies[:-2]:
            copy.start()
        copies[-2].wait()
        copies[-1].wait()
        one_out[...] = widen(one_in[...].reshape(7 * mid.rows, mid.width), mid.dup)
        for c in range(7):
            for a in range(low.depth):
                at = c * low.rows + a * low.height
                two_flat[at : at + low.height, :] = two_in[c, a]
        two_out[...] = widen(two_flat[...], low.dup)
        first_round.emit(1, coupling_faces(one_out), buffers)
        first_round.emit(2, coupling_faces(two_out), buffers)
        copies[0].wait()
        mask = active_in[...].astype(F32)
        copies[1].wait()
        rhs = [source_in[c] * mask for c in range(3)]
        for c in range(3):
            rhs_out[c] = rhs[c]
        for c in range(3):
            for copy in copies[2 + 3 * c : 5 + 3 * c]:
                copy.wait()
            it_out[c] = block_row(frozen_out, c, rhs)
        copies[-3].wait()
        its = [(loader(it_out, c),) * 2 for c in range(3)]
        first_round.emit(0, [its + [(loader(trans_out, dim),) * 2] for dim in range(3)], buffers)

    rhs, iterate, frozen, trans, one, two, *buffers = call(
        start_kernel,
        (source, active, frozen, trans, coarse_one.reshape(7, mid.rows, mid.width), coarse_two),
        [out(3, rows, LANES)] * 2
        + [out(9, rows, LANES), out(3, rows, LANES), out(7, mid.rows, LANES), out(7, low.rows, LANES)]
        + first_round.buffers(),
        [
            (3, rows, LANES),
            pltpu.VMEM((rows, LANES), jnp.int32),
            (7, mid.rows, mid.width),
            (7, low.depth, low.height, low.width),
            (7 * low.rows, low.width),
            pltpu.SemaphoreType.DMA((14,)),
        ],
        far_inputs=6,
    )
    got = swap(buffers)

    def couplings(coefs, rim, result):
        scale = OMEGA / coefs[0]
        for dim in range(3):
            result[2 * dim] = scale * rim.previous(coefs[2 + 2 * dim], dim)
            result[2 * dim + 1] = scale * rim.following(coefs[1 + 2 * dim], dim)

    def coarse_couplings(one, two, *rest):
        got, outs, scratch = rest[:swaps], rest[swaps : swaps + 2], rest[swaps + 2 :]
        for part, coefs, result, ends in ((1, one, outs[0], scratch[0]), (2, two, outs[1], scratch[1])):
            couplings(coefs, first_round.halos(part, got, ends)[0], result)

    mid_couplings, low_couplings = call(
        coarse_couplings,
        (one, two, *got),
        [out(6, mid.rows, LANES), out(6, low.rows, LANES)],
        [(1, mid.rows, LANES), (1, low.rows, LANES)],
    )

    def sweep_one(rhs, it, frozen, diag, trans, mobility, pressure, stencil, *rest):
        got, (it_out, before_out), buffers, ends = rest[:swaps], rest[swaps : swaps + 2], rest[swaps + 2 : -1], rest[-1]
        rims = first_round.halos(0, got, ends)
        trans_before = [rims[3].previous(trans[dim], dim) for dim in range(3)]
        values = [it[c] for c in range(3)]
        rest = [rhs[c] - system_row(c, values, rims[c], diag, trans, trans_before) for c in range(3)]
        for c in range(3):
            before_out[c] = trans_before[c]
            it_out[c] = values[c] + block_row(frozen, c, rest)
        channels = [(loader(it_out, c),) * 2 for c in range(3)]
        channels += [(loader(mobility, c),) * 2 for c in range(3)] + [(loader(pressure, 0),) * 2]
        second_round.emit(0, [channels + faces for faces in coupling_faces(stencil)], buffers)

    iterate, trans_before, *buffers = call(
        sweep_one,
        (rhs, iterate, frozen, diag, trans, mobility, pressure, stencil, *got),
        [out(3, rows, LANES)] * 2 + second_round.buffers(),
        [(4, rows, LANES)],
    )
    second_got = swap(buffers)

    def same(ref, channels):
        return [(loader(ref, c),) * 2 for c in channels]

    def sweep_two(rhs, it, frozen, diag, trans, trans_before, active, weights, mid_couplings, low_couplings, *rest):
        got, it_out, buffers, ends = rest[:swaps], rest[swaps], rest[swaps + 1 : -1], rest[-1]
        rims = second_round.halos(0, got, ends, range(3))
        values = [it[c] for c in range(3)]
        rest = [rhs[c] - system_row(c, values, rims[c], diag, trans, trans_before) for c in range(3)]
        for c in range(3):
            it_out[c] = values[c] + block_row(frozen, c, rest)
        factors = [(lambda at, c=c: active[at, :].astype(F32) * weights[c, at, :],) * 2 for c in range(3)]
        third_round.emit(0, [same(it_out, range(1)) + factors] * 3, buffers)
        third_round.emit(1, [same(mid_couplings, range(6))] * 3, buffers)
        third_round.emit(2, [same(low_couplings, range(6))] * 3, buffers)

    iterate, *buffers = call(
        sweep_two,
        (rhs, iterate, frozen, diag, trans, trans_before, active, weights, mid_couplings, low_couplings, *second_got),
        [out(3, rows, LANES)] + third_round.buffers(),
        [(3, rows, LANES)],
    )
    third_got = swap(buffers)

    def fine_kernel(stencil, *rest):
        got, (result, ends) = rest[:swaps], rest[swaps:]
        couplings(stencil, second_round.halos(0, got, ends, [7])[0], result)

    (fine_couplings,) = call(fine_kernel, (stencil, *second_got), [out(6, rows, LANES)], [(1, rows, LANES)])

    def products(coefs, field):
        return [[(product(coefs, 1 + 2 * dim, field), product(coefs, 2 + 2 * dim, field))] for dim in range(3)]

    def pressure_kernel(rhs, it, diag, trans, trans_before, stencil, fine_couplings, mid_couplings, low_couplings, *rest):
        got, (b_out, x_out, mid_side, low_side), buffers = rest[:swaps], rest[swaps : swaps + 4], rest[swaps + 4 : -1]
        (rim,) = third_round.halos(0, got, rest[-1], [0])
        b = rhs[0] - system_row(0, [it[c] for c in range(3)], rim, diag, trans, trans_before)
        b_out[...] = b
        x_out[...] = b * (OMEGA / stencil[0])
        ours = same(fine_couplings, range(6))
        fourth_round.emit(0, [faces + ours for faces in products(stencil, x_out)], buffers)
        for part, grid, values, side in ((1, mid, mid_couplings, mid_side), (2, low, low_couplings, low_side)):
            side[...] = pack_sides([beside_of(*faces[2]) for faces in third_round.faces(part, got)], grid.dup)
            ends = []
            for y in (0, grid.height - 1):
                lines = pl.ds(y, grid.depth, stride=grid.height)
                parts = [values[c, lines, :] for c in range(6)]
                ends.append(jnp.concatenate(parts + [side[lines, :]]))
            fourth_round.put_rows(part, 1, *ends, buffers)

    b_fine, x_fine, mid_side, low_side, *buffers = call(
        pressure_kernel,
        (rhs, iterate, diag, trans, trans_before, stencil, fine_couplings, mid_couplings, low_couplings, *third_got),
        [out(rows, LANES)] * 2 + [out(mid.rows, LANES), out(low.rows, LANES)] + fourth_round.buffers(),
        [(1, rows, LANES)],
    )
    fourth_got = swap(buffers)

    def residual_kernel(b, x, stencil, one, it, active, weights, mid_own, mid_side, low_own, low_side, *rest):
        got, (x_out, adj_out, factor_out), windows = rest[:swaps], rest[swaps : swaps + 3], rest[swaps + 3 : swaps + 7]
        buffers, (ends, temp) = rest[swaps + 7 : -2], rest[-2:]
        (rim,) = fourth_round.halos(0, got, ends, [0])
        off = off_apply(stencil, x[...], rim)
        residual = (1.0 - OMEGA) * b[...] - off
        q = (1.0 - OMEGA) * x[...] + (b[...] - off) * (OMEGA / stencil[0])
        mask = active[...].astype(F32)
        for c in range(3):
            factor = mask * weights[c]
            factor_out[c] = factor
            adj_out[c] = mask * it[c] + factor * q
        coarse = pair_sum_rows(pair_sum_x(residual, 1), depth, height, temp)
        x_out[...] = coarse * (OMEGA / one[0])
        fifth_round.emit(0, [same(adj_out, range(3))] * 3, buffers)
        near = (lambda at: x_out[at, :],) * 2
        channels = []
        for step in (mid.height, 1):
            channels.append([near, (lambda at, s=step: x_out[moved(at, s), :], lambda at, s=step: x_out[moved(at, -s), :])])
        channels.append([near, (lambda at: roll(x_out[at, :], -mid.dup, 1), lambda at: roll(x_out[at, :], mid.dup, 1))])
        fifth_round.emit(1, channels, buffers)
        for part, window, own, side, ours, theirs in (
            (1, mid_window, mid_own, mid_side, windows[0], windows[1]),
            (2, low_window, low_own, low_side, windows[2], windows[3]),
        ):
            grid, line = window.grid, window.line
            halves = fourth_round.rows(part, 1, got)
            ours[...] = jnp.zeros(ours.shape, F32)
            theirs[...] = jnp.zeros(theirs.shape, F32)
            pairs = [(ours.at[c], own.at[c], c) for c in range(6)] + [(theirs, side, 6)]
            for ref, source, c in pairs:
                for a in range(grid.depth):
                    at = a * line + window.rim
                    ref[at : at + grid.height, :] = source[a * grid.height : (a + 1) * grid.height, :]
                for y, half in zip((-1, grid.height), halves):
                    ref[pl.ds(window.rim + y, grid.depth, stride=line), :] = half[c * grid.depth : (c + 1) * grid.depth]
            ends = []
            for a in (0, grid.depth - 1):
                lines = slice(a * line, (a + 1) * line)
                parts = [fold(jnp.concatenate([ours[c, lines, :], ours[c + 1, lines, :]])) for c in (0, 2, 4)]
                ends.append(jnp.concatenate(parts + [theirs[lines, :]]))
            fifth_round.put_rows(part + 1, 0, *ends, buffers)

    mid_lines, low_lines = (mid.depth * mid_window.line, LANES), (low.depth * low_window.line, LANES)
    x_mid, adj_known, adj_factor, mid_around, mid_beside, low_around, low_beside, *buffers = call(
        residual_kernel,
        (b_fine, x_fine, stencil, one, iterate, active, weights, mid_couplings, mid_side, low_couplings, low_side, *fourth_got),
        [out(mid.rows, LANES), out(3, rows, LANES), out(3, rows, LANES)]
        + [out(6, *mid_lines), out(*mid_lines), out(6, *low_lines), out(*low_lines)]
        + fifth_round.buffers(),
        [(1, rows, LANES), (rows // 2, LANES)],
    )
    fifth_got = swap(buffers)

    def device(*steps):
        at = [lax.axis_index(name) for name in AXES]
        inside, flat = True, 0
        for position, size, step in zip(at, sizes, steps):
            inside = inside & (position + step >= 0) & (position + step < size)
        for position, size, step in zip(at, sizes, steps):
            flat = flat * size + jnp.where(inside, position + step, position)
        return flat

    last_groups = LANES // last_width
    last = jnp.concatenate([OMEGA / coarse_three[:1], coarse_three[1:]]).reshape(7, last_height, last_width)
    last = jnp.pad(last, ((0, 2 * last_groups - 7), (0, 0), (0, 0)))
    last = last.reshape(2, last_groups, last_height, last_width).transpose(0, 2, 1, 3).reshape(2 * last_height, LANES)
    keep = low.rows // low.dup
    own_at = keep + 2 * last_height
    block = own_at + 2
    signs = (-1, 1)

    def columns(near, far, sign):
        if sign < 0:
            parts = near, roll(far, 2, 1), roll(near, 2, 1)
        else:
            parts = roll(near, 2, 1), roll(far, 4, 1), roll(near, 8, 1)
        lane = lane_of(near)
        return jnp.where(lane < 2, parts[0], jnp.where(lane < 4, parts[1], jnp.where(lane < 6, parts[2], 0.0)))

    def low_kernel(x, one, mid_couplings, two, last, *rest):
        got, (sent, ends, temp) = rest[:swaps], rest[swaps:]
        (rim,) = fifth_round.halos(1, got, ends, [0])
        value = x[...]
        total = (1.0 - OMEGA) * value
        for dim in range(3):
            total = total - mid_couplings[2 * dim] * rim.previous(value, dim)
            total = total - mid_couplings[2 * dim + 1] * rim.following(value, dim)
        residual = total * (one[0] * (1.0 / OMEGA))
        b = pair_sum_rows(pair_sum_x(residual, mid.dup), mid.depth, mid.height, temp)
        field = b * (OMEGA / two[0])
        to_next = [two[2 + 2 * dim] * field for dim in range(3)]
        to_previous = [two[1 + 2 * dim] * field for dim in range(3)]
        closed = Closed(low.height, low.dup)
        inner = (1.0 - OMEGA) * b
        for dim in range(3):
            inner = inner - closed.previous(to_next[dim], dim) - closed.following(to_previous[dim], dim)
        row, lane = lax.broadcasted_iota(jnp.int32, field.shape, 0), lane_of(field)
        layer, y = row // low.height, row % low.height
        outer = [
            jnp.where(layer == 0, -to_previous[0], 0.0),
            jnp.where(layer == low.depth - 1, -to_next[0], 0.0),
            jnp.where(y == 0, -to_previous[1], jnp.where(y == low.height - 1, -to_next[1], 0.0)),
            jnp.where(lane < low.dup, -to_previous[2], jnp.where(lane >= LANES - low.dup, -to_next[2], 0.0)),
        ]
        parts = [pair_sum_rows(pair_sum_x(v, low.dup), low.depth, low.height, temp) for v in [inner] + outer]
        parts = matmul(jnp.concatenate(parts), one_hot((LANES, LANES), lambda i, j: i == 2 * low.dup * j))
        parts = [parts[k * last_height : (k + 1) * last_height] for k in range(5)]
        upper = last[:last_height] + roll(parts[0], 7 * last_width, 1)
        lower = last[last_height:]
        for k in range(4):
            lower = lower + roll(parts[1 + k], k * last_width, 1)
        packed = jnp.zeros((keep, LANES), F32)
        phase = lane_of(packed) % low.dup
        for k in range(low.dup):
            packed = jnp.where(phase == k, field[k * keep : (k + 1) * keep], packed)
        filled = jnp.concatenate([packed, upper, lower, jnp.zeros((2, LANES), F32)])
        sent[...] = jnp.broadcast_to(filled[None], (count, block, LANES))

        def near(sign, size):
            return 0 if sign < 0 else size - 1

        def line(a, y):
            return x[a * mid.height + y : a * mid.height + y + 1, :]

        def across(a):
            return x[a * mid.height : (a + 1) * mid.height, :]

        def along(y):
            return x[pl.ds(y, mid.depth, stride=mid.height), :]

        def folded(value):
            return sum(roll(value[2 * k : 2 * k + 2], 6 * k, 1) for k in range(value.shape[0] // 2))

        for sz in signs:
            a = near(sz, mid.depth)
            for sy in signs:
                y = near(sy, mid.height)
                pair = fold(jnp.concatenate([line(a, y), line(a - sz, y)]))
                sent[device(0, sy, sz), own_at : own_at + 2, :] = jnp.concatenate([pair, line(a, y - sy)])
                for sx in signs:
                    corner = columns(line(a, y), line(a, y), sx)
                    sent[device(sx, sy, sz), own_at : own_at + 1, :] = corner
            for sx in signs:
                sent[device(sx, 0, sz), own_at : own_at + 2, :] = folded(columns(across(a), across(a - sz), sx))
        for sy in signs:
            y = near(sy, mid.height)
            for sx in signs:
                sent[device(sx, sy, 0), own_at : own_at + 2, :] = folded(columns(along(y), along(y - sy), sx))

    (sent,) = call(
        low_kernel,
        (x_mid, one, mid_couplings, two, last, *fifth_got),
        [out(count, block, LANES)],
        [(1, mid.rows, LANES), (mid.rows // 2, LANES)],
    )
    everyone = lax.all_to_all(sent, AXES, 0, 0)

    def window_kernel(x, *rest):
        gots, (x_out, *lines, layers_out, lines_out, sides_out) = [rest[k * swaps : (k + 1) * swaps] for k in range(3)], rest[3 * swaps :]
        third, fourth, fifth = gots
        x_out[...] = jnp.zeros(x_out.shape, F32)
        near, far = fifth_round.faces(1, fifth)
        mid_window.fill(x_out.at[0], x[...])
        mid_window.fill(x_out.at[1], beside_of(*near[2]))
        mid_window.fill(x_out.at[2], beside_of(*far[2]))
        for faces, step in ((near, 0), (far, 1)):
            for layer, value in zip((-1 - step, mid.depth + step), faces[0]):
                x_out[0, mid_window.layer(layer), :] = value
            for y, value in zip((-1 - step, mid.height + step), faces[1]):
                x_out[0, mid_window.row(y), :] = value
        for part, window, ours, theirs in ((2, mid_window, *lines[:2]), (3, low_window, *lines[2:])):
            line = window.line
            for k, half in enumerate(fifth_round.rows(part, 0, fifth)):
                at = slice(k * line, (k + 1) * line)
                for pair in range(3):
                    both = unfold(half[pair * line : (pair + 1) * line])
                    ours[2 * pair, at, :] = both[:line]
                    ours[2 * pair + 1, at, :] = both[line:]
                theirs[at, :] = half[3 * line :]
        channels = fourth_round.faces(0, fourth, range(1, 7)) + third_round.faces(0, third, range(1, 4)) + fifth_round.faces(0, fifth)
        for c, faces in enumerate(channels):
            layers_out[c] = jnp.concatenate(faces[0])
            lines_out[c] = jnp.concatenate(faces[1])
        sides = [beside_of(*faces[2]) for faces in channels]
        for c in range(6):
            sides_out[c] = pack_sides(sides[2 * c : 2 * c + 2], 1)

    mid_ends, low_ends = (2 * mid_window.line, LANES), (2 * low_window.line, LANES)
    x_windows, *halo_inputs = call(
        window_kernel,
        (x_mid, *third_got, *fourth_got, *fifth_got),
        [out(3, mid_window.rows, LANES), out(6, *mid_ends), out(*mid_ends), out(6, *low_ends), out(*low_ends)]
        + [out(12, 2 * height, LANES), out(12, 2 * depth, LANES), out(6, rows, LANES)],
    )

    last_rows, last_line = sizes[2] * sizes[1] * last_height, sizes[1] * last_height

    def solve_last(everyone, temp):
        channels = [[] for _ in range(2 * last_groups)]
        for first in range(0, sizes[0], last_groups):
            here = range(min(last_groups, sizes[0] - first))
            for g in here:
                for y in range(sizes[1]):
                    for z in range(sizes[2]):
                        sender = ((first + g) * sizes[1] + y) * sizes[2] + z
                        for half in range(2):
                            at = half * last_rows + z * last_line + y * last_height
                            start = keep + half * last_height
                            temp[g, at : at + last_height, :] = everyone[sender, start : start + last_height, :]
            parts = [temp[g] for g in here]
            group = lane_of(parts[0]) // last_width
            for q in range(last_groups):
                value = jnp.zeros_like(parts[0])
                for g in here:
                    value = jnp.where(group == g, roll(parts[g], last_width * (g - q), 1), value)
                channels[q].append(value[:last_rows])
                channels[last_groups + q].append(value[last_rows:])
        parts = [jnp.concatenate(tiles, axis=1) for tiles in channels[: last_groups + 4]]
        stencil, (inner, back, on, beside_y, beside_x) = parts[:7], parts[7:]
        y, x = row_y(inner, last_line), lane_of(inner)
        none = jnp.zeros((last_line, inner.shape[1]), F32)
        b = inner + jnp.concatenate([back[last_line:], none]) + jnp.concatenate([none, on[:-last_line]])
        b = b + jnp.where((y % last_height == 0) & (y > 0), roll(beside_y, 1, 0), 0.0)
        b = b + jnp.where((y % last_height == last_height - 1) & (y < last_line - 1), roll(beside_y, -1, 0), 0.0)
        b = b + jnp.where((x % last_width == 0) & (x > 0), roll(beside_x, 1, 1), 0.0)
        b = b + jnp.where((x % last_width == last_width - 1) & (x < inner.shape[1] - 1), roll(beside_x, -1, 1), 0.0)
        closed = Closed(last_line, 1)
        field = start = b * stencil[0]
        for sweep in range(COARSE_SWEEPS - 1):
            field = start + (1.0 - OMEGA) * field - off_apply(stencil, field, closed) * stencil[0]
        return field

    def spread_last(field, temp):
        gx, gy, gz = (lax.axis_index(name) for name in AXES)
        half, reach = low_window.line // 2, low_window.rim // 2
        layers = low.depth // 2 + 2
        dup = 2 * low.dup

        def picked(i, j):
            return j == (gz * (low.depth // 2) + i // half - 1) * last_line + gy * last_height + i % half - reach

        def taken(i, j):
            own = (j < LANES) & (i == gx * last_width + j // dup)
            before = (j >= LANES) & (j < LANES + low.dup) & (i == gx * last_width - 1)
            after = (j >= 2 * LANES - low.dup) & (i == (gx + 1) * last_width)
            return own | before | after

        chosen = matmul(one_hot((layers * half, last_rows), picked), field)
        both = matmul(chosen, one_hot((field.shape[1], 2 * LANES), taken))
        return [spread_rows(both[:, k * LANES : (k + 1) * LANES], layers, half, temp) for k in range(2)]

    def low_windows(everyone, temp, result):
        around = [(sy, sz) for sz in (-1, 0, 1) for sy in (-1, 0, 1)]
        per = -(-len(around) * keep // 8) * 8
        for k, sx in enumerate((0, -1, 1)):
            for i, (sy, sz) in enumerate(around):
                temp[k * per + keep * i : k * per + keep * (i + 1), :] = everyone[device(sx, sy, sz), 0:keep, :]
        packed = temp[: 3 * per, :]
        lane = lane_of(packed)
        turned = {by: roll(packed, by, 1) for by in range(1 - low.dup, low.dup)}
        for k in range(low.dup):
            value = turned[-k]
            for m in range(1, low.dup):
                value = jnp.where(lane % low.dup == m, turned[m - k], value)
            own, before, after = (value[i * per : (i + 1) * per] for i in range(3))
            forms = [own]
            for cells in (1, 2):
                forms.append(beside_of(roll(before, low.dup * cells, 1), roll(after, -low.dup * cells, 1)))
            for i, (sy, sz) in enumerate(around):
                for j in range(keep):
                    a, y = divmod(k * keep + j, low.height)
                    a, y = a + sz * low.depth, y + sy * low.height
                    if -2 <= a < low.depth + 2 and -low_window.rim <= y < low.height + low_window.rim:
                        at = low_window.at(a, y)
                        for form, source in enumerate(forms):
                            result[form, at : at + 1, :] = source[keep * i + j : keep * i + j + 1]
        return [result[form] for form in range(3)]

    def mid_edges(everyone, x):
        def lines(*steps):
            return everyone[device(*steps), own_at : own_at + 2, :]

        def unfolded(value, n):
            return jnp.concatenate([roll(value, -6 * k, 1) for k in range(n // 2)])

        def sides(values, k):
            return beside_of(roll(values[0], -2 * k, 1), roll(values[1], -2 * k - 2, 1))

        for sz in signs:
            a = -1 if sz < 0 else mid.depth
            for sy in signs:
                y = -1 if sy < 0 else mid.height
                got = lines(0, sy, sz)
                pair = unfold(got[:1])
                for layer, at, value in ((a, y, pair[:1]), (a + sz, y, pair[1:]), (a, y + sy, got[1:])):
                    row = mid_window.at(layer, at)
                    x[0, row : row + 1, :] = value
                row = mid_window.at(a, y)
                x[1, row : row + 1, :] = sides([lines(sx, sy, sz)[:1] for sx in signs], 0)
            got = [unfolded(lines(sx, 0, sz), mid.height) for sx in signs]
            x[1, mid_window.layer(a), :] = sides(got, 0)
            x[1, mid_window.layer(a + sz), :] = sides(got, 1)
            x[2, mid_window.layer(a), :] = sides(got, 2)
        for sy in signs:
            y = -1 if sy < 0 else mid.height
            got = [unfolded(lines(sx, sy, 0), mid.depth) for sx in signs]
            x[1, mid_window.row(y), :] = sides(got, 0)
            x[1, mid_window.row(y + sy), :] = sides(got, 1)
            x[2, mid_window.row(y), :] = sides(got, 2)

    def full(window, lines, ends, side_lines, side_ends):
        line, none = window.line, jnp.zeros((window.line, LANES), F32)
        packed = jnp.concatenate([none, side_ends[:line, :], side_lines[...], side_ends[line:, :], none])
        return (
            lambda c: jnp.concatenate([none, ends[c, :line, :], lines[c], ends[c, line:, :], none]),
            lambda c: unpack_side(packed, c, window.grid.dup),
        )

    def gradient_factors(mobility, pressure, trans, trans_before, *rest):
        got, (inner, layer_out, line_out, side_out, ends) = rest[:swaps], rest[swaps:]
        faces = second_round.faces(0, got, range(3, 7))
        rims = [Rim(fine, f, ends, c) for c, f in enumerate(faces)]
        lines = pl.ds(0, depth, stride=height)
        drops = []
        for dim in range(3):
            drops.append(0.25 * trans[dim] * (pressure[0] - rims[3].following(pressure[0], dim)))
        side_drop = 0.25 * trans_before[2] * (faces[3][2][0] - pressure[0])
        sides = []
        for c in range(3):
            value = mobility[c]
            for dim in range(3):
                inner[3 * dim + c] = drops[dim] * (value + rims[c].following(value, dim))
            drop = 0.25 * trans_before[0, :height, :] * (faces[3][0][0] - pressure[0, :height, :])
            layer_out[c] = drop * (faces[c][0][0] + mobility[c, :height, :])
            drop = 0.25 * trans_before[1, lines, :] * (faces[3][1][0] - pressure[0, lines, :])
            line_out[c] = drop * (faces[c][1][0] + mobility[c, lines, :])
            sides.append(side_drop * (faces[c][2][0] + value))
        side_out[...] = pack_sides(sides, 1)

    gradient_inputs = call(
        gradient_factors,
        (mobility, pressure, trans, trans_before, *second_got),
        [out(9, rows, LANES), out(3, height, LANES), out(3, depth, LANES), out(rows, LANES)],
        [(4, rows, LANES)],
    )

    def final_kernel(
        everyone,
        x_windows,
        mid_around,
        mid_beside,
        low_around,
        low_beside,
        mid_ends,
        mid_side_ends,
        low_ends,
        low_side_ends,
        layer_halos,
        line_halos,
        side_halos,
        adj_known,
        adj_factor,
        couplings,
        terms,
        layer_terms,
        line_terms,
        side_terms,
        adj_out,
        grad_out,
        *scratch,
    ):
        last_temp, low_x, low_temp, x, temp, ends, around, beside, value_ref, adj, grad, sems = scratch
        added = spread_last(solve_last(everyone, last_temp), low_temp)
        low_values = low_windows(everyone, low_temp, low_x)
        pair = full(low_window, low_around, low_ends, low_beside, low_side_ends)
        results = smooth(low_values, added, pair, low_window.line, low.dup)
        inner = slice(low_window.line, (low.depth + 3) * low_window.line)
        added = [spread_rows(v[inner], low.depth + 2, low_window.line, temp) for v in results]
        x[...] = x_windows[...]
        mid_edges(everyone, x)
        pair = full(mid_window, mid_around, mid_ends, mid_beside, mid_side_ends)
        around[...], beside[...] = smooth([x[k] for k in range(3)], added, pair, mid_window.line, mid.dup)

        def own(ref):
            lines = [ref[mid_window.layer(a), :] for a in range(mid.depth)]
            return spread_rows(jnp.concatenate(lines), mid.depth, mid.height, temp)

        def layer(ref, a):
            return spread_lines(ref[mid_window.layer(a), :], temp)

        def lines(ref, y):
            return spread_lines(ref[mid_window.row(y), :], temp)

        def one_row(a, y):
            at = mid_window.at(a, y)
            return around[at : at + 1, :]

        value, side = own(around), own(beside)
        value_ref[...] = value
        layers = [(a, layer(around, a), layer(beside, a)) for a in (-1, mid.depth)]
        rows_y = [(y, lines(around, y), lines(beside, y)) for y in (-1, mid.height)]
        rim = Rim(fine, [[v[1] for v in layers], [v[1] for v in rows_y], (side, side)], ends, 0)

        def gain(value, shifts, coupling):
            total = (1.0 - OMEGA) * value
            for k in range(6):
                total = total - coupling(k) * shifts[k]
            return total

        shifts = [shift(value, dim) for dim in range(3) for shift in (rim.previous, rim.following)]
        own_gain = gain(value, shifts, lambda k: couplings[k])
        for c in range(3):
            adj[c] = adj_known[c] + adj_factor[c] * own_gain
        copies = [pltpu.make_async_copy(adj, adj_out, sems.at[3])]
        copies[0].start()

        def along_x(value, side):
            lane = lane_of(value)
            return [jnp.where(lane < 1, side, roll(value, 1, 1)), jnp.where(lane >= LANES - 1, side, roll(value, -1, 1))]

        def ended(value, low, high):
            row = lax.broadcasted_iota(jnp.int32, value.shape, 0)
            n = value.shape[0]
            return [jnp.where(row == 0, low, roll(value, 1, 0)), jnp.where(row == n - 1, high, roll(value, -1, 0))]

        layer_gains, line_gains = [], []
        for k, (a, here, there) in enumerate(layers):
            shifts = [here, value[:height]] if k == 0 else [value[rows - height :], here]
            shifts += ended(here, one_row(a, -1), one_row(a, mid.height)) + along_x(here, there)
            layer_gains.append(gain(here, shifts, lambda c: layer_halos[c, k * height : (k + 1) * height, :]))
        for k, (y, here, there) in enumerate(rows_y):
            inside = value_ref[pl.ds(0 if k == 0 else height - 1, depth, stride=height), :]
            shifts = ended(here, one_row(-1, y), one_row(mid.depth, y))
            shifts += ([here, inside] if k == 0 else [inside, here]) + along_x(here, there)
            line_gains.append(gain(here, shifts, lambda c: line_halos[c, k * depth : (k + 1) * depth, :]))
        lane = lane_of(side)
        side_rim = Rim(fine, [[v[2] for v in layers], [v[2] for v in rows_y], (side, side)], ends, 1)
        shifts = [shift(side, dim) for dim in range(2) for shift in (side_rim.previous, side_rim.following)]
        shifts += [jnp.where(lane < LANES // 2, side, value), jnp.where(lane < LANES // 2, value, side)]

        def side_halo(c):
            return unpack_side(side_halos[c // 2], 1, 1) if c % 2 else side_halos[c // 2]

        side_gain = gain(side, shifts, side_halo)
        adj_rims = []
        for c in range(3):
            known, factor = 9 + c, 6 + c
            faces = [
                [
                    layer_halos[known, k * height : (k + 1) * height, :]
                    + layer_halos[factor, k * height : (k + 1) * height, :] * layer_gains[k]
                    for k in range(2)
                ],
                [
                    line_halos[known, k * depth : (k + 1) * depth, :] + line_halos[factor, k * depth : (k + 1) * depth, :] * line_gains[k]
                    for k in range(2)
                ],
                (side_halo(known) + side_halo(factor) * side_gain,) * 2,
            ]
            adj_rims.append(Rim(fine, faces, ends, 2 + c))
        values = [adj[c] for c in range(3)]
        lines = pl.ds(0, depth, stride=height)
        parts = []
        for c in range(3):
            layer, line, side = (adj_rims[c].faces[dim][0] for dim in range(3))
            parts.append(
                (
                    layer_terms[c] * (layer - values[c][:height]),
                    line_terms[c] * (line - adj[c, lines, :]),
                    unpack_side(side_terms[...], c, 1) * (side - values[c]),
                )
            )
        below = Rim(fine, [(sum(p[dim] for p in parts),) * 2 for dim in range(3)], ends, 5)
        for dim in range(3):
            here = 0.0
            for c in range(3):
                here = here + terms[3 * dim + c] * (values[c] - adj_rims[c].following(values[c], dim))
            grad[dim] = here + below.previous(here, dim)
            copies.append(pltpu.make_async_copy(grad.at[dim], grad_out.at[dim], sems.at[dim]))
            copies[-1].start()
        for copy in copies:
            copy.wait()

    adjoint, gradient = call(
        final_kernel,
        (everyone, x_windows, mid_around, mid_beside, low_around, low_beside, *halo_inputs)
        + (adj_known, adj_factor, fine_couplings, *gradient_inputs),
        [out(3, rows, LANES)] * 2,
        [
            (min(sizes[0], last_groups), 2 * last_rows, LANES),
            (3, low_window.rows, LANES),
            (max(low_window.rows, 96), LANES),
            (3, mid_window.rows, LANES),
            (mid_window.rows, LANES),
            (6, rows, LANES),
            (mid_window.rows, LANES),
            (mid_window.rows, LANES),
            (rows, LANES),
            (3, rows, LANES),
            (3, rows, LANES),
            pltpu.SemaphoreType.DMA((4,)),
        ],
        far_outputs=2,
    )
    shape = (3, depth, height, width)
    return adjoint.reshape(shape), gradient.reshape(shape)


def solution(mesh):
    cells = P("layer", "gy", "gx")
    fields = P(None, "layer", "gy", "gx")
    return jax.shard_map(
        local,
        mesh=mesh,
        in_specs=(
            fields,
            cells,
            fields,
            fields,
            fields,
            fields,
            fields,
            fields,
            fields,
            fields,
            cells,
            fields,
        ),
        out_specs=(fields, fields),
        check_vma=False,
    )
```

```python
import itertools

import jax
import jax.numpy as jnp
from jax import lax
from jax.experimental import pallas as pl
from jax.experimental.pallas import tpu as pltpu
from jax.sharding import PartitionSpec as P

SWEEPS = 3
LEVELS = 3
COARSE_SWEEPS = 4
OMEGA = 0.8
LANES = 128
AXES = ("gx", "gy", "layer")
BY_DIM = ("layer", "gy", "gx")
ORDER = ((0, 1), (0, 0), (1, 1), (1, 0), (2, 1), (2, 0))
F32 = jnp.float32


def pair_route(axis, phase):
    sizes = [lax.axis_size(name) for name in AXES]
    k = AXES.index(axis)
    n = sizes[k]
    route = []
    for index in itertools.product(*[range(size) for size in sizes]):
        target = list(index)
        if phase == 0:
            target[k] = index[k] ^ 1
        elif 0 < index[k] < n - 1 or k == 0:
            target[k] = (((index[k] + 1) % n ^ 1) - 1) % n
        else:
            target[0] = index[0] ^ 1
        flat = [(i[0] * sizes[1] + i[1]) * sizes[2] + i[2] for i in (index, target)]
        route.append(tuple(flat))
    return route


def phases(dim):
    return min(lax.axis_size(BY_DIM[dim]), 3) - 1


def sends(dims=(0, 1, 2)):
    return [(dim, phase) for dim, phase in ORDER if dim in dims and phase < phases(dim)]


def swap(buffers, dims=(0, 1, 2)):
    return [lax.ppermute(b, AXES, pair_route(BY_DIM[dim], phase)) for b, (dim, phase) in zip(buffers, sends(dims))]


class Grid:
    def __init__(self, depth, height, dup):
        self.depth, self.height, self.dup = depth, height, dup
        self.rows = depth * height
        self.width = LANES // dup
        self.groups = self.rows // 8
        self.stride = LANES // self.groups

    def lines(self, dim):
        return (self.height, self.depth)[dim]


class Message:
    def __init__(self, *parts, dims=(0, 1, 2)):
        self.parts, self.dims = parts, dims

    def size(self, part, dim):
        part = self.parts[part]
        if isinstance(part, dict):
            return part.get(dim, 0)
        if dim not in part[2:] and len(part) > 2:
            return 0
        return 8 if dim == 2 else part[1] * part[0].lines(dim)

    def start(self, part, dim):
        return sum(self.size(i, dim) for i in range(part))

    def buffers(self):
        return [jax.ShapeDtypeStruct((self.start(len(self.parts), dim), LANES), F32) for dim, phase in sends(self.dims)]

    def put(self, dim, rows, first, last, out):
        if phases(dim) == 0:
            return
        out = dict(zip(sends(self.dims), out))
        even = lax.axis_index(BY_DIM[dim]) % 2 == 0
        out[dim, 0][rows] = jnp.where(even, last, first)
        if phases(dim) == 2:
            out[dim, 1][rows] = jnp.where(even, first, last)

    def put_rows(self, part, dim, first, last, out):
        start = self.start(part, dim)
        self.put(dim, slice(start, start + self.size(part, dim)), first, last, out)

    def emit(self, part, channels, out):
        grid = self.parts[part][0]
        lane = lax.broadcasted_iota(jnp.int32, (8, LANES), 1)
        for dim in range(3):
            if self.size(part, dim) == 0:
                continue
            start = self.start(part, dim)
            if dim == 2:
                firsts, lasts = jnp.zeros((8, LANES), F32), jnp.zeros((8, LANES), F32)
                for c, (first, last) in enumerate(channels[dim]):
                    for k in range(grid.groups):
                        at = grid.stride * k + grid.dup * c
                        here = (lane >= at) & (lane < at + grid.dup)
                        rows = slice(8 * k, 8 * k + 8)
                        firsts = jnp.where(here, roll(first(rows), at, 1), firsts)
                        lasts = jnp.where(here, roll(last(rows), at + grid.dup, 1), lasts)
                self.put(dim, slice(start, start + 8), firsts, lasts, out)
                continue
            if dim == 0:
                low, high = slice(0, grid.height), slice(grid.rows - grid.height, grid.rows)
            else:
                low, high = (pl.ds(s, grid.depth, stride=grid.height) for s in (0, grid.height - 1))
            n = grid.lines(dim)
            for c, (first, last) in enumerate(channels[dim]):
                self.put(dim, slice(start + c * n, start + (c + 1) * n), first(low), last(high), out)

    def both(self, dim, rows, got):
        if phases(dim) == 0:
            return (jnp.zeros((rows.stop - rows.start, LANES), F32),) * 2
        got = dict(zip(sends(self.dims), got))
        me, n = lax.axis_index(BY_DIM[dim]), lax.axis_size(BY_DIM[dim])
        even = me % 2 == 0
        one = got[dim, 0][rows]
        if phases(dim) == 1:
            return jnp.where(even, 0.0, one), jnp.where(even, one, 0.0)
        two = got[dim, 1][rows]
        before, after = jnp.where(even, two, one), jnp.where(even, one, two)
        return jnp.where(me > 0, before, 0.0), jnp.where(me < n - 1, after, 0.0)

    def rows(self, part, dim, got):
        start = self.start(part, dim)
        return self.both(dim, slice(start, start + self.size(part, dim)), got)

    def faces(self, part, got, channels=None):
        grid, count = self.parts[part][:2]
        channels = range(count) if channels is None else channels
        result = [[None] * 3 for _ in channels]
        for dim in range(3):
            if self.size(part, dim) == 0:
                continue
            start = self.start(part, dim)
            if dim == 2:
                sides = self.both(dim, slice(start, start + 8), got)
                for i, c in enumerate(channels):
                    parts = []
                    for side, lane in zip(sides, (0, LANES - grid.dup)):
                        pieces = [roll(side, lane - grid.stride * k - grid.dup * c, 1) for k in range(grid.groups)]
                        parts.append(jnp.concatenate(pieces))
                    result[i][dim] = tuple(parts)
            else:
                size = grid.lines(dim)
                for i, c in enumerate(channels):
                    result[i][dim] = self.both(dim, slice(start + c * size, start + (c + 1) * size), got)
        return result

    def halos(self, part, got, scratch, channels=None):
        return [Rim(self.parts[part][0], r, scratch, c) for c, r in enumerate(self.faces(part, got, channels))]


class Window:
    def __init__(self, grid, rim):
        self.grid, self.rim = grid, rim
        self.line = grid.height + 2 * rim
        self.rows = (grid.depth + 4) * self.line

    def at(self, layer, y):
        return (layer + 2) * self.line + self.rim + y

    def layer(self, layer):
        return slice(self.at(layer, 0), self.at(layer, self.grid.height))

    def row(self, y):
        return pl.ds(self.at(0, y), self.grid.depth, stride=self.line)

    def fill(self, ref, own):
        height = self.grid.height
        for a in range(self.grid.depth):
            ref[self.layer(a), :] = own[a * height : (a + 1) * height]


class Rim:
    def __init__(self, grid, faces, scratch, c):
        self.grid, self.faces = grid, faces
        ends = scratch.at[c]
        ends[pl.ds(0, grid.depth, stride=grid.height), :] = faces[1][0]
        ends[pl.ds(grid.height - 1, grid.depth, stride=grid.height), :] = faces[1][1]
        self.y_ends = ends[...]

    def previous(self, value, dim):
        g = self.grid
        if dim == 0:
            return jnp.concatenate([self.faces[0][0], value[: g.rows - g.height]])
        if dim == 1:
            return jnp.where(row_y(value, g.height) == 0, self.y_ends, roll(value, 1, 0))
        return jnp.where(lane_of(value) < g.dup, self.faces[2][0], roll(value, g.dup, 1))

    def following(self, value, dim):
        g = self.grid
        if dim == 0:
            return jnp.concatenate([value[g.height :], self.faces[0][1]])
        if dim == 1:
            return jnp.where(row_y(value, g.height) == g.height - 1, self.y_ends, roll(value, -1, 0))
        return jnp.where(lane_of(value) >= value.shape[1] - g.dup, self.faces[2][1], roll(value, -g.dup, 1))


class Closed:
    def __init__(self, height, dup):
        self.height, self.dup = height, dup

    def previous(self, value, dim):
        if dim == 0:
            return jnp.concatenate([jnp.zeros_like(value[: self.height]), value[: -self.height]])
        if dim == 1:
            return jnp.where(row_y(value, self.height) == 0, 0.0, roll(value, 1, 0))
        return jnp.where(lane_of(value) < self.dup, 0.0, roll(value, self.dup, 1))

    def following(self, value, dim):
        if dim == 0:
            return jnp.concatenate([value[self.height :], jnp.zeros_like(value[: self.height])])
        if dim == 1:
            return jnp.where(row_y(value, self.height) == self.height - 1, 0.0, roll(value, -1, 0))
        return jnp.where(lane_of(value) >= value.shape[1] - self.dup, 0.0, roll(value, -self.dup, 1))


def roll(value, shift, axis):
    shift %= value.shape[axis]
    return pltpu.roll(value, shift, axis) if shift else value


def row_y(value, height):
    return lax.broadcasted_iota(jnp.int32, value.shape, 0) % height


def lane_of(value):
    return lax.broadcasted_iota(jnp.int32, value.shape, 1)


def loader(ref, c):
    return lambda rows: ref[c, rows, :]


def product(coefs, k, ref):
    return lambda rows: coefs[k, rows, :] * ref[rows, :]


def off_apply(stencil, field, rim):
    total = 0.0
    for dim in range(3):
        total = total + rim.previous(stencil[2 + 2 * dim] * field, dim)
        total = total + rim.following(stencil[1 + 2 * dim] * field, dim)
    return total


def block_row(blocks, c, values):
    return blocks[c] * values[0] + blocks[3 + c] * values[1] + blocks[6 + c] * values[2]


def system_row(c, values, rim, blocks, trans, trans_before):
    total = block_row(blocks, c, values)
    v = values[c]
    for dim in range(3):
        total = total + trans[dim] * (v - rim.following(v, dim))
        total = total + trans_before[dim] * (v - rim.previous(v, dim))
    return total


def pair_sum_x(value, dup):
    odd = (lane_of(value) // dup) % 2 == 1
    return value + jnp.where(odd, roll(value, dup, 1), roll(value, -dup, 1))


def pair_sum_rows(value, depth, height, scratch):
    half = depth // 2
    parts = [value[2 * a * height : (2 * a + 1) * height] + value[(2 * a + 1) * height : (2 * a + 2) * height] for a in range(half)]
    whole = jnp.concatenate(parts)
    count = half * height // 2
    sums = []
    for at in range(0, whole.shape[1], LANES):
        scratch[: half * height, :] = whole[:, at : at + LANES]
        sums.append(scratch[pl.ds(0, count, stride=2), :] + scratch[pl.ds(1, count, stride=2), :])
    return jnp.concatenate(sums, axis=1)


def spread_rows(value, depth, height, scratch):
    count = depth * height
    tiles = []
    for at in range(0, value.shape[1], LANES):
        scratch[pl.ds(0, count, stride=2), :] = value[:, at : at + LANES]
        scratch[pl.ds(1, count, stride=2), :] = value[:, at : at + LANES]
        wide = scratch[: 2 * count, :]
        tiles.append(jnp.concatenate([wide[2 * height * (a // 2) : 2 * height * (a // 2 + 1)] for a in range(2 * depth)]))
    return jnp.concatenate(tiles, axis=1)


def spread_lines(value, scratch):
    count = value.shape[0]
    scratch[pl.ds(0, count, stride=2), :] = value
    scratch[pl.ds(1, count, stride=2), :] = value
    return scratch[: 2 * count, :]


def fold(value):
    half = value.shape[0] // 2
    return jnp.where(lane_of(value[:half]) % 2 == 0, value[:half], value[half:])


def unfold(value):
    even = lane_of(value) % 2 == 0
    return jnp.concatenate([jnp.where(even, value, roll(value, 1, 1)), jnp.where(even, roll(value, -1, 1), value)])


def beside_of(before, after):
    return jnp.where(lane_of(before) < LANES // 2, before, after)


def pack_sides(values, dup):
    total = jnp.zeros_like(values[0])
    lane = lane_of(total)
    for c, value in enumerate(values):
        total = jnp.where((lane >= dup * c) & (lane < dup * (c + 1)), roll(value, dup * c, 1), total)
        high = LANES - dup * c
        total = jnp.where((lane >= high - dup) & (lane < high), roll(value, -dup * c, 1), total)
    return total


def unpack_side(value, c, dup):
    return beside_of(roll(value, -dup * c, 1), roll(value, dup * c, 1))


def moved(rows, by):
    if isinstance(rows, slice):
        return slice(rows.start + by, rows.stop + by)
    return pl.ds(rows.start + by, rows.size, stride=rows.stride)


def shifts_of(value, inner, outer, line, dup, beside):
    none = jnp.zeros((line, LANES), F32)
    lane = lane_of(value)
    if beside:
        low, high = jnp.where(lane < LANES // 2, outer, inner), jnp.where(lane < LANES // 2, inner, outer)
    else:
        low, high = jnp.where(lane < dup, outer, roll(value, dup, 1)), jnp.where(lane >= LANES - dup, outer, roll(value, -dup, 1))
    return [
        jnp.concatenate([none, value[:-line]]),
        jnp.concatenate([value[line:], none]),
        roll(value, 1, 0),
        roll(value, -1, 0),
        low,
        high,
    ]


def smooth(x, added, couplings, line, dup):
    around, beside, second = x[0] + added[0], x[1] + added[1], x[2] + added[1]
    results = []
    for k, (value, shifts) in enumerate(
        (
            (around, shifts_of(around, None, beside, line, dup, False)),
            (beside, shifts_of(beside, around, second, line, dup, True)),
        )
    ):
        total = x[k] + (1.0 - OMEGA) * value
        for c in range(6):
            total = total - couplings[k](c) * shifts[c]
        results.append(total)
    return results


def one_hot(shape, hit):
    return jnp.where(hit(lax.broadcasted_iota(jnp.int32, shape, 0), lax.broadcasted_iota(jnp.int32, shape, 1)), 1.0, 0.0).astype(F32)


def matmul(values, ones):
    n = values.shape[0]
    extra = -n % 16
    if extra:
        values = jnp.concatenate([values, jnp.zeros((extra, values.shape[1]), F32)])
    parts = []
    for _ in range(3):
        parts.append(values.astype(jnp.bfloat16))
        values = values - parts[-1].astype(F32)
    product = jnp.dot(jnp.concatenate(parts), ones.astype(jnp.bfloat16), preferred_element_type=F32)
    step = n + extra
    return (product[2 * step : 2 * step + n] + product[step : step + n]) + product[:n]


def call(kernel, inputs, outputs, scratch=(), far_inputs=0, far_outputs=0):
    inputs = list(inputs)
    for i in range(far_inputs):
        inputs[i] = pltpu.with_memory_space_constraint(inputs[i], pltpu.HBM)

    def specs(count, far):
        return [pl.BlockSpec(memory_space=pltpu.HBM if i < far else pltpu.VMEM) for i in range(count)]

    return pl.pallas_call(
        kernel,
        out_shape=list(outputs),
        in_specs=specs(len(inputs), far_inputs),
        out_specs=specs(len(outputs), far_outputs),
        scratch_shapes=[pltpu.VMEM(shape, F32) if isinstance(shape, tuple) else shape for shape in scratch],
        compiler_params=pltpu.CompilerParams(vmem_limit_bytes=24 * 2**20),
    )(*inputs)


def local(
    source,
    active_cells,
    diag_blocks,
    frozen_inverses,
    transmissibility,
    pressure_weights,
    stencil_fine,
    coarse_one,
    coarse_two,
    coarse_three,
    pressure_state,
    mobilities,
):
    depth, height, width = active_cells.shape
    low_depth, low_height, low_width = coarse_two.shape[1:]
    last_height, last_width = coarse_three.shape[2:]
    fine = Grid(depth, height, 1)
    mid = Grid(depth // 2, height // 2, 2)
    low = Grid(low_depth, low_height, 4)
    mid_window, low_window = Window(mid, 4), Window(low, 2)
    sizes = [lax.axis_size(name) for name in AXES]
    count = sizes[0] * sizes[1] * sizes[2]
    swaps = len(sends())
    rows = fine.rows
    first_round = Message((fine, 4), (mid, 1), (low, 1))
    second_round = Message((fine, 4))
    third_round = Message((fine, 8), (mid, 6, 2), (low, 6, 2))
    fourth_round = Message((fine, 1), {1: 7 * mid.depth}, {1: 7 * low.depth}, (fine, 6, 1, 2))
    fifth_round = Message((fine, 3, 1, 2), (mid, 2), {2: 3 * depth})
    late_round = Message((fine, 9, 0), {0: 4 * mid_window.line}, {0: 4 * low_window.line}, dims=(0,))
    late = len(sends((0,)))

    def flat(array):
        return array.reshape(array.shape[:-3] + (rows, width))

    def out(*shape):
        return jax.ShapeDtypeStruct(shape, F32)

    source, active, diag, frozen, trans, weights, stencil, pressure, mobility = (
        flat(a)
        for a in (
            source,
            active_cells,
            diag_blocks,
            frozen_inverses,
            transmissibility,
            pressure_weights,
            stencil_fine,
            pressure_state,
            mobilities,
        )
    )
    pressure = pressure[None]

    def coupling_faces(coefs):
        return [[(loader(coefs, 1 + 2 * dim), loader(coefs, 2 + 2 * dim))] for dim in range(3)]

    def widen(values, dup):
        wide = matmul(values, one_hot((values.shape[1], LANES), lambda i, j: i == j // dup))
        return wide.reshape(7, wide.shape[0] // 7, LANES)

    def start_kernel(source, active, frozen, trans, one, two, rhs_out, it_out, frozen_out, trans_out, one_out, two_out, *rest):
        buffers, (source_in, active_in, one_in, two_in, two_flat, sems) = rest[:-6], rest[-6:]
        order = [k for c in range(3) for k in (c, 3 + c, 6 + c)]
        pairs = [(active, active_in), (source, source_in)] + [(frozen.at[k], frozen_out.at[k]) for k in order]
        pairs += [(trans, trans_out), (one, one_in), (two, two_in)]
        copies = [pltpu.make_async_copy(a, b, sems.at[i]) for i, (a, b) in enumerate(pairs)]
        for copy in copies[-2:] + copies[:-2]:
            copy.start()
        copies[-2].wait()
        copies[-1].wait()
        one_out[...] = widen(one_in[...].reshape(7 * mid.rows, mid.width), mid.dup)
        for c in range(7):
            for a in range(low.depth):
                at = c * low.rows + a * low.height
                two_flat[at : at + low.height, :] = two_in[c, a]
        two_out[...] = widen(two_flat[...], low.dup)
        first_round.emit(1, coupling_faces(one_out), buffers)
        first_round.emit(2, coupling_faces(two_out), buffers)
        copies[0].wait()
        mask = active_in[...].astype(F32)
        copies[1].wait()
        rhs = [source_in[c] * mask for c in range(3)]
        for c in range(3):
            rhs_out[c] = rhs[c]
        for c in range(3):
            for copy in copies[2 + 3 * c : 5 + 3 * c]:
                copy.wait()
            it_out[c] = block_row(frozen_out, c, rhs)
        copies[-3].wait()
        its = [(loader(it_out, c),) * 2 for c in range(3)]
        first_round.emit(0, [its + [(loader(trans_out, dim),) * 2] for dim in range(3)], buffers)

    rhs, iterate, frozen, trans, one, two, *buffers = call(
        start_kernel,
        (source, active, frozen, trans, coarse_one.reshape(7, mid.rows, mid.width), coarse_two),
        [out(3, rows, LANES)] * 2
        + [out(9, rows, LANES), out(3, rows, LANES), out(7, mid.rows, LANES), out(7, low.rows, LANES)]
        + first_round.buffers(),
        [
            (3, rows, LANES),
            pltpu.VMEM((rows, LANES), jnp.int32),
            (7, mid.rows, mid.width),
            (7, low.depth, low.height, low.width),
            (7 * low.rows, low.width),
            pltpu.SemaphoreType.DMA((14,)),
        ],
        far_inputs=6,
    )
    got = swap(buffers)

    def couplings(coefs, rim, result):
        scale = OMEGA / coefs[0]
        for dim in range(3):
            result[2 * dim] = scale * rim.previous(coefs[2 + 2 * dim], dim)
            result[2 * dim + 1] = scale * rim.following(coefs[1 + 2 * dim], dim)

    def coarse_couplings(mobility, one, two, *rest):
        got, outs, mobility_out, scratch = rest[:swaps], rest[swaps : swaps + 2], rest[swaps + 2], rest[swaps + 3 :]
        fetch = pltpu.make_async_copy(mobility, mobility_out, scratch[2])
        fetch.start()
        for part, coefs, result, ends in ((1, one, outs[0], scratch[0]), (2, two, outs[1], scratch[1])):
            couplings(coefs, first_round.halos(part, got, ends)[0], result)
        fetch.wait()

    mid_couplings, low_couplings, mobility_near = call(
        coarse_couplings,
        (mobility, one, two, *got),
        [out(6, mid.rows, LANES), out(6, low.rows, LANES), out(3, rows, LANES)],
        [(1, mid.rows, LANES), (1, low.rows, LANES), pltpu.SemaphoreType.DMA],
        far_inputs=1,
    )

    def sweep_one(rhs, it, frozen, diag, trans, stencil, *rest):
        got, (it_out, before_out), buffers, ends = rest[:swaps], rest[swaps : swaps + 2], rest[swaps + 2 : -1], rest[-1]
        rims = first_round.halos(0, got, ends)
        trans_before = [rims[3].previous(trans[dim], dim) for dim in range(3)]
        values = [it[c] for c in range(3)]
        rest = [rhs[c] - system_row(c, values, rims[c], diag, trans, trans_before) for c in range(3)]
        for c in range(3):
            before_out[c] = trans_before[c]
            it_out[c] = values[c] + block_row(frozen, c, rest)
        channels = [(loader(it_out, c),) * 2 for c in range(3)]
        second_round.emit(0, [channels + faces for faces in coupling_faces(stencil)], buffers)

    iterate, trans_before, *buffers = call(
        sweep_one,
        (rhs, iterate, frozen, diag, trans, stencil, *got),
        [out(3, rows, LANES)] * 2 + second_round.buffers(),
        [(4, rows, LANES)],
    )
    second_got = swap(buffers)

    def same(ref, channels):
        return [(loader(ref, c),) * 2 for c in channels]

    def sweep_two(
        rhs, it, frozen, diag, trans, trans_before, active, weights, mobility, pressure, mid_couplings, low_couplings, *rest
    ):
        got, it_out, buffers, ends = rest[:swaps], rest[swaps], rest[swaps + 1 : -1], rest[-1]
        rims = second_round.halos(0, got, ends, range(3))
        values = [it[c] for c in range(3)]
        rest = [rhs[c] - system_row(c, values, rims[c], diag, trans, trans_before) for c in range(3)]
        for c in range(3):
            it_out[c] = values[c] + block_row(frozen, c, rest)
        factors = [(lambda at, c=c: active[at, :].astype(F32) * weights[c, at, :],) * 2 for c in range(3)]
        states = same(mobility, range(3)) + same(pressure, range(1))
        third_round.emit(0, [same(it_out, range(1)) + factors + states] * 3, buffers)
        third_round.emit(1, [same(mid_couplings, range(6))] * 3, buffers)
        third_round.emit(2, [same(low_couplings, range(6))] * 3, buffers)

    iterate, *buffers = call(
        sweep_two,
        (rhs, iterate, frozen, diag, trans, trans_before, active, weights, mobility_near, pressure)
        + (mid_couplings, low_couplings, *second_got),
        [out(3, rows, LANES)] + third_round.buffers(),
        [(3, rows, LANES)],
    )
    third_got = swap(buffers)

    def fine_kernel(stencil, *rest):
        got, (result, ends) = rest[:swaps], rest[swaps:]
        couplings(stencil, second_round.halos(0, got, ends, [3])[0], result)

    (fine_couplings,) = call(fine_kernel, (stencil, *second_got), [out(6, rows, LANES)], [(1, rows, LANES)])

    def products(coefs, field):
        return [[(product(coefs, 1 + 2 * dim, field), product(coefs, 2 + 2 * dim, field))] for dim in range(3)]

    def pressure_kernel(rhs, it, diag, trans, trans_before, stencil, fine_couplings, mid_couplings, low_couplings, *rest):
        got, (b_out, x_out, mid_side, low_side), buffers = rest[:swaps], rest[swaps : swaps + 4], rest[swaps + 4 : -1]
        (rim,) = third_round.halos(0, got, rest[-1], [0])
        b = rhs[0] - system_row(0, [it[c] for c in range(3)], rim, diag, trans, trans_before)
        b_out[...] = b
        x_out[...] = b * (OMEGA / stencil[0])
        fourth_round.emit(0, products(stencil, x_out), buffers)
        fourth_round.emit(3, [same(fine_couplings, range(6))] * 3, buffers)
        for part, grid, values, side in ((1, mid, mid_couplings, mid_side), (2, low, low_couplings, low_side)):
            side[...] = pack_sides([beside_of(*faces[2]) for faces in third_round.faces(part, got)], grid.dup)
            ends = []
            for y in (0, grid.height - 1):
                lines = pl.ds(y, grid.depth, stride=grid.height)
                parts = [values[c, lines, :] for c in range(6)]
                ends.append(jnp.concatenate(parts + [side[lines, :]]))
            fourth_round.put_rows(part, 1, *ends, buffers)

    b_fine, x_fine, mid_side, low_side, *buffers = call(
        pressure_kernel,
        (rhs, iterate, diag, trans, trans_before, stencil, fine_couplings, mid_couplings, low_couplings, *third_got),
        [out(rows, LANES)] * 2 + [out(mid.rows, LANES), out(low.rows, LANES)] + fourth_round.buffers(),
        [(1, rows, LANES)],
    )
    fourth_got = swap(buffers)

    def residual_kernel(b, x, stencil, one, it, active, weights, *rest):
        got, (x_out, adj_out, factor_out), buffers = rest[:swaps], rest[swaps : swaps + 3], rest[swaps + 3 : -2]
        ends, temp = rest[-2:]
        (rim,) = fourth_round.halos(0, got, ends, [0])
        off = off_apply(stencil, x[...], rim)
        residual = (1.0 - OMEGA) * b[...] - off
        q = (1.0 - OMEGA) * x[...] + (b[...] - off) * (OMEGA / stencil[0])
        mask = active[...].astype(F32)
        for c in range(3):
            factor = mask * weights[c]
            factor_out[c] = factor
            adj_out[c] = mask * it[c] + factor * q
        coarse = pair_sum_rows(pair_sum_x(residual, 1), depth, height, temp)
        x_out[...] = coarse * (OMEGA / one[0])
        near = (lambda at: x_out[at, :],) * 2
        channels = []
        for step in (mid.height, 1):
            channels.append([near, (lambda at, s=step: x_out[moved(at, s), :], lambda at, s=step: x_out[moved(at, -s), :])])
        channels.append([near, (lambda at: roll(x_out[at, :], -mid.dup, 1), lambda at: roll(x_out[at, :], mid.dup, 1))])
        fifth_round.emit(1, channels, buffers)
        fifth_round.emit(0, [same(adj_out, range(3))] * 3, buffers)

    x_mid, adj_known, adj_factor, *buffers = call(
        residual_kernel,
        (b_fine, x_fine, stencil, one, iterate, active, weights, *fourth_got),
        [out(mid.rows, LANES), out(3, rows, LANES), out(3, rows, LANES)] + fifth_round.buffers(),
        [(1, rows, LANES), (rows // 2, LANES)],
    )
    fifth_got = swap(buffers)

    def lines_kernel(mid_own, mid_side, low_own, low_side, *rest):
        got, windows = rest[:swaps], rest[swaps:]
        for part, window, own, side, ours, theirs in (
            (1, mid_window, mid_own, mid_side, windows[0], windows[1]),
            (2, low_window, low_own, low_side, windows[2], windows[3]),
        ):
            grid, line = window.grid, window.line
            halves = fourth_round.rows(part, 1, got)
            ours[...] = jnp.zeros(ours.shape, F32)
            theirs[...] = jnp.zeros(theirs.shape, F32)
            pairs = [(ours.at[c], own.at[c], c) for c in range(6)] + [(theirs, side, 6)]
            for ref, source, c in pairs:
                for a in range(grid.depth):
                    at = a * line + window.rim
                    ref[at : at + grid.height, :] = source[a * grid.height : (a + 1) * grid.height, :]
                for y, half in zip((-1, grid.height), halves):
                    ref[pl.ds(window.rim + y, grid.depth, stride=line), :] = half[c * grid.depth : (c + 1) * grid.depth]

    mid_lines, low_lines = (mid.depth * mid_window.line, LANES), (low.depth * low_window.line, LANES)
    mid_around, mid_beside, low_around, low_beside = call(
        lines_kernel,
        (mid_couplings, mid_side, low_couplings, low_side, *fourth_got),
        [out(6, *mid_lines), out(*mid_lines), out(6, *low_lines), out(*low_lines)],
    )

    def device(*steps):
        at = [lax.axis_index(name) for name in AXES]
        inside, flat = True, 0
        for position, size, step in zip(at, sizes, steps):
            inside = inside & (position + step >= 0) & (position + step < size)
        for position, size, step in zip(at, sizes, steps):
            flat = flat * size + jnp.where(inside, position + step, position)
        return flat

    last_groups = LANES // last_width
    last = jnp.concatenate([OMEGA / coarse_three[:1], coarse_three[1:]]).reshape(7, last_height, last_width)
    last = jnp.pad(last, ((0, 2 * last_groups - 7), (0, 0), (0, 0)))
    last = last.reshape(2, last_groups, last_height, last_width).transpose(0, 2, 1, 3).reshape(2 * last_height, LANES)
    keep = low.rows // low.dup
    own_at = keep + 2 * last_height
    block = own_at + 2
    signs = (-1, 1)

    def columns(near, far, sign):
        if sign < 0:
            parts = near, roll(far, 2, 1), roll(near, 2, 1)
        else:
            parts = roll(near, 2, 1), roll(far, 4, 1), roll(near, 8, 1)
        lane = lane_of(near)
        return jnp.where(lane < 2, parts[0], jnp.where(lane < 4, parts[1], jnp.where(lane < 6, parts[2], 0.0)))

    def low_kernel(x, one, mid_couplings, two, last, *rest):
        got, (sent, mark, ends, temp) = rest[:swaps], rest[swaps:]
        (rim,) = fifth_round.halos(1, got, ends, [0])
        value = x[...]
        total = (1.0 - OMEGA) * value
        for dim in range(3):
            total = total - mid_couplings[2 * dim] * rim.previous(value, dim)
            total = total - mid_couplings[2 * dim + 1] * rim.following(value, dim)
        residual = total * (one[0] * (1.0 / OMEGA))
        b = pair_sum_rows(pair_sum_x(residual, mid.dup), mid.depth, mid.height, temp)
        field = b * (OMEGA / two[0])
        to_next = [two[2 + 2 * dim] * field for dim in range(3)]
        to_previous = [two[1 + 2 * dim] * field for dim in range(3)]
        closed = Closed(low.height, low.dup)
        inner = (1.0 - OMEGA) * b
        for dim in range(3):
            inner = inner - closed.previous(to_next[dim], dim) - closed.following(to_previous[dim], dim)
        row, lane = lax.broadcasted_iota(jnp.int32, field.shape, 0), lane_of(field)
        layer, y = row // low.height, row % low.height
        outer = [
            jnp.where(layer == 0, -to_previous[0], 0.0),
            jnp.where(layer == low.depth - 1, -to_next[0], 0.0),
            jnp.where(y == 0, -to_previous[1], jnp.where(y == low.height - 1, -to_next[1], 0.0)),
            jnp.where(lane < low.dup, -to_previous[2], jnp.where(lane >= LANES - low.dup, -to_next[2], 0.0)),
        ]
        parts = [pair_sum_rows(pair_sum_x(v, low.dup), low.depth, low.height, temp) for v in [inner] + outer]
        parts = matmul(jnp.concatenate(parts), one_hot((LANES, LANES), lambda i, j: i == 2 * low.dup * j))
        parts = [parts[k * last_height : (k + 1) * last_height] for k in range(5)]
        upper = last[:last_height] + roll(parts[0], 7 * last_width, 1)
        lower = last[last_height:]
        for k in range(4):
            lower = lower + roll(parts[1 + k], k * last_width, 1)
        packed = jnp.zeros((keep, LANES), F32)
        phase = lane_of(packed) % low.dup
        for k in range(low.dup):
            packed = jnp.where(phase == k, field[k * keep : (k + 1) * keep], packed)
        filled = jnp.concatenate([packed, upper, lower, jnp.zeros((2, LANES), F32)])
        sent[...] = jnp.broadcast_to(filled[None], (count, block, LANES))
        mark[...] = filled

        def near(sign, size):
            return 0 if sign < 0 else size - 1

        def line(a, y):
            return x[a * mid.height + y : a * mid.height + y + 1, :]

        def across(a):
            return x[a * mid.height : (a + 1) * mid.height, :]

        def along(y):
            return x[pl.ds(y, mid.depth, stride=mid.height), :]

        def folded(value):
            return sum(roll(value[2 * k : 2 * k + 2], 6 * k, 1) for k in range(value.shape[0] // 2))

        for sz in signs:
            a = near(sz, mid.depth)
            for sy in signs:
                y = near(sy, mid.height)
                pair = fold(jnp.concatenate([line(a, y), line(a - sz, y)]))
                sent[device(0, sy, sz), own_at : own_at + 2, :] = jnp.concatenate([pair, line(a, y - sy)])
                for sx in signs:
                    corner = columns(line(a, y), line(a, y), sx)
                    sent[device(sx, sy, sz), own_at : own_at + 1, :] = corner
            for sx in signs:
                sent[device(sx, 0, sz), own_at : own_at + 2, :] = folded(columns(across(a), across(a - sz), sx))
        for sy in signs:
            y = near(sy, mid.height)
            for sx in signs:
                sent[device(sx, sy, 0), own_at : own_at + 2, :] = folded(columns(along(y), along(y - sy), sx))

    sent, mark = call(
        low_kernel,
        (x_mid, one, mid_couplings, two, last, *fifth_got),
        [out(count, block, LANES), out(block, LANES)],
        [(1, mid.rows, LANES), (mid.rows // 2, LANES)],
    )
    everyone = lax.all_to_all(sent, AXES, 0, 0)

    def late_kernel(mark, adj, couplings, mid_around, mid_beside, low_around, low_beside, *buffers):
        late_round.emit(0, [same(adj, range(3)) + same(couplings, range(6))], buffers)
        for part, window, ours, theirs in ((1, mid_window, mid_around, mid_beside), (2, low_window, low_around, low_beside)):
            ends = []
            for a in (0, window.grid.depth - 1):
                lines = slice(a * window.line, (a + 1) * window.line)
                parts = [fold(jnp.concatenate([ours[c, lines, :], ours[c + 1, lines, :]])) for c in (0, 2, 4)]
                ends.append(jnp.concatenate(parts + [theirs[lines, :]]))
            late_round.put_rows(part, 0, *ends, buffers)

    buffers = call(
        late_kernel,
        (mark, adj_known, fine_couplings, mid_around, mid_beside, low_around, low_beside),
        late_round.buffers(),
    )
    late_got = swap(buffers, (0,))

    def window_kernel(mark, x, *rest):
        (third, fourth, fifth), (x_out, lines_out, sides_out) = [rest[k * swaps : (k + 1) * swaps] for k in range(3)], rest[3 * swaps :]
        x_out[...] = jnp.zeros(x_out.shape, F32)
        near, far = fifth_round.faces(1, fifth)
        mid_window.fill(x_out.at[0], x[...])
        mid_window.fill(x_out.at[1], beside_of(*near[2]))
        mid_window.fill(x_out.at[2], beside_of(*far[2]))
        for faces, step in ((near, 0), (far, 1)):
            for layer, value in zip((-1 - step, mid.depth + step), faces[0]):
                x_out[0, mid_window.layer(layer), :] = value
            for y, value in zip((-1 - step, mid.height + step), faces[1]):
                x_out[0, mid_window.row(y), :] = value
        channels = fourth_round.faces(3, fourth) + third_round.faces(0, third, range(1, 4)) + fifth_round.faces(0, fifth)
        for c, faces in enumerate(channels):
            lines_out[c] = jnp.concatenate(faces[1])
        sides = [beside_of(*faces[2]) for faces in channels]
        for c in range(6):
            sides_out[c] = pack_sides(sides[2 * c : 2 * c + 2], 1)

    x_windows, line_halos, side_halos = call(
        window_kernel,
        (mark, x_mid, *third_got, *fourth_got, *fifth_got),
        [out(3, mid_window.rows, LANES), out(12, 2 * depth, LANES), out(6, rows, LANES)],
    )

    def ends_kernel(*rest):
        third, got, (*lines, layers_out) = rest[:swaps], rest[swaps : swaps + late], rest[swaps + late :]
        for part, window, ours, theirs in ((1, mid_window, *lines[:2]), (2, low_window, *lines[2:])):
            line = window.line
            for k, half in enumerate(late_round.rows(part, 0, got)):
                at = slice(k * line, (k + 1) * line)
                for pair in range(3):
                    both = unfold(half[pair * line : (pair + 1) * line])
                    ours[2 * pair, at, :] = both[:line]
                    ours[2 * pair + 1, at, :] = both[line:]
                theirs[at, :] = half[3 * line :]
        channels = late_round.faces(0, got)
        channels = channels[3:] + third_round.faces(0, third, range(1, 4)) + channels[:3]
        for c, faces in enumerate(channels):
            layers_out[c] = jnp.concatenate(faces[0])

    mid_ends, low_ends = (2 * mid_window.line, LANES), (2 * low_window.line, LANES)
    *ends, layer_halos = call(
        ends_kernel,
        (*third_got, *late_got),
        [out(6, *mid_ends), out(*mid_ends), out(6, *low_ends), out(*low_ends), out(12, 2 * height, LANES)],
    )

    last_rows, last_line = sizes[2] * sizes[1] * last_height, sizes[1] * last_height
    last_base = -(-(last_line + low_window.rim) // 8) * 8

    def solve_last(everyone, temp):
        channels = [[] for _ in range(2 * last_groups)]
        for first in range(0, sizes[0], last_groups):
            here = range(min(last_groups, sizes[0] - first))
            for g in here:
                for y in range(sizes[1]):
                    for z in range(sizes[2]):
                        sender = ((first + g) * sizes[1] + y) * sizes[2] + z
                        for half in range(2):
                            at = half * last_rows + z * last_line + y * last_height
                            start = keep + half * last_height
                            temp[g, at : at + last_height, :] = everyone[sender, start : start + last_height, :]
            parts = [temp[g] for g in here]
            group = lane_of(parts[0]) // last_width
            for q in range(last_groups):
                value = jnp.zeros_like(parts[0])
                for g in here:
                    value = jnp.where(group == g, roll(parts[g], last_width * (g - q), 1), value)
                channels[q].append(value[:last_rows])
                channels[last_groups + q].append(value[last_rows:])
        parts = [jnp.concatenate(tiles, axis=1) for tiles in channels[: last_groups + 4]]
        stencil, (inner, back, on, beside_y, beside_x) = parts[:7], parts[7:]
        y, x = row_y(inner, last_line), lane_of(inner)
        none = jnp.zeros((last_line, inner.shape[1]), F32)
        b = inner + jnp.concatenate([back[last_line:], none]) + jnp.concatenate([none, on[:-last_line]])
        b = b + jnp.where((y % last_height == 0) & (y > 0), roll(beside_y, 1, 0), 0.0)
        b = b + jnp.where((y % last_height == last_height - 1) & (y < last_line - 1), roll(beside_y, -1, 0), 0.0)
        b = b + jnp.where((x % last_width == 0) & (x > 0), roll(beside_x, 1, 1), 0.0)
        b = b + jnp.where((x % last_width == last_width - 1) & (x < inner.shape[1] - 1), roll(beside_x, -1, 1), 0.0)
        closed = Closed(last_line, 1)
        field = start = b * stencil[0]
        for sweep in range(COARSE_SWEEPS - 1):
            field = start + (1.0 - OMEGA) * field - off_apply(stencil, field, closed) * stencil[0]
        return field

    def spread_last(field, temp):
        gx, gy, gz = (lax.axis_index(name) for name in AXES)
        half, reach = low_window.line // 2, low_window.rim // 2
        layers = low.depth // 2 + 2
        dup = 2 * low.dup

        def taken(i, j):
            own = (j < LANES) & (i == gx * last_width + j // dup)
            before = (j >= LANES) & (j < LANES + low.dup) & (i == gx * last_width - 1)
            after = (j >= 2 * LANES - low.dup) & (i == (gx + 1) * last_width)
            return own | before | after

        at = last_base + (gz * (low.depth // 2) - 1) * last_line + gy * last_height - reach
        tiles = []
        for tile in range(0, field.shape[1], LANES):
            temp[...] = jnp.zeros(temp.shape, F32)
            temp[last_base : last_base + last_rows, :] = field[:, tile : tile + LANES]
            tiles.append(jnp.concatenate([temp[pl.ds(at + k * last_line, half), :] for k in range(layers)]))
        both = matmul(jnp.concatenate(tiles, axis=1), one_hot((field.shape[1], 2 * LANES), taken))
        return [spread_rows(both[:, k * LANES : (k + 1) * LANES], layers, half, temp) for k in range(2)]

    def low_windows(everyone, temp, result):
        around = [(sy, sz) for sz in (-1, 0, 1) for sy in (-1, 0, 1)]
        per = -(-len(around) * keep // 8) * 8
        for k, sx in enumerate((0, -1, 1)):
            for i, (sy, sz) in enumerate(around):
                temp[k * per + keep * i : k * per + keep * (i + 1), :] = everyone[device(sx, sy, sz), 0:keep, :]
        packed = temp[: 3 * per, :]
        lane = lane_of(packed)
        turned = {by: roll(packed, by, 1) for by in range(1 - low.dup, low.dup)}
        for k in range(low.dup):
            value = turned[-k]
            for m in range(1, low.dup):
                value = jnp.where(lane % low.dup == m, turned[m - k], value)
            own, before, after = (value[i * per : (i + 1) * per] for i in range(3))
            forms = [own]
            for cells in (1, 2):
                forms.append(beside_of(roll(before, low.dup * cells, 1), roll(after, -low.dup * cells, 1)))
            for i, (sy, sz) in enumerate(around):
                for j in range(keep):
                    a, y = divmod(k * keep + j, low.height)
                    a, y = a + sz * low.depth, y + sy * low.height
                    if -2 <= a < low.depth + 2 and -low_window.rim <= y < low.height + low_window.rim:
                        at = low_window.at(a, y)
                        for form, source in enumerate(forms):
                            result[form, at : at + 1, :] = source[keep * i + j : keep * i + j + 1]
        return [result[form] for form in range(3)]

    def mid_edges(everyone, x):
        def lines(*steps):
            return everyone[device(*steps), own_at : own_at + 2, :]

        def unfolded(value, n):
            return jnp.concatenate([roll(value, -6 * k, 1) for k in range(n // 2)])

        def sides(values, k):
            return beside_of(roll(values[0], -2 * k, 1), roll(values[1], -2 * k - 2, 1))

        for sz in signs:
            a = -1 if sz < 0 else mid.depth
            for sy in signs:
                y = -1 if sy < 0 else mid.height
                got = lines(0, sy, sz)
                pair = unfold(got[:1])
                for layer, at, value in ((a, y, pair[:1]), (a + sz, y, pair[1:]), (a, y + sy, got[1:])):
                    row = mid_window.at(layer, at)
                    x[0, row : row + 1, :] = value
                row = mid_window.at(a, y)
                x[1, row : row + 1, :] = sides([lines(sx, sy, sz)[:1] for sx in signs], 0)
            got = [unfolded(lines(sx, 0, sz), mid.height) for sx in signs]
            x[1, mid_window.layer(a), :] = sides(got, 0)
            x[1, mid_window.layer(a + sz), :] = sides(got, 1)
            x[2, mid_window.layer(a), :] = sides(got, 2)
        for sy in signs:
            y = -1 if sy < 0 else mid.height
            got = [unfolded(lines(sx, sy, 0), mid.depth) for sx in signs]
            x[1, mid_window.row(y), :] = sides(got, 0)
            x[1, mid_window.row(y + sy), :] = sides(got, 1)
            x[2, mid_window.row(y), :] = sides(got, 2)

    def full(window, lines, ends, side_lines, side_ends):
        line, none = window.line, jnp.zeros((window.line, LANES), F32)
        packed = jnp.concatenate([none, side_ends[:line, :], side_lines[...], side_ends[line:, :], none])
        return (
            lambda c: jnp.concatenate([none, ends[c, :line, :], lines[c], ends[c, line:, :], none]),
            lambda c: unpack_side(packed, c, window.grid.dup),
        )

    def gradient_factors(mobility, pressure, trans, trans_before, *rest):
        got, (inner, layer_out, line_out, side_out, ends) = rest[:swaps], rest[swaps:]
        faces = third_round.faces(0, got, range(4, 8))
        rims = [Rim(fine, f, ends, c) for c, f in enumerate(faces)]
        lines = pl.ds(0, depth, stride=height)
        drops = []
        for dim in range(3):
            drops.append(0.25 * trans[dim] * (pressure[0] - rims[3].following(pressure[0], dim)))
        side_drop = 0.25 * trans_before[2] * (faces[3][2][0] - pressure[0])
        sides = []
        for c in range(3):
            value = mobility[c]
            for dim in range(3):
                inner[3 * dim + c] = drops[dim] * (value + rims[c].following(value, dim))
            drop = 0.25 * trans_before[0, :height, :] * (faces[3][0][0] - pressure[0, :height, :])
            layer_out[c] = drop * (faces[c][0][0] + mobility[c, :height, :])
            drop = 0.25 * trans_before[1, lines, :] * (faces[3][1][0] - pressure[0, lines, :])
            line_out[c] = drop * (faces[c][1][0] + mobility[c, lines, :])
            sides.append(side_drop * (faces[c][2][0] + value))
        side_out[...] = pack_sides(sides, 1)

    gradient_inputs = call(
        gradient_factors,
        (mobility, pressure, trans, trans_before, *third_got),
        [out(9, rows, LANES), out(3, height, LANES), out(3, depth, LANES), out(rows, LANES)],
        [(4, rows, LANES)],
    )

    def final_kernel(
        everyone,
        x_windows,
        mid_around,
        mid_beside,
        low_around,
        low_beside,
        mid_ends,
        mid_side_ends,
        low_ends,
        low_side_ends,
        layer_halos,
        line_halos,
        side_halos,
        adj_known,
        adj_factor,
        couplings,
        terms,
        layer_terms,
        line_terms,
        side_terms,
        adj_out,
        grad_out,
        *scratch,
    ):
        last_temp, low_x, low_temp, x, temp, ends, around, beside, value_ref, adj, grad, sems = scratch
        added = spread_last(solve_last(everyone, last_temp), low_temp)
        low_values = low_windows(everyone, low_temp, low_x)
        pair = full(low_window, low_around, low_ends, low_beside, low_side_ends)
        results = smooth(low_values, added, pair, low_window.line, low.dup)
        inner = slice(low_window.line, (low.depth + 3) * low_window.line)
        added = [spread_rows(v[inner], low.depth + 2, low_window.line, temp) for v in results]
        x[...] = x_windows[...]
        mid_edges(everyone, x)
        pair = full(mid_window, mid_around, mid_ends, mid_beside, mid_side_ends)
        around[...], beside[...] = smooth([x[k] for k in range(3)], added, pair, mid_window.line, mid.dup)

        def own(ref):
            lines = [ref[mid_window.layer(a), :] for a in range(mid.depth)]
            return spread_rows(jnp.concatenate(lines), mid.depth, mid.height, temp)

        def layer(ref, a):
            return spread_lines(ref[mid_window.layer(a), :], temp)

        def lines(ref, y):
            return spread_lines(ref[mid_window.row(y), :], temp)

        def one_row(a, y):
            at = mid_window.at(a, y)
            return around[at : at + 1, :]

        value, side = own(around), own(beside)
        value_ref[...] = value
        layers = [(a, layer(around, a), layer(beside, a)) for a in (-1, mid.depth)]
        rows_y = [(y, lines(around, y), lines(beside, y)) for y in (-1, mid.height)]
        rim = Rim(fine, [[v[1] for v in layers], [v[1] for v in rows_y], (side, side)], ends, 0)

        def gain(value, shifts, coupling):
            total = (1.0 - OMEGA) * value
            for k in range(6):
                total = total - coupling(k) * shifts[k]
            return total

        shifts = [shift(value, dim) for dim in range(3) for shift in (rim.previous, rim.following)]
        own_gain = gain(value, shifts, lambda k: couplings[k])
        for c in range(3):
            adj[c] = adj_known[c] + adj_factor[c] * own_gain
        copies = [pltpu.make_async_copy(adj, adj_out, sems.at[3])]
        copies[0].start()

        def along_x(value, side):
            lane = lane_of(value)
            return [jnp.where(lane < 1, side, roll(value, 1, 1)), jnp.where(lane >= LANES - 1, side, roll(value, -1, 1))]

        def ended(value, low, high):
            row = lax.broadcasted_iota(jnp.int32, value.shape, 0)
            n = value.shape[0]
            return [jnp.where(row == 0, low, roll(value, 1, 0)), jnp.where(row == n - 1, high, roll(value, -1, 0))]

        layer_gains, line_gains = [], []
        for k, (a, here, there) in enumerate(layers):
            shifts = [here, value[:height]] if k == 0 else [value[rows - height :], here]
            shifts += ended(here, one_row(a, -1), one_row(a, mid.height)) + along_x(here, there)
            layer_gains.append(gain(here, shifts, lambda c: layer_halos[c, k * height : (k + 1) * height, :]))
        for k, (y, here, there) in enumerate(rows_y):
            inside = value_ref[pl.ds(0 if k == 0 else height - 1, depth, stride=height), :]
            shifts = ended(here, one_row(-1, y), one_row(mid.depth, y))
            shifts += ([here, inside] if k == 0 else [inside, here]) + along_x(here, there)
            line_gains.append(gain(here, shifts, lambda c: line_halos[c, k * depth : (k + 1) * depth, :]))
        lane = lane_of(side)
        side_rim = Rim(fine, [[v[2] for v in layers], [v[2] for v in rows_y], (side, side)], ends, 1)
        shifts = [shift(side, dim) for dim in range(2) for shift in (side_rim.previous, side_rim.following)]
        shifts += [jnp.where(lane < LANES // 2, side, value), jnp.where(lane < LANES // 2, value, side)]

        def side_halo(c):
            return unpack_side(side_halos[c // 2], 1, 1) if c % 2 else side_halos[c // 2]

        side_gain = gain(side, shifts, side_halo)
        adj_rims = []
        for c in range(3):
            known, factor = 9 + c, 6 + c
            faces = [
                [
                    layer_halos[known, k * height : (k + 1) * height, :]
                    + layer_halos[factor, k * height : (k + 1) * height, :] * layer_gains[k]
                    for k in range(2)
                ],
                [
                    line_halos[known, k * depth : (k + 1) * depth, :] + line_halos[factor, k * depth : (k + 1) * depth, :] * line_gains[k]
                    for k in range(2)
                ],
                (side_halo(known) + side_halo(factor) * side_gain,) * 2,
            ]
            adj_rims.append(Rim(fine, faces, ends, 2 + c))
        values = [adj[c] for c in range(3)]
        lines = pl.ds(0, depth, stride=height)
        parts = []
        for c in range(3):
            layer, line, side = (adj_rims[c].faces[dim][0] for dim in range(3))
            parts.append(
                (
                    layer_terms[c] * (layer - values[c][:height]),
                    line_terms[c] * (line - adj[c, lines, :]),
                    unpack_side(side_terms[...], c, 1) * (side - values[c]),
                )
            )
        below = Rim(fine, [(sum(p[dim] for p in parts),) * 2 for dim in range(3)], ends, 5)
        for dim in range(3):
            here = 0.0
            for c in range(3):
                here = here + terms[3 * dim + c] * (values[c] - adj_rims[c].following(values[c], dim))
            grad[dim] = here + below.previous(here, dim)
            copies.append(pltpu.make_async_copy(grad.at[dim], grad_out.at[dim], sems.at[dim]))
            copies[-1].start()
        for copy in copies:
            copy.wait()

    adjoint, gradient = call(
        final_kernel,
        (everyone, x_windows, mid_around, mid_beside, low_around, low_beside, *ends, layer_halos)
        + (line_halos, side_halos, adj_known, adj_factor, fine_couplings, *gradient_inputs),
        [out(3, rows, LANES)] * 2,
        [
            (min(sizes[0], last_groups), 2 * last_rows, LANES),
            (3, low_window.rows, LANES),
            (max(low_window.rows, 96, 2 * last_base + last_rows), LANES),
            (3, mid_window.rows, LANES),
            (mid_window.rows, LANES),
            (6, rows, LANES),
            (mid_window.rows, LANES),
            (mid_window.rows, LANES),
            (rows, LANES),
            (3, rows, LANES),
            (3, rows, LANES),
            pltpu.SemaphoreType.DMA((4,)),
        ],
        far_outputs=2,
    )
    shape = (3, depth, height, width)
    return adjoint.reshape(shape), gradient.reshape(shape)


def solution(mesh):
    cells = P("layer", "gy", "gx")
    fields = P(None, "layer", "gy", "gx")
    return jax.shard_map(
        local,
        mesh=mesh,
        in_specs=(
            fields,
            cells,
            fields,
            fields,
            fields,
            fields,
            fields,
            fields,
            fields,
            fields,
            cells,
            fields,
        ),
        out_specs=(fields, fields),
        check_vma=False,
    )
```

```python
import itertools

import jax
import jax.numpy as jnp
from jax import lax
from jax.experimental import pallas as pl
from jax.experimental.pallas import tpu as pltpu
from jax.sharding import PartitionSpec as P

SWEEPS = 3
LEVELS = 3
COARSE_SWEEPS = 4
OMEGA = 0.8
LANES = 128
AXES = ("gx", "gy", "layer")
BY_DIM = ("layer", "gy", "gx")
ORDER = ((0, 1), (0, 0), (1, 1), (1, 0), (2, 1), (2, 0))
F32 = jnp.float32


def pair_route(axis, phase):
    sizes = [lax.axis_size(name) for name in AXES]
    k = AXES.index(axis)
    n = sizes[k]
    route = []
    for index in itertools.product(*[range(size) for size in sizes]):
        target = list(index)
        if phase == 0:
            target[k] = index[k] ^ 1
        elif 0 < index[k] < n - 1 or k == 0:
            target[k] = (((index[k] + 1) % n ^ 1) - 1) % n
        else:
            target[0] = index[0] ^ 1
        flat = [(i[0] * sizes[1] + i[1]) * sizes[2] + i[2] for i in (index, target)]
        route.append(tuple(flat))
    return route


def phases(dim):
    return min(lax.axis_size(BY_DIM[dim]), 3) - 1


def sends(dims=(0, 1, 2)):
    return [(dim, phase) for dim, phase in ORDER if dim in dims and phase < phases(dim)]


def swap(buffers, dims=(0, 1, 2)):
    return [lax.ppermute(b, AXES, pair_route(BY_DIM[dim], phase)) for b, (dim, phase) in zip(buffers, sends(dims))]


class Grid:
    def __init__(self, depth, height, dup):
        self.depth, self.height, self.dup = depth, height, dup
        self.rows = depth * height
        self.width = LANES // dup
        self.groups = self.rows // 8

    def lines(self, dim):
        return (self.height, self.depth)[dim]

    def tiles(self, count):
        return -(-2 * self.dup * count * self.groups // LANES)

    def place(self, count, c, k):
        return divmod(2 * self.dup * (count * k + c), LANES)


class Message:
    def __init__(self, *parts, dims=(0, 1, 2)):
        self.parts, self.dims = parts, dims

    def size(self, part, dim):
        part = self.parts[part]
        if isinstance(part, dict):
            return part.get(dim, 0)
        if dim not in part[2:] and len(part) > 2:
            return 0
        return part[0].tiles(part[1]) * 8 if dim == 2 else part[1] * part[0].lines(dim)

    def start(self, part, dim):
        return sum(self.size(i, dim) for i in range(part))

    def buffers(self):
        return [jax.ShapeDtypeStruct((self.start(len(self.parts), dim), LANES), F32) for dim, phase in sends(self.dims)]

    def put(self, dim, rows, first, last, out):
        if phases(dim) == 0:
            return
        out = dict(zip(sends(self.dims), out))
        even = lax.axis_index(BY_DIM[dim]) % 2 == 0
        out[dim, 0][rows] = last if first is last else jnp.where(even, last, first)
        if phases(dim) == 2:
            out[dim, 1][rows] = last if first is last else jnp.where(even, first, last)

    def put_rows(self, part, dim, first, last, out):
        start = self.start(part, dim)
        self.put(dim, slice(start, start + self.size(part, dim)), first, last, out)

    def emit(self, part, channels, out):
        grid = self.parts[part][0]
        lane = lax.broadcasted_iota(jnp.int32, (8, LANES), 1)
        for dim in range(3):
            if self.size(part, dim) == 0:
                continue
            start = self.start(part, dim)
            if dim == 2:
                count, dup = self.parts[part][1], grid.dup
                tiles = [jnp.zeros((8, LANES), F32)] * grid.tiles(count)
                for c, (first, last) in enumerate(channels[dim]):
                    for k in range(grid.groups):
                        tile, at = grid.place(count, c, k)
                        rows = slice(8 * k, 8 * k + 8)
                        value = last(rows)
                        if first is not last:
                            value = jnp.where(lane < dup, first(rows), value)
                        here = (lane >= at) & (lane < at + 2 * dup)
                        tiles[tile] = jnp.where(here, roll(value, at + dup, 1), tiles[tile])
                value = jnp.concatenate(tiles)
                self.put(dim, slice(start, start + 8 * len(tiles)), value, value, out)
                continue
            if dim == 0:
                low, high = slice(0, grid.height), slice(grid.rows - grid.height, grid.rows)
            else:
                low, high = (pl.ds(s, grid.depth, stride=grid.height) for s in (0, grid.height - 1))
            n = grid.lines(dim)
            for c, (first, last) in enumerate(channels[dim]):
                self.put(dim, slice(start + c * n, start + (c + 1) * n), first(low), last(high), out)

    def both(self, dim, rows, got):
        if phases(dim) == 0:
            return (jnp.zeros((rows.stop - rows.start, LANES), F32),) * 2
        got = dict(zip(sends(self.dims), got))
        me, n = lax.axis_index(BY_DIM[dim]), lax.axis_size(BY_DIM[dim])
        even = me % 2 == 0
        one = got[dim, 0][rows]
        if phases(dim) == 1:
            return jnp.where(even, 0.0, one), jnp.where(even, one, 0.0)
        two = got[dim, 1][rows]
        before, after = jnp.where(even, two, one), jnp.where(even, one, two)
        return jnp.where(me > 0, before, 0.0), jnp.where(me < n - 1, after, 0.0)

    def rows(self, part, dim, got):
        start = self.start(part, dim)
        return self.both(dim, slice(start, start + self.size(part, dim)), got)

    def faces(self, part, got, channels=None):
        grid, count = self.parts[part][:2]
        channels = range(count) if channels is None else channels
        result = [[None] * 3 for _ in channels]
        for dim in range(3):
            if self.size(part, dim) == 0:
                continue
            start = self.start(part, dim)
            if dim == 2:
                dup = grid.dup
                before, after = self.both(dim, slice(start, start + 8 * grid.tiles(count)), got)
                merged = jnp.where(lane_of(before) % (2 * dup) < dup, roll(after, -dup, 1), roll(before, dup, 1))
                for i, c in enumerate(channels):
                    pieces = []
                    for k in range(grid.groups):
                        tile, at = grid.place(count, c, k)
                        pieces.append(roll(merged[8 * tile : 8 * tile + 8], -at - dup, 1))
                    result[i][dim] = (jnp.concatenate(pieces),) * 2
            else:
                size = grid.lines(dim)
                for i, c in enumerate(channels):
                    result[i][dim] = self.both(dim, slice(start + c * size, start + (c + 1) * size), got)
        return result

    def halos(self, part, got, scratch, channels=None):
        return [Rim(self.parts[part][0], r, scratch, c) for c, r in enumerate(self.faces(part, got, channels))]


class Window:
    def __init__(self, grid, rim):
        self.grid, self.rim = grid, rim
        self.line = grid.height + 2 * rim
        self.rows = (grid.depth + 4) * self.line

    def at(self, layer, y):
        return (layer + 2) * self.line + self.rim + y

    def layer(self, layer):
        return slice(self.at(layer, 0), self.at(layer, self.grid.height))

    def row(self, y):
        return pl.ds(self.at(0, y), self.grid.depth, stride=self.line)

    def fill(self, ref, own):
        height = self.grid.height
        for a in range(self.grid.depth):
            ref[self.layer(a), :] = own[a * height : (a + 1) * height]


class Rim:
    def __init__(self, grid, faces, scratch, c):
        self.grid, self.faces = grid, faces
        ends = scratch.at[c]
        ends[pl.ds(0, grid.depth, stride=grid.height), :] = faces[1][0]
        ends[pl.ds(grid.height - 1, grid.depth, stride=grid.height), :] = faces[1][1]
        self.y_ends = ends[...]

    def previous(self, value, dim):
        g = self.grid
        if dim == 0:
            return jnp.concatenate([self.faces[0][0], value[: g.rows - g.height]])
        if dim == 1:
            return jnp.where(row_y(value, g.height) == 0, self.y_ends, roll(value, 1, 0))
        return jnp.where(lane_of(value) < g.dup, self.faces[2][0], roll(value, g.dup, 1))

    def following(self, value, dim):
        g = self.grid
        if dim == 0:
            return jnp.concatenate([value[g.height :], self.faces[0][1]])
        if dim == 1:
            return jnp.where(row_y(value, g.height) == g.height - 1, self.y_ends, roll(value, -1, 0))
        return jnp.where(lane_of(value) >= value.shape[1] - g.dup, self.faces[2][1], roll(value, -g.dup, 1))


class Closed:
    def __init__(self, height, dup):
        self.height, self.dup = height, dup

    def previous(self, value, dim):
        if dim == 0:
            return jnp.concatenate([jnp.zeros_like(value[: self.height]), value[: -self.height]])
        if dim == 1:
            return jnp.where(row_y(value, self.height) == 0, 0.0, roll(value, 1, 0))
        return jnp.where(lane_of(value) < self.dup, 0.0, roll(value, self.dup, 1))

    def following(self, value, dim):
        if dim == 0:
            return jnp.concatenate([value[self.height :], jnp.zeros_like(value[: self.height])])
        if dim == 1:
            return jnp.where(row_y(value, self.height) == self.height - 1, 0.0, roll(value, -1, 0))
        return jnp.where(lane_of(value) >= value.shape[1] - self.dup, 0.0, roll(value, -self.dup, 1))


def roll(value, shift, axis):
    shift %= value.shape[axis]
    return pltpu.roll(value, shift, axis) if shift else value


def row_y(value, height):
    return lax.broadcasted_iota(jnp.int32, value.shape, 0) % height


def lane_of(value):
    return lax.broadcasted_iota(jnp.int32, value.shape, 1)


def loader(ref, c):
    return lambda rows: ref[c, rows, :]


def product(coefs, k, ref):
    return lambda rows: coefs[k, rows, :] * ref[rows, :]


def off_apply(stencil, field, rim):
    total = 0.0
    for dim in range(3):
        total = total + rim.previous(stencil[2 + 2 * dim] * field, dim)
        total = total + rim.following(stencil[1 + 2 * dim] * field, dim)
    return total


def block_row(blocks, c, values):
    return blocks[c] * values[0] + blocks[3 + c] * values[1] + blocks[6 + c] * values[2]


def system_row(c, values, rim, blocks, trans, trans_before):
    total = block_row(blocks, c, values)
    v = values[c]
    for dim in range(3):
        total = total + trans[dim] * (v - rim.following(v, dim))
        total = total + trans_before[dim] * (v - rim.previous(v, dim))
    return total


def pair_sum_x(value, dup):
    odd = (lane_of(value) // dup) % 2 == 1
    return value + jnp.where(odd, roll(value, dup, 1), roll(value, -dup, 1))


def pair_sum_rows(value, depth, height, scratch):
    half = depth // 2
    parts = [value[2 * a * height : (2 * a + 1) * height] + value[(2 * a + 1) * height : (2 * a + 2) * height] for a in range(half)]
    whole = jnp.concatenate(parts)
    count = half * height // 2
    sums = []
    for at in range(0, whole.shape[1], LANES):
        scratch[: half * height, :] = whole[:, at : at + LANES]
        sums.append(scratch[pl.ds(0, count, stride=2), :] + scratch[pl.ds(1, count, stride=2), :])
    return jnp.concatenate(sums, axis=1)


def spread_rows(value, depth, height, scratch):
    count = depth * height
    tiles = []
    for at in range(0, value.shape[1], LANES):
        scratch[pl.ds(0, count, stride=2), :] = value[:, at : at + LANES]
        scratch[pl.ds(1, count, stride=2), :] = value[:, at : at + LANES]
        wide = scratch[: 2 * count, :]
        tiles.append(jnp.concatenate([wide[2 * height * (a // 2) : 2 * height * (a // 2 + 1)] for a in range(2 * depth)]))
    return jnp.concatenate(tiles, axis=1)


def spread_lines(value, scratch):
    count = value.shape[0]
    scratch[pl.ds(0, count, stride=2), :] = value
    scratch[pl.ds(1, count, stride=2), :] = value
    return scratch[: 2 * count, :]


def fold(value):
    half = value.shape[0] // 2
    return jnp.where(lane_of(value[:half]) % 2 == 0, value[:half], value[half:])


def unfold(value):
    even = lane_of(value) % 2 == 0
    return jnp.concatenate([jnp.where(even, value, roll(value, 1, 1)), jnp.where(even, roll(value, -1, 1), value)])


def beside_of(before, after):
    if before is after:
        return before
    return jnp.where(lane_of(before) < LANES // 2, before, after)


def pack_sides(values, dup):
    total = jnp.zeros_like(values[0])
    lane = lane_of(total)
    for c, value in enumerate(values):
        total = jnp.where((lane >= dup * c) & (lane < dup * (c + 1)), roll(value, dup * c, 1), total)
        high = LANES - dup * c
        total = jnp.where((lane >= high - dup) & (lane < high), roll(value, -dup * c, 1), total)
    return total


def unpack_side(value, c, dup):
    return beside_of(roll(value, -dup * c, 1), roll(value, dup * c, 1))


def moved(rows, by):
    if isinstance(rows, slice):
        return slice(rows.start + by, rows.stop + by)
    return pl.ds(rows.start + by, rows.size, stride=rows.stride)


def shifts_of(value, inner, outer, line, dup, beside):
    none = jnp.zeros((line, LANES), F32)
    lane = lane_of(value)
    if beside:
        low, high = jnp.where(lane < LANES // 2, outer, inner), jnp.where(lane < LANES // 2, inner, outer)
    else:
        low, high = jnp.where(lane < dup, outer, roll(value, dup, 1)), jnp.where(lane >= LANES - dup, outer, roll(value, -dup, 1))
    return [
        jnp.concatenate([none, value[:-line]]),
        jnp.concatenate([value[line:], none]),
        roll(value, 1, 0),
        roll(value, -1, 0),
        low,
        high,
    ]


def smooth(x, added, couplings, line, dup):
    around, beside, second = x[0] + added[0], x[1] + added[1], x[2] + added[1]
    results = []
    for k, (value, shifts) in enumerate(
        (
            (around, shifts_of(around, None, beside, line, dup, False)),
            (beside, shifts_of(beside, around, second, line, dup, True)),
        )
    ):
        total = x[k] + (1.0 - OMEGA) * value
        for c in range(6):
            total = total - couplings[k](c) * shifts[c]
        results.append(total)
    return results


def one_hot(shape, hit):
    return jnp.where(hit(lax.broadcasted_iota(jnp.int32, shape, 0), lax.broadcasted_iota(jnp.int32, shape, 1)), 1.0, 0.0).astype(F32)


def matmul(values, ones):
    n = values.shape[0]
    extra = -n % 16
    if extra:
        values = jnp.concatenate([values, jnp.zeros((extra, values.shape[1]), F32)])
    parts = []
    for _ in range(3):
        parts.append(values.astype(jnp.bfloat16))
        values = values - parts[-1].astype(F32)
    product = jnp.dot(jnp.concatenate(parts), ones.astype(jnp.bfloat16), preferred_element_type=F32)
    step = n + extra
    return (product[2 * step : 2 * step + n] + product[step : step + n]) + product[:n]


def call(kernel, inputs, outputs, scratch=(), far_inputs=0, far_outputs=0):
    inputs = list(inputs)
    for i in range(far_inputs):
        inputs[i] = pltpu.with_memory_space_constraint(inputs[i], pltpu.HBM)

    def specs(count, far):
        return [pl.BlockSpec(memory_space=pltpu.HBM if i < far else pltpu.VMEM) for i in range(count)]

    return pl.pallas_call(
        kernel,
        out_shape=list(outputs),
        in_specs=specs(len(inputs), far_inputs),
        out_specs=specs(len(outputs), far_outputs),
        scratch_shapes=[pltpu.VMEM(shape, F32) if isinstance(shape, tuple) else shape for shape in scratch],
        compiler_params=pltpu.CompilerParams(vmem_limit_bytes=24 * 2**20),
    )(*inputs)


def local(
    source,
    active_cells,
    diag_blocks,
    frozen_inverses,
    transmissibility,
    pressure_weights,
    stencil_fine,
    coarse_one,
    coarse_two,
    coarse_three,
    pressure_state,
    mobilities,
):
    depth, height, width = active_cells.shape
    low_depth, low_height, low_width = coarse_two.shape[1:]
    last_height, last_width = coarse_three.shape[2:]
    fine = Grid(depth, height, 1)
    mid = Grid(depth // 2, height // 2, 2)
    low = Grid(low_depth, low_height, 4)
    mid_window, low_window = Window(mid, 4), Window(low, 2)
    sizes = [lax.axis_size(name) for name in AXES]
    count = sizes[0] * sizes[1] * sizes[2]
    swaps = len(sends())
    rows = fine.rows
    first_round = Message((fine, 4), (mid, 1), (low, 1))
    second_round = Message((fine, 4))
    third_round = Message((fine, 8), (mid, 6, 2), (low, 6, 2))
    fourth_round = Message((fine, 1), {1: 4 * mid.depth}, {1: 4 * low.depth}, {2: 4 * depth})
    fifth_round = Message((mid, 2), {1: 2 * depth}, {2: 3 * depth})
    late_round = Message((fine, 9), {0: 4 * mid_window.line}, {0: 4 * low_window.line})

    def flat(array):
        return array.reshape(array.shape[:-3] + (rows, width))

    def out(*shape):
        return jax.ShapeDtypeStruct(shape, F32)

    source, active, diag, frozen, trans, weights, stencil, pressure, mobility = (
        flat(a)
        for a in (
            source,
            active_cells,
            diag_blocks,
            frozen_inverses,
            transmissibility,
            pressure_weights,
            stencil_fine,
            pressure_state,
            mobilities,
        )
    )
    pressure = pressure[None]

    def coupling_faces(coefs):
        return [[(loader(coefs, 1 + 2 * dim), loader(coefs, 2 + 2 * dim))] for dim in range(3)]

    def widen(values, dup):
        wide = matmul(values, one_hot((values.shape[1], LANES), lambda i, j: i == j // dup))
        return wide.reshape(7, wide.shape[0] // 7, LANES)

    def start_kernel(source, active, frozen, trans, one, two, rhs_out, it_out, frozen_out, trans_out, one_out, two_out, *rest):
        buffers, (source_in, active_in, one_in, two_in, two_flat, sems) = rest[:-6], rest[-6:]
        order = [k for c in range(3) for k in (c, 3 + c, 6 + c)]
        pairs = [(active, active_in), (source, source_in)] + [(frozen.at[k], frozen_out.at[k]) for k in order]
        pairs += [(trans, trans_out), (one, one_in), (two, two_in)]
        copies = [pltpu.make_async_copy(a, b, sems.at[i]) for i, (a, b) in enumerate(pairs)]
        for copy in copies[-2:] + copies[:-2]:
            copy.start()
        copies[-2].wait()
        copies[-1].wait()
        one_out[...] = widen(one_in[...].reshape(7 * mid.rows, mid.width), mid.dup)
        for c in range(7):
            for a in range(low.depth):
                at = c * low.rows + a * low.height
                two_flat[at : at + low.height, :] = two_in[c, a]
        two_out[...] = widen(two_flat[...], low.dup)
        first_round.emit(1, coupling_faces(one_out), buffers)
        first_round.emit(2, coupling_faces(two_out), buffers)
        copies[0].wait()
        mask = active_in[...].astype(F32)
        copies[1].wait()
        rhs = [source_in[c] * mask for c in range(3)]
        for c in range(3):
            rhs_out[c] = rhs[c]
        for c in range(3):
            for copy in copies[2 + 3 * c : 5 + 3 * c]:
                copy.wait()
            it_out[c] = block_row(frozen_out, c, rhs)
        copies[-3].wait()
        its = [(loader(it_out, c),) * 2 for c in range(3)]
        first_round.emit(0, [its + [(loader(trans_out, dim),) * 2] for dim in range(3)], buffers)

    rhs, iterate, frozen, trans, one, two, *buffers = call(
        start_kernel,
        (source, active, frozen, trans, coarse_one.reshape(7, mid.rows, mid.width), coarse_two),
        [out(3, rows, LANES)] * 2
        + [out(9, rows, LANES), out(3, rows, LANES), out(7, mid.rows, LANES), out(7, low.rows, LANES)]
        + first_round.buffers(),
        [
            (3, rows, LANES),
            pltpu.VMEM((rows, LANES), jnp.int32),
            (7, mid.rows, mid.width),
            (7, low.depth, low.height, low.width),
            (7 * low.rows, low.width),
            pltpu.SemaphoreType.DMA((14,)),
        ],
        far_inputs=6,
    )
    got = swap(buffers)

    def couplings(coefs, rim, result):
        scale = OMEGA / coefs[0]
        for dim in range(3):
            result[2 * dim] = scale * rim.previous(coefs[2 + 2 * dim], dim)
            result[2 * dim + 1] = scale * rim.following(coefs[1 + 2 * dim], dim)

    def coarse_couplings(mobility, one, two, *rest):
        got, outs, mobility_out, scratch = rest[:swaps], rest[swaps : swaps + 2], rest[swaps + 2], rest[swaps + 3 :]
        fetch = pltpu.make_async_copy(mobility, mobility_out, scratch[2])
        fetch.start()
        for part, coefs, result, ends in ((1, one, outs[0], scratch[0]), (2, two, outs[1], scratch[1])):
            couplings(coefs, first_round.halos(part, got, ends)[0], result)
        fetch.wait()

    mid_couplings, low_couplings, mobility_near = call(
        coarse_couplings,
        (mobility, one, two, *got),
        [out(6, mid.rows, LANES), out(6, low.rows, LANES), out(3, rows, LANES)],
        [(1, mid.rows, LANES), (1, low.rows, LANES), pltpu.SemaphoreType.DMA],
        far_inputs=1,
    )

    def sweep_one(rhs, it, frozen, diag, trans, stencil, *rest):
        got, (it_out, before_out), buffers, ends = rest[:swaps], rest[swaps : swaps + 2], rest[swaps + 2 : -1], rest[-1]
        rims = first_round.halos(0, got, ends)
        trans_before = [rims[3].previous(trans[dim], dim) for dim in range(3)]
        values = [it[c] for c in range(3)]
        rest = [rhs[c] - system_row(c, values, rims[c], diag, trans, trans_before) for c in range(3)]
        for c in range(3):
            before_out[c] = trans_before[c]
            it_out[c] = values[c] + block_row(frozen, c, rest)
        channels = [(loader(it_out, c),) * 2 for c in range(3)]
        second_round.emit(0, [channels + faces for faces in coupling_faces(stencil)], buffers)

    iterate, trans_before, *buffers = call(
        sweep_one,
        (rhs, iterate, frozen, diag, trans, stencil, *got),
        [out(3, rows, LANES)] * 2 + second_round.buffers(),
        [(4, rows, LANES)],
    )
    second_got = swap(buffers)

    def same(ref, channels):
        return [(loader(ref, c),) * 2 for c in channels]

    def sweep_two(
        rhs, it, frozen, diag, trans, trans_before, active, weights, mobility, pressure, mid_couplings, low_couplings, *rest
    ):
        got, it_out, buffers, ends = rest[:swaps], rest[swaps], rest[swaps + 1 : -1], rest[-1]
        rims = second_round.halos(0, got, ends, range(3))
        values = [it[c] for c in range(3)]
        rest = [rhs[c] - system_row(c, values, rims[c], diag, trans, trans_before) for c in range(3)]
        for c in range(3):
            it_out[c] = values[c] + block_row(frozen, c, rest)
        factors = [(lambda at, c=c: active[at, :].astype(F32) * weights[c, at, :],) * 2 for c in range(3)]
        states = same(mobility, range(3)) + same(pressure, range(1))
        third_round.emit(0, [same(it_out, range(1)) + factors + states] * 3, buffers)
        third_round.emit(1, [same(mid_couplings, range(6))] * 3, buffers)
        third_round.emit(2, [same(low_couplings, range(6))] * 3, buffers)

    iterate, *buffers = call(
        sweep_two,
        (rhs, iterate, frozen, diag, trans, trans_before, active, weights, mobility_near, pressure)
        + (mid_couplings, low_couplings, *second_got),
        [out(3, rows, LANES)] + third_round.buffers(),
        [(3, rows, LANES)],
    )
    third_got = swap(buffers)

    def fine_kernel(stencil, *rest):
        got, (result, ends) = rest[:swaps], rest[swaps:]
        couplings(stencil, second_round.halos(0, got, ends, [3])[0], result)

    (fine_couplings,) = call(fine_kernel, (stencil, *second_got), [out(6, rows, LANES)], [(1, rows, LANES)])

    def products(coefs, field):
        return [[(product(coefs, 1 + 2 * dim, field), product(coefs, 2 + 2 * dim, field))] for dim in range(3)]

    def pressure_kernel(rhs, it, diag, trans, trans_before, stencil, fine_couplings, mid_couplings, low_couplings, *rest):
        got, (b_out, x_out, mid_side, low_side), buffers = rest[:swaps], rest[swaps : swaps + 4], rest[swaps + 4 : -1]
        (rim,) = third_round.halos(0, got, rest[-1], [0])
        b = rhs[0] - system_row(0, [it[c] for c in range(3)], rim, diag, trans, trans_before)
        b_out[...] = b
        x_out[...] = b * (OMEGA / stencil[0])
        fourth_round.emit(0, products(stencil, x_out), buffers)
        for part, grid, values, side in ((1, mid, mid_couplings, mid_side), (2, low, low_couplings, low_side)):
            side[...] = pack_sides([beside_of(*faces[2]) for faces in third_round.faces(part, got)], grid.dup)
            ends = []
            for y in (0, grid.height - 1):
                lines = pl.ds(y, grid.depth, stride=grid.height)
                parts = [fold(jnp.concatenate([values[c, lines, :], values[c + 1, lines, :]])) for c in (0, 2, 4)]
                ends.append(jnp.concatenate(parts + [side[lines, :]]))
            fourth_round.put_rows(part, 1, *ends, buffers)

    b_fine, x_fine, mid_side, low_side, *buffers = call(
        pressure_kernel,
        (rhs, iterate, diag, trans, trans_before, stencil, fine_couplings, mid_couplings, low_couplings, *third_got),
        [out(rows, LANES)] * 2 + [out(mid.rows, LANES), out(low.rows, LANES)] + fourth_round.buffers(),
        [(1, rows, LANES)],
    )
    fourth_got = swap(buffers)

    def residual_kernel(b, x, stencil, one, it, active, weights, *rest):
        got, (x_out, adj_out, factor_out), buffers = rest[:swaps], rest[swaps : swaps + 3], rest[swaps + 3 : -2]
        ends, temp = rest[-2:]
        (rim,) = fourth_round.halos(0, got, ends, [0])
        off = off_apply(stencil, x[...], rim)
        residual = (1.0 - OMEGA) * b[...] - off
        q = (1.0 - OMEGA) * x[...] + (b[...] - off) * (OMEGA / stencil[0])
        mask = active[...].astype(F32)
        for c in range(3):
            factor = mask * weights[c]
            factor_out[c] = factor
            adj_out[c] = mask * it[c] + factor * q
        coarse = pair_sum_rows(pair_sum_x(residual, 1), depth, height, temp)
        x_out[...] = coarse * (OMEGA / one[0])
        near = (lambda at: x_out[at, :],) * 2
        channels = []
        for step in (mid.height, 1):
            channels.append([near, (lambda at, s=step: x_out[moved(at, s), :], lambda at, s=step: x_out[moved(at, -s), :])])
        channels.append([near, (lambda at: roll(x_out[at, :], -mid.dup, 1), lambda at: roll(x_out[at, :], mid.dup, 1))])
        fifth_round.emit(0, channels, buffers)

    x_mid, adj_known, adj_factor, *buffers = call(
        residual_kernel,
        (b_fine, x_fine, stencil, one, iterate, active, weights, *fourth_got),
        [out(mid.rows, LANES), out(3, rows, LANES), out(3, rows, LANES)] + fifth_round.buffers(),
        [(1, rows, LANES), (rows // 2, LANES)],
    )
    fifth_got = swap(buffers)

    def lines_kernel(mid_own, mid_side, low_own, low_side, *rest):
        got, windows = rest[:swaps], rest[swaps:]
        for part, window, own, side, ours, theirs in (
            (1, mid_window, mid_own, mid_side, windows[0], windows[1]),
            (2, low_window, low_own, low_side, windows[2], windows[3]),
        ):
            grid, line = window.grid, window.line
            halves = []
            for half in fourth_round.rows(part, 1, got):
                pairs = [unfold(half[k * grid.depth : (k + 1) * grid.depth]) for k in range(3)]
                halves.append(jnp.concatenate(pairs + [half[3 * grid.depth :]]))
            ours[...] = jnp.zeros(ours.shape, F32)
            theirs[...] = jnp.zeros(theirs.shape, F32)
            pairs = [(ours.at[c], own.at[c], c) for c in range(6)] + [(theirs, side, 6)]
            for ref, source, c in pairs:
                for a in range(grid.depth):
                    at = a * line + window.rim
                    ref[at : at + grid.height, :] = source[a * grid.height : (a + 1) * grid.height, :]
                for y, half in zip((-1, grid.height), halves):
                    ref[pl.ds(window.rim + y, grid.depth, stride=line), :] = half[c * grid.depth : (c + 1) * grid.depth]

    mid_lines, low_lines = (mid.depth * mid_window.line, LANES), (low.depth * low_window.line, LANES)
    mid_around, mid_beside, low_around, low_beside = call(
        lines_kernel,
        (mid_couplings, mid_side, low_couplings, low_side, *fourth_got),
        [out(6, *mid_lines), out(*mid_lines), out(6, *low_lines), out(*low_lines)],
    )

    def device(*steps):
        at = [lax.axis_index(name) for name in AXES]
        inside, flat = True, 0
        for position, size, step in zip(at, sizes, steps):
            inside = inside & (position + step >= 0) & (position + step < size)
        for position, size, step in zip(at, sizes, steps):
            flat = flat * size + jnp.where(inside, position + step, position)
        return flat

    last_groups = LANES // last_width
    last = jnp.concatenate([OMEGA / coarse_three[:1], coarse_three[1:]]).reshape(7, last_height, last_width)
    last = jnp.pad(last, ((0, 2 * last_groups - 7), (0, 0), (0, 0)))
    last = last.reshape(2, last_groups, last_height, last_width).transpose(0, 2, 1, 3).reshape(2 * last_height, LANES)
    keep = low.rows // low.dup
    own_at = keep + 2 * last_height
    block = own_at + 2
    signs = (-1, 1)

    def columns(near, far, sign):
        if sign < 0:
            parts = near, roll(far, 2, 1), roll(near, 2, 1)
        else:
            parts = roll(near, 2, 1), roll(far, 4, 1), roll(near, 8, 1)
        lane = lane_of(near)
        return jnp.where(lane < 2, parts[0], jnp.where(lane < 4, parts[1], jnp.where(lane < 6, parts[2], 0.0)))

    def low_kernel(x, one, mid_couplings, two, last, *rest):
        got, (sent, mark, ends, temp) = rest[:swaps], rest[swaps:]
        (rim,) = fifth_round.halos(0, got, ends, [0])
        value = x[...]
        total = (1.0 - OMEGA) * value
        for dim in range(3):
            total = total - mid_couplings[2 * dim] * rim.previous(value, dim)
            total = total - mid_couplings[2 * dim + 1] * rim.following(value, dim)
        residual = total * (one[0] * (1.0 / OMEGA))
        b = pair_sum_rows(pair_sum_x(residual, mid.dup), mid.depth, mid.height, temp)
        field = b * (OMEGA / two[0])
        to_next = [two[2 + 2 * dim] * field for dim in range(3)]
        to_previous = [two[1 + 2 * dim] * field for dim in range(3)]
        closed = Closed(low.height, low.dup)
        inner = (1.0 - OMEGA) * b
        for dim in range(3):
            inner = inner - closed.previous(to_next[dim], dim) - closed.following(to_previous[dim], dim)
        row, lane = lax.broadcasted_iota(jnp.int32, field.shape, 0), lane_of(field)
        layer, y = row // low.height, row % low.height
        outer = [
            jnp.where(layer == 0, -to_previous[0], 0.0),
            jnp.where(layer == low.depth - 1, -to_next[0], 0.0),
            jnp.where(y == 0, -to_previous[1], jnp.where(y == low.height - 1, -to_next[1], 0.0)),
            jnp.where(lane < low.dup, -to_previous[2], jnp.where(lane >= LANES - low.dup, -to_next[2], 0.0)),
        ]
        parts = [pair_sum_rows(pair_sum_x(v, low.dup), low.depth, low.height, temp) for v in [inner] + outer]
        parts = matmul(jnp.concatenate(parts), one_hot((LANES, LANES), lambda i, j: i == 2 * low.dup * j))
        parts = [parts[k * last_height : (k + 1) * last_height] for k in range(5)]
        upper = last[:last_height] + roll(parts[0], 7 * last_width, 1)
        lower = last[last_height:]
        for k in range(4):
            lower = lower + roll(parts[1 + k], k * last_width, 1)
        packed = jnp.zeros((keep, LANES), F32)
        phase = lane_of(packed) % low.dup
        for k in range(low.dup):
            packed = jnp.where(phase == k, field[k * keep : (k + 1) * keep], packed)
        filled = jnp.concatenate([packed, upper, lower, jnp.zeros((2, LANES), F32)])
        sent[...] = jnp.broadcast_to(filled[None], (count, block, LANES))
        mark[...] = filled

        def near(sign, size):
            return 0 if sign < 0 else size - 1

        def line(a, y):
            return x[a * mid.height + y : a * mid.height + y + 1, :]

        def across(a):
            return x[a * mid.height : (a + 1) * mid.height, :]

        def along(y):
            return x[pl.ds(y, mid.depth, stride=mid.height), :]

        def folded(value):
            return sum(roll(value[2 * k : 2 * k + 2], 6 * k, 1) for k in range(value.shape[0] // 2))

        for sz in signs:
            a = near(sz, mid.depth)
            for sy in signs:
                y = near(sy, mid.height)
                pair = fold(jnp.concatenate([line(a, y), line(a - sz, y)]))
                sent[device(0, sy, sz), own_at : own_at + 2, :] = jnp.concatenate([pair, line(a, y - sy)])
                for sx in signs:
                    corner = columns(line(a, y), line(a, y), sx)
                    sent[device(sx, sy, sz), own_at : own_at + 1, :] = corner
            for sx in signs:
                sent[device(sx, 0, sz), own_at : own_at + 2, :] = folded(columns(across(a), across(a - sz), sx))
        for sy in signs:
            y = near(sy, mid.height)
            for sx in signs:
                sent[device(sx, sy, 0), own_at : own_at + 2, :] = folded(columns(along(y), along(y - sy), sx))

    sent, mark = call(
        low_kernel,
        (x_mid, one, mid_couplings, two, last, *fifth_got),
        [out(count, block, LANES), out(block, LANES)],
        [(1, mid.rows, LANES), (mid.rows // 2, LANES)],
    )
    everyone = lax.all_to_all(sent, AXES, 0, 0)

    def late_kernel(mark, adj, couplings, mid_around, mid_beside, low_around, low_beside, *buffers):
        late_round.emit(0, [same(couplings, range(6)) + same(adj, range(3))] * 3, buffers)
        for part, window, ours, theirs in ((1, mid_window, mid_around, mid_beside), (2, low_window, low_around, low_beside)):
            ends = []
            for a in (0, window.grid.depth - 1):
                lines = slice(a * window.line, (a + 1) * window.line)
                parts = [fold(jnp.concatenate([ours[c, lines, :], ours[c + 1, lines, :]])) for c in (0, 2, 4)]
                ends.append(jnp.concatenate(parts + [theirs[lines, :]]))
            late_round.put_rows(part, 0, *ends, buffers)

    buffers = call(
        late_kernel,
        (mark, adj_known, fine_couplings, mid_around, mid_beside, low_around, low_beside),
        late_round.buffers(),
    )
    late_got = swap(buffers)

    def window_kernel(mark, x, *rest):
        got, (x_out,) = rest[:swaps], rest[swaps:]
        x_out[...] = jnp.zeros(x_out.shape, F32)
        near, far = fifth_round.faces(0, got)
        mid_window.fill(x_out.at[0], x[...])
        mid_window.fill(x_out.at[1], beside_of(*near[2]))
        mid_window.fill(x_out.at[2], beside_of(*far[2]))
        for faces, step in ((near, 0), (far, 1)):
            for layer, value in zip((-1 - step, mid.depth + step), faces[0]):
                x_out[0, mid_window.layer(layer), :] = value
            for y, value in zip((-1 - step, mid.height + step), faces[1]):
                x_out[0, mid_window.row(y), :] = value

    (x_windows,) = call(window_kernel, (mark, x_mid, *fifth_got), [out(3, mid_window.rows, LANES)])

    last_rows, last_line = sizes[2] * sizes[1] * last_height, sizes[1] * last_height
    last_base = -(-(last_line + low_window.rim) // 8) * 8

    def solve_last(everyone, temp):
        channels = [[] for _ in range(2 * last_groups)]
        for first in range(0, sizes[0], last_groups):
            here = range(min(last_groups, sizes[0] - first))
            for g in here:
                for y in range(sizes[1]):
                    for z in range(sizes[2]):
                        sender = ((first + g) * sizes[1] + y) * sizes[2] + z
                        for half in range(2):
                            at = half * last_rows + z * last_line + y * last_height
                            start = keep + half * last_height
                            temp[g, at : at + last_height, :] = everyone[sender, start : start + last_height, :]
            parts = [temp[g] for g in here]
            group = lane_of(parts[0]) // last_width
            for q in range(last_groups):
                value = jnp.zeros_like(parts[0])
                for g in here:
                    value = jnp.where(group == g, roll(parts[g], last_width * (g - q), 1), value)
                channels[q].append(value[:last_rows])
                channels[last_groups + q].append(value[last_rows:])
        parts = [jnp.concatenate(tiles, axis=1) for tiles in channels[: last_groups + 4]]
        stencil, (inner, back, on, beside_y, beside_x) = parts[:7], parts[7:]
        y, x = row_y(inner, last_line), lane_of(inner)
        none = jnp.zeros((last_line, inner.shape[1]), F32)
        b = inner + jnp.concatenate([back[last_line:], none]) + jnp.concatenate([none, on[:-last_line]])
        b = b + jnp.where((y % last_height == 0) & (y > 0), roll(beside_y, 1, 0), 0.0)
        b = b + jnp.where((y % last_height == last_height - 1) & (y < last_line - 1), roll(beside_y, -1, 0), 0.0)
        b = b + jnp.where((x % last_width == 0) & (x > 0), roll(beside_x, 1, 1), 0.0)
        b = b + jnp.where((x % last_width == last_width - 1) & (x < inner.shape[1] - 1), roll(beside_x, -1, 1), 0.0)
        closed = Closed(last_line, 1)
        field = start = b * stencil[0]
        for sweep in range(COARSE_SWEEPS - 1):
            field = start + (1.0 - OMEGA) * field - off_apply(stencil, field, closed) * stencil[0]
        return field

    def spread_last(field, temp):
        gx, gy, gz = (lax.axis_index(name) for name in AXES)
        half, reach = low_window.line // 2, low_window.rim // 2
        layers = low.depth // 2 + 2
        dup = 2 * low.dup

        def taken(i, j):
            own = (j < LANES) & (i == gx * last_width + j // dup)
            before = (j >= LANES) & (j < LANES + low.dup) & (i == gx * last_width - 1)
            after = (j >= 2 * LANES - low.dup) & (i == (gx + 1) * last_width)
            return own | before | after

        at = last_base + (gz * (low.depth // 2) - 1) * last_line + gy * last_height - reach
        tiles = []
        for tile in range(0, field.shape[1], LANES):
            temp[...] = jnp.zeros(temp.shape, F32)
            temp[last_base : last_base + last_rows, :] = field[:, tile : tile + LANES]
            tiles.append(jnp.concatenate([temp[pl.ds(at + k * last_line, half), :] for k in range(layers)]))
        both = matmul(jnp.concatenate(tiles, axis=1), one_hot((field.shape[1], 2 * LANES), taken))
        return [spread_rows(both[:, k * LANES : (k + 1) * LANES], layers, half, temp) for k in range(2)]

    def low_windows(everyone, temp, result):
        around = [(sy, sz) for sz in (-1, 0, 1) for sy in (-1, 0, 1)]
        per = -(-len(around) * keep // 8) * 8
        for k, sx in enumerate((0, -1, 1)):
            for i, (sy, sz) in enumerate(around):
                temp[k * per + keep * i : k * per + keep * (i + 1), :] = everyone[device(sx, sy, sz), 0:keep, :]
        packed = temp[: 3 * per, :]
        lane = lane_of(packed)
        turned = {by: roll(packed, by, 1) for by in range(1 - low.dup, low.dup)}
        for k in range(low.dup):
            value = turned[-k]
            for m in range(1, low.dup):
                value = jnp.where(lane % low.dup == m, turned[m - k], value)
            own, before, after = (value[i * per : (i + 1) * per] for i in range(3))
            forms = [own]
            for cells in (1, 2):
                forms.append(beside_of(roll(before, low.dup * cells, 1), roll(after, -low.dup * cells, 1)))
            for i, (sy, sz) in enumerate(around):
                for j in range(keep):
                    a, y = divmod(k * keep + j, low.height)
                    a, y = a + sz * low.depth, y + sy * low.height
                    if -2 <= a < low.depth + 2 and -low_window.rim <= y < low.height + low_window.rim:
                        at = low_window.at(a, y)
                        for form, source in enumerate(forms):
                            result[form, at : at + 1, :] = source[keep * i + j : keep * i + j + 1]
        return [result[form] for form in range(3)]

    def mid_edges(everyone, x):
        def lines(*steps):
            return everyone[device(*steps), own_at : own_at + 2, :]

        def unfolded(value, n):
            return jnp.concatenate([roll(value, -6 * k, 1) for k in range(n // 2)])

        def sides(values, k):
            return beside_of(roll(values[0], -2 * k, 1), roll(values[1], -2 * k - 2, 1))

        for sz in signs:
            a = -1 if sz < 0 else mid.depth
            for sy in signs:
                y = -1 if sy < 0 else mid.height
                got = lines(0, sy, sz)
                pair = unfold(got[:1])
                for layer, at, value in ((a, y, pair[:1]), (a + sz, y, pair[1:]), (a, y + sy, got[1:])):
                    row = mid_window.at(layer, at)
                    x[0, row : row + 1, :] = value
                row = mid_window.at(a, y)
                x[1, row : row + 1, :] = sides([lines(sx, sy, sz)[:1] for sx in signs], 0)
            got = [unfolded(lines(sx, 0, sz), mid.height) for sx in signs]
            x[1, mid_window.layer(a), :] = sides(got, 0)
            x[1, mid_window.layer(a + sz), :] = sides(got, 1)
            x[2, mid_window.layer(a), :] = sides(got, 2)
        for sy in signs:
            y = -1 if sy < 0 else mid.height
            got = [unfolded(lines(sx, sy, 0), mid.depth) for sx in signs]
            x[1, mid_window.row(y), :] = sides(got, 0)
            x[1, mid_window.row(y + sy), :] = sides(got, 1)
            x[2, mid_window.row(y), :] = sides(got, 2)

    def full(part, window, lines, side_lines, got):
        line, none = window.line, jnp.zeros((window.line, LANES), F32)
        ends = late_round.rows(part, 0, got)
        packed = jnp.concatenate([none, ends[0][3 * line :], side_lines[...], ends[1][3 * line :], none])

        def around(c):
            pair = slice(c // 2 * line, (c // 2 + 1) * line)
            own = slice(c % 2 * line, (c % 2 + 1) * line)
            return jnp.concatenate([none, unfold(ends[0][pair])[own], lines[c], unfold(ends[1][pair])[own], none])

        return around, lambda c: unpack_side(packed, c, window.grid.dup)

    def gradient_factors(mobility, pressure, trans, trans_before, *rest):
        got, (inner, layer_out, line_out, side_out, ends) = rest[:swaps], rest[swaps:]
        faces = third_round.faces(0, got, range(4, 8))
        rims = [Rim(fine, f, ends, c) for c, f in enumerate(faces)]
        lines = pl.ds(0, depth, stride=height)
        drops = []
        for dim in range(3):
            drops.append(0.25 * trans[dim] * (pressure[0] - rims[3].following(pressure[0], dim)))
        side_drop = 0.25 * trans_before[2] * (faces[3][2][0] - pressure[0])
        sides = []
        for c in range(3):
            value = mobility[c]
            for dim in range(3):
                inner[3 * dim + c] = drops[dim] * (value + rims[c].following(value, dim))
            drop = 0.25 * trans_before[0, :height, :] * (faces[3][0][0] - pressure[0, :height, :])
            layer_out[c] = drop * (faces[c][0][0] + mobility[c, :height, :])
            drop = 0.25 * trans_before[1, lines, :] * (faces[3][1][0] - pressure[0, lines, :])
            line_out[c] = drop * (faces[c][1][0] + mobility[c, lines, :])
            sides.append(side_drop * (faces[c][2][0] + value))
        side_out[...] = pack_sides(sides, 1)

    gradient_inputs = call(
        gradient_factors,
        (mobility, pressure, trans, trans_before, *third_got),
        [out(9, rows, LANES), out(3, height, LANES), out(3, depth, LANES), out(rows, LANES)],
        [(4, rows, LANES)],
    )

    def final_kernel(
        everyone,
        x_windows,
        mid_around,
        mid_beside,
        low_around,
        low_beside,
        adj_known,
        adj_factor,
        couplings,
        terms,
        layer_terms,
        line_terms,
        side_terms,
        *rest,
    ):
        late_got, third_got, (adj_out, grad_out) = rest[:swaps], rest[swaps : 2 * swaps], rest[2 * swaps : 2 * swaps + 2]
        last_temp, low_x, low_temp, x, temp, ends, around, beside, value_ref, adj, grad, sems = rest[2 * swaps + 2 :]
        x[...] = x_windows[...]
        mid_edges(everyone, x)
        low_values = low_windows(everyone, low_temp, low_x)
        added = spread_last(solve_last(everyone, last_temp), temp)
        pair = full(2, low_window, low_around, low_beside, late_got)
        results = smooth(low_values, added, pair, low_window.line, low.dup)
        inner = slice(low_window.line, (low.depth + 3) * low_window.line)
        added = [spread_rows(v[inner], low.depth + 2, low_window.line, temp) for v in results]
        pair = full(1, mid_window, mid_around, mid_beside, late_got)
        beyond = late_round.faces(0, late_got)
        factors = third_round.faces(0, third_got, range(1, 4))
        around[...], beside[...] = smooth([x[k] for k in range(3)], added, pair, mid_window.line, mid.dup)

        def own(ref):
            lines = [ref[mid_window.layer(a), :] for a in range(mid.depth)]
            return spread_rows(jnp.concatenate(lines), mid.depth, mid.height, temp)

        def layer(ref, a):
            return spread_lines(ref[mid_window.layer(a), :], temp)

        def lines(ref, y):
            return spread_lines(ref[mid_window.row(y), :], temp)

        def one_row(a, y):
            at = mid_window.at(a, y)
            return around[at : at + 1, :]

        value, side = own(around), own(beside)
        value_ref[...] = value
        layers = [(a, layer(around, a), layer(beside, a)) for a in (-1, mid.depth)]
        rows_y = [(y, lines(around, y), lines(beside, y)) for y in (-1, mid.height)]
        rim = Rim(fine, [[v[1] for v in layers], [v[1] for v in rows_y], (side, side)], ends, 0)

        def gain(value, shifts, coupling):
            total = (1.0 - OMEGA) * value
            for k in range(6):
                total = total - coupling(k) * shifts[k]
            return total

        shifts = [shift(value, dim) for dim in range(3) for shift in (rim.previous, rim.following)]
        own_gain = gain(value, shifts, lambda k: couplings[k])
        for c in range(3):
            adj[c] = adj_known[c] + adj_factor[c] * own_gain
        copies = [pltpu.make_async_copy(adj, adj_out, sems.at[3])]
        copies[0].start()

        def along_x(value, side):
            lane = lane_of(value)
            return [jnp.where(lane < 1, side, roll(value, 1, 1)), jnp.where(lane >= LANES - 1, side, roll(value, -1, 1))]

        def ended(value, low, high):
            row = lax.broadcasted_iota(jnp.int32, value.shape, 0)
            n = value.shape[0]
            return [jnp.where(row == 0, low, roll(value, 1, 0)), jnp.where(row == n - 1, high, roll(value, -1, 0))]

        layer_gains, line_gains = [], []
        for k, (a, here, there) in enumerate(layers):
            shifts = [here, value[:height]] if k == 0 else [value[rows - height :], here]
            shifts += ended(here, one_row(a, -1), one_row(a, mid.height)) + along_x(here, there)
            layer_gains.append(gain(here, shifts, lambda c: beyond[c][0][k]))
        for k, (y, here, there) in enumerate(rows_y):
            inside = value_ref[pl.ds(0 if k == 0 else height - 1, depth, stride=height), :]
            shifts = ended(here, one_row(-1, y), one_row(mid.depth, y))
            shifts += ([here, inside] if k == 0 else [inside, here]) + along_x(here, there)
            line_gains.append(gain(here, shifts, lambda c: beyond[c][1][k]))
        lane = lane_of(side)
        side_rim = Rim(fine, [[v[2] for v in layers], [v[2] for v in rows_y], (side, side)], ends, 1)
        shifts = [shift(side, dim) for dim in range(2) for shift in (side_rim.previous, side_rim.following)]
        shifts += [jnp.where(lane < LANES // 2, side, value), jnp.where(lane < LANES // 2, value, side)]
        side_gain = gain(side, shifts, lambda c: beyond[c][2][0])
        adj_rims = []
        for c in range(3):
            known, factor = beyond[6 + c], factors[c]
            faces = [[known[dim][k] + factor[dim][k] * gains[k] for k in range(2)] for dim, gains in enumerate((layer_gains, line_gains))]
            faces.append((known[2][0] + factor[2][0] * side_gain,) * 2)
            adj_rims.append(Rim(fine, faces, ends, 2 + c))
        values = [adj[c] for c in range(3)]
        lines = pl.ds(0, depth, stride=height)
        parts = []
        for c in range(3):
            layer, line, side = (adj_rims[c].faces[dim][0] for dim in range(3))
            parts.append(
                (
                    layer_terms[c] * (layer - values[c][:height]),
                    line_terms[c] * (line - adj[c, lines, :]),
                    unpack_side(side_terms[...], c, 1) * (side - values[c]),
                )
            )
        below = Rim(fine, [(sum(p[dim] for p in parts),) * 2 for dim in range(3)], ends, 5)
        for dim in range(3):
            here = 0.0
            for c in range(3):
                here = here + terms[3 * dim + c] * (values[c] - adj_rims[c].following(values[c], dim))
            grad[dim] = here + below.previous(here, dim)
            copies.append(pltpu.make_async_copy(grad.at[dim], grad_out.at[dim], sems.at[dim]))
            copies[-1].start()
        for copy in copies:
            copy.wait()

    adjoint, gradient = call(
        final_kernel,
        (everyone, x_windows, mid_around, mid_beside, low_around, low_beside)
        + (adj_known, adj_factor, fine_couplings, *gradient_inputs, *late_got, *third_got),
        [out(3, rows, LANES)] * 2,
        [
            (min(sizes[0], last_groups), 2 * last_rows, LANES),
            (3, low_window.rows, LANES),
            (max(low_window.rows, 96, 2 * last_base + last_rows), LANES),
            (3, mid_window.rows, LANES),
            (max(mid_window.rows, 2 * last_base + last_rows), LANES),
            (6, rows, LANES),
            (mid_window.rows, LANES),
            (mid_window.rows, LANES),
            (rows, LANES),
            (3, rows, LANES),
            (3, rows, LANES),
            pltpu.SemaphoreType.DMA((4,)),
        ],
        far_outputs=2,
    )
    shape = (3, depth, height, width)
    return adjoint.reshape(shape), gradient.reshape(shape)


def solution(mesh):
    cells = P("layer", "gy", "gx")
    fields = P(None, "layer", "gy", "gx")
    return jax.shard_map(
        local,
        mesh=mesh,
        in_specs=(
            fields,
            cells,
            fields,
            fields,
            fields,
            fields,
            fields,
            fields,
            fields,
            fields,
            cells,
            fields,
        ),
        out_specs=(fields, fields),
        check_vma=False,
    )
```

```python
import itertools

import jax
import jax.numpy as jnp
from jax import lax
from jax.experimental import pallas as pl
from jax.experimental.pallas import tpu as pltpu
from jax.sharding import PartitionSpec as P

SWEEPS = 3
LEVELS = 3
COARSE_SWEEPS = 4
OMEGA = 0.8
LANES = 128
AXES = ("gx", "gy", "layer")
BY_DIM = ("layer", "gy", "gx")
ORDER = ((0, 1), (0, 0), (1, 1), (1, 0), (2, 1), (2, 0))
F32 = jnp.float32


def pair_route(axis, phase):
    sizes = [lax.axis_size(name) for name in AXES]
    k = AXES.index(axis)
    n = sizes[k]
    route = []
    for index in itertools.product(*[range(size) for size in sizes]):
        target = list(index)
        if phase == 0:
            target[k] = index[k] ^ 1
        elif 0 < index[k] < n - 1 or k == 0:
            target[k] = (((index[k] + 1) % n ^ 1) - 1) % n
        else:
            target[0] = index[0] ^ 1
        flat = [(i[0] * sizes[1] + i[1]) * sizes[2] + i[2] for i in (index, target)]
        route.append(tuple(flat))
    return route


def phases(dim):
    return min(lax.axis_size(BY_DIM[dim]), 3) - 1


def sends(dims=(0, 1, 2)):
    return [(dim, phase) for dim, phase in ORDER if dim in dims and phase < phases(dim)]


def swap(buffers, dims=(0, 1, 2)):
    return [lax.ppermute(b, AXES, pair_route(BY_DIM[dim], phase)) for b, (dim, phase) in zip(buffers, sends(dims))]


class Grid:
    def __init__(self, depth, height, dup):
        self.depth, self.height, self.dup = depth, height, dup
        self.rows = depth * height
        self.width = LANES // dup
        self.groups = self.rows // 8

    def lines(self, dim):
        return (self.height, self.depth)[dim]

    def tiles(self, count):
        return -(-2 * self.dup * count * self.groups // LANES)

    def place(self, c, k):
        return divmod(2 * self.dup * (self.groups * c + k), LANES)


class Message:
    def __init__(self, *parts, dims=(0, 1, 2)):
        self.parts, self.dims = parts, dims

    def size(self, part, dim):
        part = self.parts[part]
        if isinstance(part, dict):
            return part.get(dim, 0)
        if dim not in part[2:] and len(part) > 2:
            return 0
        return part[0].tiles(part[1]) * 8 if dim == 2 else part[1] * part[0].lines(dim)

    def start(self, part, dim):
        return sum(self.size(i, dim) for i in range(part))

    def buffers(self):
        return [jax.ShapeDtypeStruct((self.start(len(self.parts), dim), LANES), F32) for dim, phase in sends(self.dims)]

    def put(self, dim, rows, first, last, out):
        if phases(dim) == 0:
            return
        out = dict(zip(sends(self.dims), out))
        even = lax.axis_index(BY_DIM[dim]) % 2 == 0
        out[dim, 0][rows] = last if first is last else jnp.where(even, last, first)
        if phases(dim) == 2:
            out[dim, 1][rows] = last if first is last else jnp.where(even, first, last)

    def put_rows(self, part, dim, first, last, out):
        start = self.start(part, dim)
        self.put(dim, slice(start, start + self.size(part, dim)), first, last, out)

    def emit(self, part, channels, out):
        grid = self.parts[part][0]
        lane = lax.broadcasted_iota(jnp.int32, (8, LANES), 1)
        for dim in range(3):
            if self.size(part, dim) == 0:
                continue
            start = self.start(part, dim)
            if dim == 2:
                count, dup = self.parts[part][1], grid.dup
                tiles = [jnp.zeros((8, LANES), F32)] * grid.tiles(count)
                for c, (first, last) in enumerate(channels[dim]):
                    for k in range(grid.groups):
                        tile, at = grid.place(c, k)
                        rows = slice(8 * k, 8 * k + 8)
                        value = last(rows)
                        if first is not last:
                            value = jnp.where(lane < dup, first(rows), value)
                        here = (lane >= at) & (lane < at + 2 * dup)
                        tiles[tile] = jnp.where(here, roll(value, at + dup, 1), tiles[tile])
                value = jnp.concatenate(tiles)
                self.put(dim, slice(start, start + 8 * len(tiles)), value, value, out)
                continue
            if dim == 0:
                low, high = slice(0, grid.height), slice(grid.rows - grid.height, grid.rows)
            else:
                low, high = (pl.ds(s, grid.depth, stride=grid.height) for s in (0, grid.height - 1))
            n = grid.lines(dim)
            for c, (first, last) in enumerate(channels[dim]):
                self.put(dim, slice(start + c * n, start + (c + 1) * n), first(low), last(high), out)

    def both(self, dim, rows, got):
        if phases(dim) == 0:
            return (jnp.zeros((rows.stop - rows.start, LANES), F32),) * 2
        got = dict(zip(sends(self.dims), got))
        me, n = lax.axis_index(BY_DIM[dim]), lax.axis_size(BY_DIM[dim])
        even = me % 2 == 0
        one = got[dim, 0][rows]
        if phases(dim) == 1:
            return jnp.where(even, 0.0, one), jnp.where(even, one, 0.0)
        two = got[dim, 1][rows]
        before, after = jnp.where(even, two, one), jnp.where(even, one, two)
        return jnp.where(me > 0, before, 0.0), jnp.where(me < n - 1, after, 0.0)

    def rows(self, part, dim, got):
        start = self.start(part, dim)
        return self.both(dim, slice(start, start + self.size(part, dim)), got)

    def faces(self, part, got, channels=None):
        grid, count = self.parts[part][:2]
        channels = range(count) if channels is None else channels
        result = [[None] * 3 for _ in channels]
        for dim in range(3):
            if self.size(part, dim) == 0:
                continue
            start = self.start(part, dim)
            if dim == 2:
                dup = grid.dup
                merged = self.sides(part, got)
                for i, c in enumerate(channels):
                    pieces = []
                    for k in range(grid.groups):
                        tile, at = grid.place(c, k)
                        pieces.append(roll(merged[8 * tile : 8 * tile + 8], -at - dup, 1))
                    result[i][dim] = (jnp.concatenate(pieces),) * 2
            else:
                size = grid.lines(dim)
                for i, c in enumerate(channels):
                    result[i][dim] = self.both(dim, slice(start + c * size, start + (c + 1) * size), got)
        return result

    def sides(self, part, got):
        grid, count = self.parts[part][:2]
        start, dup = self.start(part, 2), grid.dup
        before, after = self.both(2, slice(start, start + 8 * grid.tiles(count)), got)
        return jnp.where(lane_of(before) % (2 * dup) < dup, roll(after, -dup, 1), roll(before, dup, 1))

    def columns(self, part, got, channels=None):
        grid, count = self.parts[part][:2]
        merged = self.sides(part, got)
        places = [grid.place(c, 0) for c in (range(count) if channels is None else channels)]
        return [roll(merged[8 * tile : 8 * tile + 8], -at, 1) for tile, at in places]

    def halos(self, part, got, scratch, channels=None):
        return [Rim(self.parts[part][0], r, scratch, c) for c, r in enumerate(self.faces(part, got, channels))]


class Window:
    def __init__(self, grid, rim):
        self.grid, self.rim = grid, rim
        self.line = grid.height + 2 * rim
        self.rows = (grid.depth + 4) * self.line

    def at(self, layer, y):
        return (layer + 2) * self.line + self.rim + y

    def layer(self, layer):
        return slice(self.at(layer, 0), self.at(layer, self.grid.height))

    def row(self, y):
        return pl.ds(self.at(0, y), self.grid.depth, stride=self.line)

    def fill(self, ref, own):
        height = self.grid.height
        for a in range(self.grid.depth):
            ref[self.layer(a), :] = own[a * height : (a + 1) * height]


class Rim:
    def __init__(self, grid, faces, scratch, c):
        self.grid, self.faces = grid, faces
        ends = scratch.at[c]
        ends[pl.ds(0, grid.depth, stride=grid.height), :] = faces[1][0]
        ends[pl.ds(grid.height - 1, grid.depth, stride=grid.height), :] = faces[1][1]
        self.y_ends = ends[...]

    def previous(self, value, dim):
        g = self.grid
        if dim == 0:
            return jnp.concatenate([self.faces[0][0], value[: g.rows - g.height]])
        if dim == 1:
            return jnp.where(row_y(value, g.height) == 0, self.y_ends, roll(value, 1, 0))
        return jnp.where(lane_of(value) < g.dup, self.faces[2][0], roll(value, g.dup, 1))

    def following(self, value, dim):
        g = self.grid
        if dim == 0:
            return jnp.concatenate([value[g.height :], self.faces[0][1]])
        if dim == 1:
            return jnp.where(row_y(value, g.height) == g.height - 1, self.y_ends, roll(value, -1, 0))
        return jnp.where(lane_of(value) >= value.shape[1] - g.dup, self.faces[2][1], roll(value, -g.dup, 1))


class Closed:
    def __init__(self, height, dup):
        self.height, self.dup = height, dup

    def previous(self, value, dim):
        if dim == 0:
            return jnp.concatenate([jnp.zeros_like(value[: self.height]), value[: -self.height]])
        if dim == 1:
            return jnp.where(row_y(value, self.height) == 0, 0.0, roll(value, 1, 0))
        return jnp.where(lane_of(value) < self.dup, 0.0, roll(value, self.dup, 1))

    def following(self, value, dim):
        if dim == 0:
            return jnp.concatenate([value[self.height :], jnp.zeros_like(value[: self.height])])
        if dim == 1:
            return jnp.where(row_y(value, self.height) == self.height - 1, 0.0, roll(value, -1, 0))
        return jnp.where(lane_of(value) >= value.shape[1] - self.dup, 0.0, roll(value, -self.dup, 1))


def roll(value, shift, axis):
    shift %= value.shape[axis]
    return pltpu.roll(value, shift, axis) if shift else value


def row_y(value, height):
    return lax.broadcasted_iota(jnp.int32, value.shape, 0) % height


def lane_of(value):
    return lax.broadcasted_iota(jnp.int32, value.shape, 1)


def loader(ref, c):
    return lambda rows: ref[c, rows, :]


def product(coefs, k, ref):
    return lambda rows: coefs[k, rows, :] * ref[rows, :]


def off_apply(stencil, field, rim):
    total = 0.0
    for dim in range(3):
        total = total + rim.previous(stencil[2 + 2 * dim] * field, dim)
        total = total + rim.following(stencil[1 + 2 * dim] * field, dim)
    return total


def block_row(blocks, c, values):
    return blocks[c] * values[0] + blocks[3 + c] * values[1] + blocks[6 + c] * values[2]


def system_row(c, values, rim, blocks, trans, trans_before):
    total = block_row(blocks, c, values)
    v = values[c]
    for dim in range(3):
        total = total + trans[dim] * (v - rim.following(v, dim))
        total = total + trans_before[dim] * (v - rim.previous(v, dim))
    return total


def pair_sum_x(value, dup):
    odd = (lane_of(value) // dup) % 2 == 1
    return value + jnp.where(odd, roll(value, dup, 1), roll(value, -dup, 1))


def pair_sum_rows(value, depth, height, scratch):
    half = depth // 2
    parts = [value[2 * a * height : (2 * a + 1) * height] + value[(2 * a + 1) * height : (2 * a + 2) * height] for a in range(half)]
    whole = jnp.concatenate(parts)
    count = half * height // 2
    sums = []
    for at in range(0, whole.shape[1], LANES):
        scratch[: half * height, :] = whole[:, at : at + LANES]
        sums.append(scratch[pl.ds(0, count, stride=2), :] + scratch[pl.ds(1, count, stride=2), :])
    return jnp.concatenate(sums, axis=1)


def spread_rows(value, depth, height, scratch):
    count = depth * height
    tiles = []
    for at in range(0, value.shape[1], LANES):
        scratch[pl.ds(0, count, stride=2), :] = value[:, at : at + LANES]
        scratch[pl.ds(1, count, stride=2), :] = value[:, at : at + LANES]
        wide = scratch[: 2 * count, :]
        tiles.append(jnp.concatenate([wide[2 * height * (a // 2) : 2 * height * (a // 2 + 1)] for a in range(2 * depth)]))
    return jnp.concatenate(tiles, axis=1)


def spread_lines(value, scratch):
    count = value.shape[0]
    scratch[pl.ds(0, count, stride=2), :] = value
    scratch[pl.ds(1, count, stride=2), :] = value
    return scratch[: 2 * count, :]


def fold(value):
    half = value.shape[0] // 2
    return jnp.where(lane_of(value[:half]) % 2 == 0, value[:half], value[half:])


def unfold(value):
    even = lane_of(value) % 2 == 0
    return jnp.concatenate([jnp.where(even, value, roll(value, 1, 1)), jnp.where(even, roll(value, -1, 1), value)])


def beside_of(before, after):
    if before is after:
        return before
    return jnp.where(lane_of(before) < LANES // 2, before, after)


def pack_sides(values, dup):
    total = jnp.zeros_like(values[0])
    lane = lane_of(total)
    for c, value in enumerate(values):
        total = jnp.where((lane >= dup * c) & (lane < dup * (c + 1)), roll(value, dup * c, 1), total)
        high = LANES - dup * c
        total = jnp.where((lane >= high - dup) & (lane < high), roll(value, -dup * c, 1), total)
    return total


def unpack_side(value, c, dup):
    return beside_of(roll(value, -dup * c, 1), roll(value, dup * c, 1))


def pack_column(value):
    tile = jnp.zeros((8, LANES), F32)
    lane = lane_of(tile)
    for k in range(value.shape[0] // 8):
        tile = jnp.where((lane >= 2 * k) & (lane < 2 * k + 2), roll(value[8 * k : 8 * k + 8], 2 * k + 1, 1), tile)
    return tile


def unpack_column(tile, rows):
    return jnp.concatenate([roll(tile, -2 * k - 1, 1) for k in range(rows // 8)])


def column_ends(value, per, last):
    step = per - 1 if last else 1
    turned = pltpu.roll(value, step, 1, stride=per, stride_axis=0)
    lane, row = lane_of(value), lax.broadcasted_iota(jnp.int32, value.shape, 0)
    here = (lane // per == row) & (lane % per >= per - 2 if last else lane % per < 2)
    return jnp.sum(jnp.where(here, turned, 0.0), axis=0, keepdims=True)


def moved(rows, by):
    if isinstance(rows, slice):
        return slice(rows.start + by, rows.stop + by)
    return pl.ds(rows.start + by, rows.size, stride=rows.stride)


def shifts_of(value, inner, outer, line, dup, beside):
    none = jnp.zeros((line, LANES), F32)
    lane = lane_of(value)
    if beside:
        low, high = jnp.where(lane < LANES // 2, outer, inner), jnp.where(lane < LANES // 2, inner, outer)
    else:
        low, high = jnp.where(lane < dup, outer, roll(value, dup, 1)), jnp.where(lane >= LANES - dup, outer, roll(value, -dup, 1))
    return [
        jnp.concatenate([none, value[:-line]]),
        jnp.concatenate([value[line:], none]),
        roll(value, 1, 0),
        roll(value, -1, 0),
        low,
        high,
    ]


def smooth(x, added, couplings, line, dup):
    around, beside, second = x[0] + added[0], x[1] + added[1], x[2] + added[1]
    results = []
    for k, (value, shifts) in enumerate(
        (
            (around, shifts_of(around, None, beside, line, dup, False)),
            (beside, shifts_of(beside, around, second, line, dup, True)),
        )
    ):
        total = x[k] + (1.0 - OMEGA) * value
        for c in range(6):
            total = total - couplings[k](c) * shifts[c]
        results.append(total)
    return results


def one_hot(shape, hit):
    return jnp.where(hit(lax.broadcasted_iota(jnp.int32, shape, 0), lax.broadcasted_iota(jnp.int32, shape, 1)), 1.0, 0.0).astype(F32)


def matmul(values, ones):
    n = values.shape[0]
    extra = -n % 16
    if extra:
        values = jnp.concatenate([values, jnp.zeros((extra, values.shape[1]), F32)])
    parts = []
    for _ in range(3):
        parts.append(values.astype(jnp.bfloat16))
        values = values - parts[-1].astype(F32)
    product = jnp.dot(jnp.concatenate(parts), ones.astype(jnp.bfloat16), preferred_element_type=F32)
    step = n + extra
    return (product[2 * step : 2 * step + n] + product[step : step + n]) + product[:n]


def call(kernel, inputs, outputs, scratch=(), far_inputs=0, far_outputs=0):
    inputs = list(inputs)
    for i in range(far_inputs):
        inputs[i] = pltpu.with_memory_space_constraint(inputs[i], pltpu.HBM)

    def specs(count, far):
        return [pl.BlockSpec(memory_space=pltpu.HBM if i < far else pltpu.VMEM) for i in range(count)]

    return pl.pallas_call(
        kernel,
        out_shape=list(outputs),
        in_specs=specs(len(inputs), far_inputs),
        out_specs=specs(len(outputs), far_outputs),
        scratch_shapes=[pltpu.VMEM(shape, F32) if isinstance(shape, tuple) else shape for shape in scratch],
        compiler_params=pltpu.CompilerParams(vmem_limit_bytes=24 * 2**20),
    )(*inputs)


def local(
    source,
    active_cells,
    diag_blocks,
    frozen_inverses,
    transmissibility,
    pressure_weights,
    stencil_fine,
    coarse_one,
    coarse_two,
    coarse_three,
    pressure_state,
    mobilities,
):
    depth, height, width = active_cells.shape
    low_depth, low_height, low_width = coarse_two.shape[1:]
    last_height, last_width = coarse_three.shape[2:]
    fine = Grid(depth, height, 1)
    mid = Grid(depth // 2, height // 2, 2)
    low = Grid(low_depth, low_height, 4)
    mid_window, low_window = Window(mid, 4), Window(low, 2)
    sizes = [lax.axis_size(name) for name in AXES]
    count = sizes[0] * sizes[1] * sizes[2]
    swaps = len(sends())
    rows = fine.rows
    first_round = Message((fine, 4), (mid, 1), (low, 1))
    second_round = Message((fine, 4))
    third_round = Message((fine, 8), (mid, 6, 2), (low, 6, 2))
    fourth_round = Message((fine, 1), {1: 4 * mid.depth}, {1: 4 * low.depth}, (fine, 6, 2), {2: 2 * depth})
    fifth_round = Message((mid, 2), (fine, 3, 2), {1: 2 * depth}, {2: 2 * depth})
    late_round = Message((fine, 9, 0, 1), {0: 4 * mid_window.line}, {0: 4 * low_window.line}, dims=(0, 1))
    late = len(sends((0, 1)))

    def flat(array):
        return array.reshape(array.shape[:-3] + (rows, width))

    def out(*shape):
        return jax.ShapeDtypeStruct(shape, F32)

    source, active, diag, frozen, trans, weights, stencil, pressure, mobility = (
        flat(a)
        for a in (
            source,
            active_cells,
            diag_blocks,
            frozen_inverses,
            transmissibility,
            pressure_weights,
            stencil_fine,
            pressure_state,
            mobilities,
        )
    )
    pressure = pressure[None]

    def coupling_faces(coefs):
        return [[(loader(coefs, 1 + 2 * dim), loader(coefs, 2 + 2 * dim))] for dim in range(3)]

    def widen(values, dup):
        wide = matmul(values, one_hot((values.shape[1], LANES), lambda i, j: i == j // dup))
        return wide.reshape(7, wide.shape[0] // 7, LANES)

    def start_kernel(source, active, frozen, trans, one, two, rhs_out, it_out, frozen_out, trans_out, one_out, two_out, *rest):
        buffers, (source_in, active_in, one_in, two_in, two_flat, sems) = rest[:-6], rest[-6:]
        order = [k for c in range(3) for k in (c, 3 + c, 6 + c)]
        pairs = [(active, active_in), (source, source_in)] + [(frozen.at[k], frozen_out.at[k]) for k in order]
        pairs += [(trans, trans_out), (one, one_in), (two, two_in)]
        copies = [pltpu.make_async_copy(a, b, sems.at[i]) for i, (a, b) in enumerate(pairs)]
        for copy in copies[-2:] + copies[:-2]:
            copy.start()
        copies[-2].wait()
        copies[-1].wait()
        one_out[...] = widen(one_in[...].reshape(7 * mid.rows, mid.width), mid.dup)
        for c in range(7):
            for a in range(low.depth):
                at = c * low.rows + a * low.height
                two_flat[at : at + low.height, :] = two_in[c, a]
        two_out[...] = widen(two_flat[...], low.dup)
        first_round.emit(1, coupling_faces(one_out), buffers)
        first_round.emit(2, coupling_faces(two_out), buffers)
        copies[0].wait()
        mask = active_in[...].astype(F32)
        copies[1].wait()
        rhs = [source_in[c] * mask for c in range(3)]
        for c in range(3):
            rhs_out[c] = rhs[c]
        for c in range(3):
            for copy in copies[2 + 3 * c : 5 + 3 * c]:
                copy.wait()
            it_out[c] = block_row(frozen_out, c, rhs)
        copies[-3].wait()
        its = [(loader(it_out, c),) * 2 for c in range(3)]
        first_round.emit(0, [its + [(loader(trans_out, dim),) * 2] for dim in range(3)], buffers)

    rhs, iterate, frozen, trans, one, two, *buffers = call(
        start_kernel,
        (source, active, frozen, trans, coarse_one.reshape(7, mid.rows, mid.width), coarse_two),
        [out(3, rows, LANES)] * 2
        + [out(9, rows, LANES), out(3, rows, LANES), out(7, mid.rows, LANES), out(7, low.rows, LANES)]
        + first_round.buffers(),
        [
            (3, rows, LANES),
            pltpu.VMEM((rows, LANES), jnp.int32),
            (7, mid.rows, mid.width),
            (7, low.depth, low.height, low.width),
            (7 * low.rows, low.width),
            pltpu.SemaphoreType.DMA((14,)),
        ],
        far_inputs=6,
    )
    got = swap(buffers)

    def couplings(coefs, rim, result):
        scale = OMEGA / coefs[0]
        for dim in range(3):
            result[2 * dim] = scale * rim.previous(coefs[2 + 2 * dim], dim)
            result[2 * dim + 1] = scale * rim.following(coefs[1 + 2 * dim], dim)

    def coarse_couplings(mobility, one, two, *rest):
        got, outs, mobility_out, scratch = rest[:swaps], rest[swaps : swaps + 2], rest[swaps + 2], rest[swaps + 3 :]
        fetch = pltpu.make_async_copy(mobility, mobility_out, scratch[2])
        fetch.start()
        for part, coefs, result, ends in ((1, one, outs[0], scratch[0]), (2, two, outs[1], scratch[1])):
            couplings(coefs, first_round.halos(part, got, ends)[0], result)
        fetch.wait()

    mid_couplings, low_couplings, mobility_near = call(
        coarse_couplings,
        (mobility, one, two, *got),
        [out(6, mid.rows, LANES), out(6, low.rows, LANES), out(3, rows, LANES)],
        [(1, mid.rows, LANES), (1, low.rows, LANES), pltpu.SemaphoreType.DMA],
        far_inputs=1,
    )

    def sweep_one(rhs, it, frozen, diag, trans, stencil, *rest):
        got, (it_out, before_out), buffers, ends = rest[:swaps], rest[swaps : swaps + 2], rest[swaps + 2 : -1], rest[-1]
        rims = first_round.halos(0, got, ends)
        trans_before = [rims[3].previous(trans[dim], dim) for dim in range(3)]
        values = [it[c] for c in range(3)]
        rest = [rhs[c] - system_row(c, values, rims[c], diag, trans, trans_before) for c in range(3)]
        for c in range(3):
            before_out[c] = trans_before[c]
            it_out[c] = values[c] + block_row(frozen, c, rest)
        channels = [(loader(it_out, c),) * 2 for c in range(3)]
        second_round.emit(0, [channels + faces for faces in coupling_faces(stencil)], buffers)

    iterate, trans_before, *buffers = call(
        sweep_one,
        (rhs, iterate, frozen, diag, trans, stencil, *got),
        [out(3, rows, LANES)] * 2 + second_round.buffers(),
        [(4, rows, LANES)],
    )
    second_got = swap(buffers)

    def same(ref, channels):
        return [(loader(ref, c),) * 2 for c in channels]

    def sweep_two(
        rhs, it, frozen, diag, trans, trans_before, active, weights, mobility, pressure, mid_couplings, low_couplings, *rest
    ):
        got, it_out, buffers, ends = rest[:swaps], rest[swaps], rest[swaps + 1 : -1], rest[-1]
        rims = second_round.halos(0, got, ends, range(3))
        values = [it[c] for c in range(3)]
        rest = [rhs[c] - system_row(c, values, rims[c], diag, trans, trans_before) for c in range(3)]
        for c in range(3):
            it_out[c] = values[c] + block_row(frozen, c, rest)
        factors = [(lambda at, c=c: active[at, :].astype(F32) * weights[c, at, :],) * 2 for c in range(3)]
        states = same(mobility, range(3)) + same(pressure, range(1))
        third_round.emit(0, [same(it_out, range(1)) + factors + states] * 3, buffers)
        third_round.emit(1, [same(mid_couplings, range(6))] * 3, buffers)
        third_round.emit(2, [same(low_couplings, range(6))] * 3, buffers)

    iterate, *buffers = call(
        sweep_two,
        (rhs, iterate, frozen, diag, trans, trans_before, active, weights, mobility_near, pressure)
        + (mid_couplings, low_couplings, *second_got),
        [out(3, rows, LANES)] + third_round.buffers(),
        [(3, rows, LANES)],
    )
    third_got = swap(buffers)

    def fine_kernel(stencil, *rest):
        got, (result, ends) = rest[:swaps], rest[swaps:]
        couplings(stencil, second_round.halos(0, got, ends, [3])[0], result)

    (fine_couplings,) = call(fine_kernel, (stencil, *second_got), [out(6, rows, LANES)], [(1, rows, LANES)])

    def products(coefs, field):
        return [[(product(coefs, 1 + 2 * dim, field), product(coefs, 2 + 2 * dim, field))] for dim in range(3)]

    def pressure_kernel(rhs, it, diag, trans, trans_before, stencil, fine_couplings, mid_couplings, low_couplings, *rest):
        got, (b_out, x_out, mid_side, low_side), buffers = rest[:swaps], rest[swaps : swaps + 4], rest[swaps + 4 : -1]
        (rim,) = third_round.halos(0, got, rest[-1], [0])
        b = rhs[0] - system_row(0, [it[c] for c in range(3)], rim, diag, trans, trans_before)
        b_out[...] = b
        x_out[...] = b * (OMEGA / stencil[0])
        fourth_round.emit(0, products(stencil, x_out), buffers)
        fourth_round.emit(3, [same(fine_couplings, range(6))] * 3, buffers)
        for part, grid, values, side in ((1, mid, mid_couplings, mid_side), (2, low, low_couplings, low_side)):
            side[...] = pack_sides([beside_of(*faces[2]) for faces in third_round.faces(part, got)], grid.dup)
            ends = []
            for y in (0, grid.height - 1):
                lines = pl.ds(y, grid.depth, stride=grid.height)
                parts = [fold(jnp.concatenate([values[c, lines, :], values[c + 1, lines, :]])) for c in (0, 2, 4)]
                ends.append(jnp.concatenate(parts + [side[lines, :]]))
            fourth_round.put_rows(part, 1, *ends, buffers)

    b_fine, x_fine, mid_side, low_side, *buffers = call(
        pressure_kernel,
        (rhs, iterate, diag, trans, trans_before, stencil, fine_couplings, mid_couplings, low_couplings, *third_got),
        [out(rows, LANES)] * 2 + [out(mid.rows, LANES), out(low.rows, LANES)] + fourth_round.buffers(),
        [(1, rows, LANES)],
    )
    fourth_got = swap(buffers)

    def residual_kernel(b, x, stencil, one, it, active, weights, *rest):
        got, (x_out, adj_out, factor_out), buffers = rest[:swaps], rest[swaps : swaps + 3], rest[swaps + 3 : -2]
        ends, temp = rest[-2:]
        (rim,) = fourth_round.halos(0, got, ends, [0])
        off = off_apply(stencil, x[...], rim)
        residual = (1.0 - OMEGA) * b[...] - off
        q = (1.0 - OMEGA) * x[...] + (b[...] - off) * (OMEGA / stencil[0])
        mask = active[...].astype(F32)
        for c in range(3):
            factor = mask * weights[c]
            factor_out[c] = factor
            adj_out[c] = mask * it[c] + factor * q
        coarse = pair_sum_rows(pair_sum_x(residual, 1), depth, height, temp)
        x_out[...] = coarse * (OMEGA / one[0])
        near = (lambda at: x_out[at, :],) * 2
        channels = []
        for step in (mid.height, 1):
            channels.append([near, (lambda at, s=step: x_out[moved(at, s), :], lambda at, s=step: x_out[moved(at, -s), :])])
        channels.append([near, (lambda at: roll(x_out[at, :], -mid.dup, 1), lambda at: roll(x_out[at, :], mid.dup, 1))])
        fifth_round.emit(0, channels, buffers)
        fifth_round.emit(1, [same(adj_out, range(3))] * 3, buffers)

    x_mid, adj_known, adj_factor, *buffers = call(
        residual_kernel,
        (b_fine, x_fine, stencil, one, iterate, active, weights, *fourth_got),
        [out(mid.rows, LANES), out(3, rows, LANES), out(3, rows, LANES)] + fifth_round.buffers(),
        [(1, rows, LANES), (rows // 2, LANES)],
    )
    fifth_got = swap(buffers)

    def lines_kernel(mid_own, mid_side, low_own, low_side, *rest):
        got, windows = rest[:swaps], rest[swaps:]
        for part, window, own, side, ours, theirs in (
            (1, mid_window, mid_own, mid_side, windows[0], windows[1]),
            (2, low_window, low_own, low_side, windows[2], windows[3]),
        ):
            grid, line = window.grid, window.line
            halves = []
            for half in fourth_round.rows(part, 1, got):
                pairs = [unfold(half[k * grid.depth : (k + 1) * grid.depth]) for k in range(3)]
                halves.append(jnp.concatenate(pairs + [half[3 * grid.depth :]]))
            ours[...] = jnp.zeros(ours.shape, F32)
            theirs[...] = jnp.zeros(theirs.shape, F32)
            pairs = [(ours.at[c], own.at[c], c) for c in range(6)] + [(theirs, side, 6)]
            for ref, source, c in pairs:
                for a in range(grid.depth):
                    at = a * line + window.rim
                    ref[at : at + grid.height, :] = source[a * grid.height : (a + 1) * grid.height, :]
                for y, half in zip((-1, grid.height), halves):
                    ref[pl.ds(window.rim + y, grid.depth, stride=line), :] = half[c * grid.depth : (c + 1) * grid.depth]

    mid_lines, low_lines = (mid.depth * mid_window.line, LANES), (low.depth * low_window.line, LANES)
    mid_around, mid_beside, low_around, low_beside = call(
        lines_kernel,
        (mid_couplings, mid_side, low_couplings, low_side, *fourth_got),
        [out(6, *mid_lines), out(*mid_lines), out(6, *low_lines), out(*low_lines)],
    )

    def device(*steps):
        at = [lax.axis_index(name) for name in AXES]
        inside, flat = True, 0
        for position, size, step in zip(at, sizes, steps):
            inside = inside & (position + step >= 0) & (position + step < size)
        for position, size, step in zip(at, sizes, steps):
            flat = flat * size + jnp.where(inside, position + step, position)
        return flat

    last_groups = LANES // last_width
    last = jnp.concatenate([OMEGA / coarse_three[:1], coarse_three[1:]]).reshape(7, last_height, last_width)
    last = jnp.pad(last, ((0, 2 * last_groups - 7), (0, 0), (0, 0)))
    last = last.reshape(2, last_groups, last_height, last_width).transpose(0, 2, 1, 3).reshape(2 * last_height, LANES)
    keep = low.rows // low.dup
    own_at = keep + 2 * last_height
    block = own_at + 2
    signs = (-1, 1)

    def columns(near, far, sign):
        if sign < 0:
            parts = near, roll(far, 2, 1), roll(near, 2, 1)
        else:
            parts = roll(near, 2, 1), roll(far, 4, 1), roll(near, 8, 1)
        lane = lane_of(near)
        return jnp.where(lane < 2, parts[0], jnp.where(lane < 4, parts[1], jnp.where(lane < 6, parts[2], 0.0)))

    def low_kernel(x, one, mid_couplings, two, last, *rest):
        got, (sent, mark, ends, temp) = rest[:swaps], rest[swaps:]
        (rim,) = fifth_round.halos(0, got, ends, [0])
        value = x[...]
        total = (1.0 - OMEGA) * value
        for dim in range(3):
            total = total - mid_couplings[2 * dim] * rim.previous(value, dim)
            total = total - mid_couplings[2 * dim + 1] * rim.following(value, dim)
        residual = total * (one[0] * (1.0 / OMEGA))
        b = pair_sum_rows(pair_sum_x(residual, mid.dup), mid.depth, mid.height, temp.at[0])
        field = b * (OMEGA / two[0])
        to_next = [two[2 + 2 * dim] * field for dim in range(3)]
        to_previous = [two[1 + 2 * dim] * field for dim in range(3)]
        closed = Closed(low.height, low.dup)
        inner = (1.0 - OMEGA) * b
        for dim in range(3):
            inner = inner - closed.previous(to_next[dim], dim) - closed.following(to_previous[dim], dim)
        row, lane = lax.broadcasted_iota(jnp.int32, field.shape, 0), lane_of(field)
        layer, y = row // low.height, row % low.height
        outer = [
            jnp.where(layer == 0, -to_previous[0], 0.0),
            jnp.where(layer == low.depth - 1, -to_next[0], 0.0),
            jnp.where(y == 0, -to_previous[1], jnp.where(y == low.height - 1, -to_next[1], 0.0)),
            jnp.where(lane < low.dup, -to_previous[2], jnp.where(lane >= LANES - low.dup, -to_next[2], 0.0)),
        ]
        parts = [inner] + outer
        parts = [pair_sum_rows(pair_sum_x(v, low.dup), low.depth, low.height, temp.at[1 + k]) for k, v in enumerate(parts)]
        parts = matmul(jnp.concatenate(parts), one_hot((LANES, LANES), lambda i, j: i == 2 * low.dup * j))
        parts = [parts[k * last_height : (k + 1) * last_height] for k in range(5)]
        upper = last[:last_height] + roll(parts[0], 7 * last_width, 1)
        lower = last[last_height:]
        for k in range(4):
            lower = lower + roll(parts[1 + k], k * last_width, 1)
        packed = jnp.zeros((keep, LANES), F32)
        phase = lane_of(packed) % low.dup
        for k in range(low.dup):
            packed = jnp.where(phase == k, field[k * keep : (k + 1) * keep], packed)
        filled = jnp.concatenate([packed, upper, lower, jnp.zeros((2, LANES), F32)])
        sent[...] = jnp.broadcast_to(filled[None], (count, block, LANES))
        mark[...] = filled

        def near(sign, size):
            return 0 if sign < 0 else size - 1

        def line(a, y):
            return x[a * mid.height + y : a * mid.height + y + 1, :]

        def across(a):
            return x[a * mid.height : (a + 1) * mid.height, :]

        def along(y):
            return x[pl.ds(y, mid.depth, stride=mid.height), :]

        def folded(value):
            return sum(roll(value[2 * k : 2 * k + 2], 6 * k, 1) for k in range(value.shape[0] // 2))

        for sz in signs:
            a = near(sz, mid.depth)
            for sy in signs:
                y = near(sy, mid.height)
                pair = fold(jnp.concatenate([line(a, y), line(a - sz, y)]))
                sent[device(0, sy, sz), own_at : own_at + 2, :] = jnp.concatenate([pair, line(a, y - sy)])
                for sx in signs:
                    corner = columns(line(a, y), line(a, y), sx)
                    sent[device(sx, sy, sz), own_at : own_at + 1, :] = corner
            for sx in signs:
                sent[device(sx, 0, sz), own_at : own_at + 2, :] = folded(columns(across(a), across(a - sz), sx))
        for sy in signs:
            y = near(sy, mid.height)
            for sx in signs:
                sent[device(sx, sy, 0), own_at : own_at + 2, :] = folded(columns(along(y), along(y - sy), sx))

    sent, mark = call(
        low_kernel,
        (x_mid, one, mid_couplings, two, last, *fifth_got),
        [out(count, block, LANES), out(block, LANES)],
        [(1, mid.rows, LANES), (6, mid.rows // 2, LANES)],
    )
    everyone = lax.all_to_all(sent, AXES, 0, 0)

    def late_kernel(mark, adj, couplings, mid_around, mid_beside, low_around, low_beside, *buffers):
        late_round.emit(0, [same(couplings, range(6)) + same(adj, range(3))] * 3, buffers)
        for part, window, ours, theirs in ((1, mid_window, mid_around, mid_beside), (2, low_window, low_around, low_beside)):
            ends = []
            for a in (0, window.grid.depth - 1):
                lines = slice(a * window.line, (a + 1) * window.line)
                parts = [fold(jnp.concatenate([ours[c, lines, :], ours[c + 1, lines, :]])) for c in (0, 2, 4)]
                ends.append(jnp.concatenate(parts + [theirs[lines, :]]))
            late_round.put_rows(part, 0, *ends, buffers)

    buffers = call(
        late_kernel,
        (mark, adj_known, fine_couplings, mid_around, mid_beside, low_around, low_beside),
        late_round.buffers(),
    )
    late_got = swap(buffers, (0, 1))

    def window_kernel(mark, x, *rest):
        got, (x_out,) = rest[:swaps], rest[swaps:]
        x_out[...] = jnp.zeros(x_out.shape, F32)
        near, far = fifth_round.faces(0, got)
        mid_window.fill(x_out.at[0], x[...])
        mid_window.fill(x_out.at[1], beside_of(*near[2]))
        mid_window.fill(x_out.at[2], beside_of(*far[2]))
        for faces, step in ((near, 0), (far, 1)):
            for layer, value in zip((-1 - step, mid.depth + step), faces[0]):
                x_out[0, mid_window.layer(layer), :] = value
            for y, value in zip((-1 - step, mid.height + step), faces[1]):
                x_out[0, mid_window.row(y), :] = value

    (x_windows,) = call(window_kernel, (mark, x_mid, *fifth_got), [out(3, mid_window.rows, LANES)])

    last_rows, last_line = sizes[2] * sizes[1] * last_height, sizes[1] * last_height
    last_base = -(-(last_line + low_window.rim) // 8) * 8

    def solve_last(everyone, temp):
        channels = [[] for _ in range(2 * last_groups)]
        for first in range(0, sizes[0], last_groups):
            here = range(min(last_groups, sizes[0] - first))
            for g in here:
                for y in range(sizes[1]):
                    for z in range(sizes[2]):
                        sender = ((first + g) * sizes[1] + y) * sizes[2] + z
                        for half in range(2):
                            at = half * last_rows + z * last_line + y * last_height
                            start = keep + half * last_height
                            temp[g, at : at + last_height, :] = everyone[sender, start : start + last_height, :]
            parts = [temp[g] for g in here]
            group = lane_of(parts[0]) // last_width
            for q in range(last_groups):
                value = jnp.zeros_like(parts[0])
                for g in here:
                    value = jnp.where(group == g, roll(parts[g], last_width * (g - q), 1), value)
                channels[q].append(value[:last_rows])
                channels[last_groups + q].append(value[last_rows:])
        parts = [jnp.concatenate(tiles, axis=1) for tiles in channels[: last_groups + 4]]
        stencil, (inner, back, on, beside_y, beside_x) = parts[:7], parts[7:]
        y, x = row_y(inner, last_line), lane_of(inner)
        none = jnp.zeros((last_line, inner.shape[1]), F32)
        b = inner + jnp.concatenate([back[last_line:], none]) + jnp.concatenate([none, on[:-last_line]])
        b = b + jnp.where((y % last_height == 0) & (y > 0), roll(beside_y, 1, 0), 0.0)
        b = b + jnp.where((y % last_height == last_height - 1) & (y < last_line - 1), roll(beside_y, -1, 0), 0.0)
        b = b + jnp.where((x % last_width == 0) & (x > 0), roll(beside_x, 1, 1), 0.0)
        b = b + jnp.where((x % last_width == last_width - 1) & (x < inner.shape[1] - 1), roll(beside_x, -1, 1), 0.0)
        closed = Closed(last_line, 1)
        field = start = b * stencil[0]
        for sweep in range(COARSE_SWEEPS - 1):
            field = start + (1.0 - OMEGA) * field - off_apply(stencil, field, closed) * stencil[0]
        return field

    def spread_last(field, temp):
        gx, gy, gz = (lax.axis_index(name) for name in AXES)
        half, reach = low_window.line // 2, low_window.rim // 2
        layers = low.depth // 2 + 2
        dup = 2 * low.dup

        def taken(i, j):
            own = (j < LANES) & (i == gx * last_width + j // dup)
            before = (j >= LANES) & (j < LANES + low.dup) & (i == gx * last_width - 1)
            after = (j >= 2 * LANES - low.dup) & (i == (gx + 1) * last_width)
            return own | before | after

        at = last_base + (gz * (low.depth // 2) - 1) * last_line + gy * last_height - reach
        tiles = []
        for tile in range(0, field.shape[1], LANES):
            temp[12] = jnp.zeros(temp.shape[1:], F32)
            temp[12, last_base : last_base + last_rows, :] = field[:, tile : tile + LANES]
            tiles.append(jnp.concatenate([temp[12, pl.ds(at + k * last_line, half), :] for k in range(layers)]))
        both = matmul(jnp.concatenate(tiles, axis=1), one_hot((field.shape[1], 2 * LANES), taken))
        return [spread_rows(both[:, k * LANES : (k + 1) * LANES], layers, half, temp.at[13 + k]) for k in range(2)]

    def low_windows(everyone, temp, result):
        around = [(sy, sz) for sz in (-1, 0, 1) for sy in (-1, 0, 1)]
        per = -(-len(around) * keep // 8) * 8
        for k, sx in enumerate((0, -1, 1)):
            for i, (sy, sz) in enumerate(around):
                temp[k * per + keep * i : k * per + keep * (i + 1), :] = everyone[device(sx, sy, sz), 0:keep, :]
        packed = temp[: 3 * per, :]
        lane = lane_of(packed)
        turned = {by: roll(packed, by, 1) for by in range(1 - low.dup, low.dup)}
        for k in range(low.dup):
            value = turned[-k]
            for m in range(1, low.dup):
                value = jnp.where(lane % low.dup == m, turned[m - k], value)
            own, before, after = (value[i * per : (i + 1) * per] for i in range(3))
            forms = [own]
            for cells in (1, 2):
                forms.append(beside_of(roll(before, low.dup * cells, 1), roll(after, -low.dup * cells, 1)))
            for i, (sy, sz) in enumerate(around):
                for j in range(keep):
                    a, y = divmod(k * keep + j, low.height)
                    a, y = a + sz * low.depth, y + sy * low.height
                    if -2 <= a < low.depth + 2 and -low_window.rim <= y < low.height + low_window.rim:
                        at = low_window.at(a, y)
                        for form, source in enumerate(forms):
                            result[form, at : at + 1, :] = source[keep * i + j : keep * i + j + 1]
        return [result[form] for form in range(3)]

    def mid_edges(everyone, x):
        def lines(*steps):
            return everyone[device(*steps), own_at : own_at + 2, :]

        def unfolded(value, n):
            return jnp.concatenate([roll(value, -6 * k, 1) for k in range(n // 2)])

        def sides(values, k):
            return beside_of(roll(values[0], -2 * k, 1), roll(values[1], -2 * k - 2, 1))

        for sz in signs:
            a = -1 if sz < 0 else mid.depth
            for sy in signs:
                y = -1 if sy < 0 else mid.height
                got = lines(0, sy, sz)
                pair = unfold(got[:1])
                for layer, at, value in ((a, y, pair[:1]), (a + sz, y, pair[1:]), (a, y + sy, got[1:])):
                    row = mid_window.at(layer, at)
                    x[0, row : row + 1, :] = value
                row = mid_window.at(a, y)
                x[1, row : row + 1, :] = sides([lines(sx, sy, sz)[:1] for sx in signs], 0)
            got = [unfolded(lines(sx, 0, sz), mid.height) for sx in signs]
            x[1, mid_window.layer(a), :] = sides(got, 0)
            x[1, mid_window.layer(a + sz), :] = sides(got, 1)
            x[2, mid_window.layer(a), :] = sides(got, 2)
        for sy in signs:
            y = -1 if sy < 0 else mid.height
            got = [unfolded(lines(sx, sy, 0), mid.depth) for sx in signs]
            x[1, mid_window.row(y), :] = sides(got, 0)
            x[1, mid_window.row(y + sy), :] = sides(got, 1)
            x[2, mid_window.row(y), :] = sides(got, 2)

    def full(part, window, lines, side_lines, got):
        line, none = window.line, jnp.zeros((window.line, LANES), F32)
        ends = late_round.rows(part, 0, got)
        packed = jnp.concatenate([none, ends[0][3 * line :], side_lines[...], ends[1][3 * line :], none])

        def around(c):
            pair = slice(c // 2 * line, (c // 2 + 1) * line)
            own = slice(c % 2 * line, (c % 2 + 1) * line)
            return jnp.concatenate([none, unfold(ends[0][pair])[own], lines[c], unfold(ends[1][pair])[own], none])

        return around, lambda c: unpack_side(packed, c, window.grid.dup)

    def gradient_factors(mobility, pressure, trans, trans_before, *rest):
        got, (inner, layer_out, line_out, side_out, ends) = rest[:swaps], rest[swaps:]
        faces = third_round.faces(0, got, range(4, 8))
        rims = [Rim(fine, f, ends, c) for c, f in enumerate(faces)]
        lines = pl.ds(0, depth, stride=height)
        drops = []
        for dim in range(3):
            drops.append(0.25 * trans[dim] * (pressure[0] - rims[3].following(pressure[0], dim)))
        side_drop = 0.25 * trans_before[2] * (faces[3][2][0] - pressure[0])
        sides = []
        for c in range(3):
            value = mobility[c]
            for dim in range(3):
                inner[3 * dim + c] = drops[dim] * (value + rims[c].following(value, dim))
            drop = 0.25 * trans_before[0, :height, :] * (faces[3][0][0] - pressure[0, :height, :])
            layer_out[c] = drop * (faces[c][0][0] + mobility[c, :height, :])
            drop = 0.25 * trans_before[1, lines, :] * (faces[3][1][0] - pressure[0, lines, :])
            line_out[c] = drop * (faces[c][1][0] + mobility[c, lines, :])
            sides.append(side_drop * (faces[c][2][0] + value))
        side_out[...] = pack_sides(sides, 1)

    gradient_inputs = call(
        gradient_factors,
        (mobility, pressure, trans, trans_before, *third_got),
        [out(9, rows, LANES), out(3, height, LANES), out(3, depth, LANES), out(rows, LANES)],
        [(4, rows, LANES)],
    )

    def final_kernel(
        everyone,
        x_windows,
        mid_around,
        mid_beside,
        low_around,
        low_beside,
        adj_known,
        adj_factor,
        couplings,
        terms,
        layer_terms,
        line_terms,
        side_terms,
        *rest,
    ):
        late_got, third_got, fourth_got, fifth_got = (rest[max(0, k * swaps + late - swaps) : k * swaps + late] for k in range(4))
        rest = rest[3 * swaps + late :]
        adj_out, grad_out = rest[:2]
        last_temp, low_x, low_temp, x, temp, ends, around, beside, value_ref, adj, grad, sems = rest[2:]
        x[...] = x_windows[...]
        mid_edges(everyone, x)
        low_values = low_windows(everyone, low_temp, low_x)
        added = spread_last(solve_last(everyone, last_temp), temp)
        pair = full(2, low_window, low_around, low_beside, late_got)
        results = smooth(low_values, added, pair, low_window.line, low.dup)
        inner = slice(low_window.line, (low.depth + 3) * low_window.line)
        added = [spread_rows(v[inner], low.depth + 2, low_window.line, temp.at[10 + k]) for k, v in enumerate(results)]
        pair = full(1, mid_window, mid_around, mid_beside, late_got)
        beyond = late_round.faces(0, late_got)
        columns = fourth_round.columns(3, fourth_got) + third_round.columns(0, third_got, range(1, 4))
        columns += fifth_round.columns(1, fifth_got)
        factors = third_round.faces(0, third_got, range(1, 4))
        around[...], beside[...] = smooth([x[k] for k in range(3)], added, pair, mid_window.line, mid.dup)

        def own(ref, slot):
            lines = [ref[mid_window.layer(a), :] for a in range(mid.depth)]
            return spread_rows(jnp.concatenate(lines), mid.depth, mid.height, temp.at[slot])

        def layer(ref, a, slot):
            return spread_lines(ref[mid_window.layer(a), :], temp.at[slot])

        def lines(ref, y, slot):
            return spread_lines(ref[mid_window.row(y), :], temp.at[slot])

        def one_row(a, y):
            at = mid_window.at(a, y)
            return around[at : at + 1, :]

        value, side = own(around, 0), own(beside, 1)
        value_ref[...] = value
        layers = [(a, layer(around, a, k), layer(beside, a, k + 1)) for k, a in ((2, -1), (4, mid.depth))]
        rows_y = [(y, lines(around, y, k), lines(beside, y, k + 1)) for k, y in ((6, -1), (8, mid.height))]
        rim = Rim(fine, [[v[1] for v in layers], [v[1] for v in rows_y], (side, side)], ends, 0)

        def gain(value, shifts, coupling):
            total = (1.0 - OMEGA) * value
            for k in range(6):
                total = total - coupling(k) * shifts[k]
            return total

        shifts = [shift(value, dim) for dim in range(3) for shift in (rim.previous, rim.following)]
        own_gain = gain(value, shifts, lambda k: couplings[k])
        for c in range(3):
            adj[c] = adj_known[c] + adj_factor[c] * own_gain
        copies = [pltpu.make_async_copy(adj, adj_out, sems.at[3])]
        copies[0].start()

        def along_x(value, side):
            lane = lane_of(value)
            return [jnp.where(lane < 1, side, roll(value, 1, 1)), jnp.where(lane >= LANES - 1, side, roll(value, -1, 1))]

        def ended(value, low, high):
            row = lax.broadcasted_iota(jnp.int32, value.shape, 0)
            n = value.shape[0]
            return [jnp.where(row == 0, low, roll(value, 1, 0)), jnp.where(row == n - 1, high, roll(value, -1, 0))]

        layer_gains, line_gains = [], []
        for k, (a, here, there) in enumerate(layers):
            shifts = [here, value[:height]] if k == 0 else [value[rows - height :], here]
            shifts += ended(here, one_row(a, -1), one_row(a, mid.height)) + along_x(here, there)
            layer_gains.append(gain(here, shifts, lambda c: beyond[c][0][k]))
        for k, (y, here, there) in enumerate(rows_y):
            inside = value_ref[pl.ds(0 if k == 0 else height - 1, depth, stride=height), :]
            shifts = ended(here, one_row(-1, y), one_row(mid.depth, y))
            shifts += ([here, inside] if k == 0 else [inside, here]) + along_x(here, there)
            line_gains.append(gain(here, shifts, lambda c: beyond[c][1][k]))
        per = height // 4
        beside_column, own_column = pack_column(side), pack_column(value)
        lane, row = lane_of(own_column), lax.broadcasted_iota(jnp.int32, (8, LANES), 0)
        ends_z = [pack_column(v[2]) for v in layers]
        top = 2 * fine.groups - per
        shifts = [
            jnp.where(lane < per, ends_z[0], roll(beside_column, per, 1)),
            jnp.where(lane >= top, roll(ends_z[1], top, 1), roll(beside_column, -per, 1)),
        ]
        up, down = roll(beside_column, 1, 0), roll(beside_column, -1, 0)
        ends_y = [column_ends(rows_y[k][2], per, k == 1) for k in range(2)]
        shifts += [
            jnp.where(row > 0, up, jnp.where(lane % per < 2, ends_y[0], roll(up, 2, 1))),
            jnp.where(row < 7, down, jnp.where(lane % per >= per - 2, ends_y[1], roll(down, -2, 1))),
            jnp.where(lane % 2 == 1, beside_column, own_column),
            jnp.where(lane % 2 == 1, own_column, beside_column),
        ]
        side_gain = gain(beside_column, shifts, lambda c: columns[c])
        adj_rims = []
        for c in range(3):
            known, factor = beyond[6 + c], factors[c]
            faces = [[known[dim][k] + factor[dim][k] * gains[k] for k in range(2)] for dim, gains in enumerate((layer_gains, line_gains))]
            faces.append((unpack_column(columns[9 + c] + columns[6 + c] * side_gain, rows),) * 2)
            adj_rims.append(Rim(fine, faces, ends, 2 + c))
        values = [adj[c] for c in range(3)]
        lines = pl.ds(0, depth, stride=height)
        parts = []
        for c in range(3):
            layer, line, side = (adj_rims[c].faces[dim][0] for dim in range(3))
            parts.append(
                (
                    layer_terms[c] * (layer - values[c][:height]),
                    line_terms[c] * (line - adj[c, lines, :]),
                    unpack_side(side_terms[...], c, 1) * (side - values[c]),
                )
            )
        below = Rim(fine, [(sum(p[dim] for p in parts),) * 2 for dim in range(3)], ends, 5)
        for dim in range(3):
            here = 0.0
            for c in range(3):
                here = here + terms[3 * dim + c] * (values[c] - adj_rims[c].following(values[c], dim))
            grad[dim] = here + below.previous(here, dim)
            copies.append(pltpu.make_async_copy(grad.at[dim], grad_out.at[dim], sems.at[dim]))
            copies[-1].start()
        for copy in copies:
            copy.wait()

    adjoint, gradient = call(
        final_kernel,
        (everyone, x_windows, mid_around, mid_beside, low_around, low_beside)
        + (adj_known, adj_factor, fine_couplings, *gradient_inputs, *late_got, *third_got, *fourth_got, *fifth_got),
        [out(3, rows, LANES)] * 2,
        [
            (min(sizes[0], last_groups), 2 * last_rows, LANES),
            (3, low_window.rows, LANES),
            (max(low_window.rows, 96, 2 * last_base + last_rows), LANES),
            (3, mid_window.rows, LANES),
            (15, max(mid_window.rows, 2 * last_base + last_rows), LANES),
            (6, rows, LANES),
            (mid_window.rows, LANES),
            (mid_window.rows, LANES),
            (rows, LANES),
            (3, rows, LANES),
            (3, rows, LANES),
            pltpu.SemaphoreType.DMA((4,)),
        ],
        far_outputs=2,
    )
    shape = (3, depth, height, width)
    return adjoint.reshape(shape), gradient.reshape(shape)


def solution(mesh):
    cells = P("layer", "gy", "gx")
    fields = P(None, "layer", "gy", "gx")
    return jax.shard_map(
        local,
        mesh=mesh,
        in_specs=(
            fields,
            cells,
            fields,
            fields,
            fields,
            fields,
            fields,
            fields,
            fields,
            fields,
            cells,
            fields,
        ),
        out_specs=(fields, fields),
        check_vma=False,
    )
```

```python
import itertools

import jax
import jax.numpy as jnp
from jax import lax
from jax.experimental import pallas as pl
from jax.experimental.pallas import tpu as pltpu
from jax.sharding import PartitionSpec as P

SWEEPS = 3
LEVELS = 3
COARSE_SWEEPS = 4
OMEGA = 0.8
LANES = 128
AXES = ("gx", "gy", "layer")
BY_DIM = ("layer", "gy", "gx")
ORDER = ((0, 1), (0, 0), (1, 1), (1, 0), (2, 1), (2, 0))
F32 = jnp.float32


def pair_route(axis, phase):
    sizes = [lax.axis_size(name) for name in AXES]
    k = AXES.index(axis)
    n = sizes[k]
    route = []
    for index in itertools.product(*[range(size) for size in sizes]):
        target = list(index)
        if phase == 0:
            target[k] = index[k] ^ 1
        elif 0 < index[k] < n - 1 or k == 0:
            target[k] = (((index[k] + 1) % n ^ 1) - 1) % n
        else:
            target[0] = index[0] ^ 1
        flat = [(i[0] * sizes[1] + i[1]) * sizes[2] + i[2] for i in (index, target)]
        route.append(tuple(flat))
    return route


def phases(dim):
    return min(lax.axis_size(BY_DIM[dim]), 3) - 1


def sends(dims=(0, 1, 2)):
    return [(dim, phase) for dim, phase in ORDER if dim in dims and phase < phases(dim)]


def swap(buffers, dims=(0, 1, 2)):
    return [lax.ppermute(b, AXES, pair_route(BY_DIM[dim], phase)) for b, (dim, phase) in zip(buffers, sends(dims))]


class Grid:
    def __init__(self, depth, height, dup):
        self.depth, self.height, self.dup = depth, height, dup
        self.rows = depth * height
        self.width = LANES // dup
        self.groups = self.rows // 8

    def lines(self, dim):
        return (self.height, self.depth)[dim]

    def tiles(self, count):
        return -(-2 * self.dup * count * self.groups // LANES)

    def place(self, c, k):
        return divmod(2 * self.dup * (self.groups * c + k), LANES)


class Message:
    def __init__(self, *parts, dims=(0, 1, 2)):
        self.parts, self.dims = parts, dims

    def size(self, part, dim):
        part = self.parts[part]
        if isinstance(part, dict):
            return part.get(dim, 0)
        if dim not in part[2:] and len(part) > 2:
            return 0
        return part[0].tiles(part[1]) * 8 if dim == 2 else part[1] * part[0].lines(dim)

    def start(self, part, dim):
        return sum(self.size(i, dim) for i in range(part))

    def buffers(self):
        return [jax.ShapeDtypeStruct((self.start(len(self.parts), dim), LANES), F32) for dim, phase in sends(self.dims)]

    def put(self, dim, rows, first, last, out):
        if phases(dim) == 0:
            return
        out = dict(zip(sends(self.dims), out))
        even = lax.axis_index(BY_DIM[dim]) % 2 == 0
        out[dim, 0][rows] = last if first is last else jnp.where(even, last, first)
        if phases(dim) == 2:
            out[dim, 1][rows] = last if first is last else jnp.where(even, first, last)

    def put_rows(self, part, dim, first, last, out):
        start = self.start(part, dim)
        self.put(dim, slice(start, start + self.size(part, dim)), first, last, out)

    def packed(self, part, pairs):
        grid = self.parts[part][0]
        lane = lax.broadcasted_iota(jnp.int32, (8, LANES), 1)
        count, dup = self.parts[part][1], grid.dup
        tiles = [jnp.zeros((8, LANES), F32)] * grid.tiles(count)
        for c, (first, last) in enumerate(pairs):
            for k in range(grid.groups):
                tile, at = grid.place(c, k)
                rows = slice(8 * k, 8 * k + 8)
                value = last(rows)
                if first is not last:
                    value = jnp.where(lane < dup, first(rows), value)
                here = (lane >= at) & (lane < at + 2 * dup)
                tiles[tile] = jnp.where(here, roll(value, at + dup, 1), tiles[tile])
        return jnp.concatenate(tiles)

    def emit(self, part, channels, out):
        grid = self.parts[part][0]
        lane = lax.broadcasted_iota(jnp.int32, (8, LANES), 1)
        for dim in range(3):
            if self.size(part, dim) == 0:
                continue
            start = self.start(part, dim)
            if dim == 2:
                value = self.packed(part, channels[dim])
                self.put(dim, slice(start, start + value.shape[0]), value, value, out)
                continue
            if dim == 0:
                low, high = slice(0, grid.height), slice(grid.rows - grid.height, grid.rows)
            else:
                low, high = (pl.ds(s, grid.depth, stride=grid.height) for s in (0, grid.height - 1))
            n = grid.lines(dim)
            for c, (first, last) in enumerate(channels[dim]):
                self.put(dim, slice(start + c * n, start + (c + 1) * n), first(low), last(high), out)

    def both(self, dim, rows, got):
        if phases(dim) == 0:
            return (jnp.zeros((rows.stop - rows.start, LANES), F32),) * 2
        got = dict(zip(sends(self.dims), got))
        me, n = lax.axis_index(BY_DIM[dim]), lax.axis_size(BY_DIM[dim])
        even = me % 2 == 0
        one = got[dim, 0][rows]
        if phases(dim) == 1:
            return jnp.where(even, 0.0, one), jnp.where(even, one, 0.0)
        two = got[dim, 1][rows]
        before, after = jnp.where(even, two, one), jnp.where(even, one, two)
        return jnp.where(me > 0, before, 0.0), jnp.where(me < n - 1, after, 0.0)

    def rows(self, part, dim, got):
        start = self.start(part, dim)
        return self.both(dim, slice(start, start + self.size(part, dim)), got)

    def faces(self, part, got, channels=None):
        grid, count = self.parts[part][:2]
        channels = range(count) if channels is None else channels
        result = [[None] * 3 for _ in channels]
        for dim in range(3):
            if self.size(part, dim) == 0:
                continue
            start = self.start(part, dim)
            if dim == 2:
                dup = grid.dup
                merged = self.sides(part, got)
                for i, c in enumerate(channels):
                    pieces = []
                    for k in range(grid.groups):
                        tile, at = grid.place(c, k)
                        pieces.append(roll(merged[8 * tile : 8 * tile + 8], -at - dup, 1))
                    result[i][dim] = (jnp.concatenate(pieces),) * 2
            else:
                size = grid.lines(dim)
                for i, c in enumerate(channels):
                    result[i][dim] = self.both(dim, slice(start + c * size, start + (c + 1) * size), got)
        return result

    def sides(self, part, got):
        grid, count = self.parts[part][:2]
        start, dup = self.start(part, 2), grid.dup
        before, after = self.both(2, slice(start, start + 8 * grid.tiles(count)), got)
        return jnp.where(lane_of(before) % (2 * dup) < dup, roll(after, -dup, 1), roll(before, dup, 1))

    def columns(self, part, got, channels=None):
        grid, count = self.parts[part][:2]
        merged = self.sides(part, got)
        places = [grid.place(c, 0) for c in (range(count) if channels is None else channels)]
        return [roll(merged[8 * tile : 8 * tile + 8], -at, 1) for tile, at in places]

    def halos(self, part, got, scratch, channels=None):
        return [Rim(self.parts[part][0], r, scratch, c) for c, r in enumerate(self.faces(part, got, channels))]


class Window:
    def __init__(self, grid, rim):
        self.grid, self.rim = grid, rim
        self.line = grid.height + 2 * rim
        self.rows = (grid.depth + 4) * self.line

    def at(self, layer, y):
        return (layer + 2) * self.line + self.rim + y

    def layer(self, layer):
        return slice(self.at(layer, 0), self.at(layer, self.grid.height))

    def row(self, y):
        return pl.ds(self.at(0, y), self.grid.depth, stride=self.line)

    def fill(self, ref, own):
        height = self.grid.height
        for a in range(self.grid.depth):
            ref[self.layer(a), :] = own[a * height : (a + 1) * height]


class Rim:
    def __init__(self, grid, faces, scratch, c):
        self.grid, self.faces = grid, faces
        ends = scratch.at[c]
        ends[pl.ds(0, grid.depth, stride=grid.height), :] = faces[1][0]
        ends[pl.ds(grid.height - 1, grid.depth, stride=grid.height), :] = faces[1][1]
        self.y_ends = ends[...]

    def previous(self, value, dim):
        g = self.grid
        if dim == 0:
            return jnp.concatenate([self.faces[0][0], value[: g.rows - g.height]])
        if dim == 1:
            return jnp.where(row_y(value, g.height) == 0, self.y_ends, roll(value, 1, 0))
        return jnp.where(lane_of(value) < g.dup, self.faces[2][0], roll(value, g.dup, 1))

    def following(self, value, dim):
        g = self.grid
        if dim == 0:
            return jnp.concatenate([value[g.height :], self.faces[0][1]])
        if dim == 1:
            return jnp.where(row_y(value, g.height) == g.height - 1, self.y_ends, roll(value, -1, 0))
        return jnp.where(lane_of(value) >= value.shape[1] - g.dup, self.faces[2][1], roll(value, -g.dup, 1))


class Closed:
    def __init__(self, height, dup):
        self.height, self.dup = height, dup

    def previous(self, value, dim):
        if dim == 0:
            return jnp.concatenate([jnp.zeros_like(value[: self.height]), value[: -self.height]])
        if dim == 1:
            return jnp.where(row_y(value, self.height) == 0, 0.0, roll(value, 1, 0))
        return jnp.where(lane_of(value) < self.dup, 0.0, roll(value, self.dup, 1))

    def following(self, value, dim):
        if dim == 0:
            return jnp.concatenate([value[self.height :], jnp.zeros_like(value[: self.height])])
        if dim == 1:
            return jnp.where(row_y(value, self.height) == self.height - 1, 0.0, roll(value, -1, 0))
        return jnp.where(lane_of(value) >= value.shape[1] - self.dup, 0.0, roll(value, -self.dup, 1))


def roll(value, shift, axis):
    shift %= value.shape[axis]
    return pltpu.roll(value, shift, axis) if shift else value


def row_y(value, height):
    return lax.broadcasted_iota(jnp.int32, value.shape, 0) % height


def lane_of(value):
    return lax.broadcasted_iota(jnp.int32, value.shape, 1)


def loader(ref, c):
    return lambda rows: ref[c, rows, :]


def product(coefs, k, ref):
    return lambda rows: coefs[k, rows, :] * ref[rows, :]


def off_apply(stencil, field, rim):
    total = 0.0
    for dim in range(3):
        total = total + rim.previous(stencil[2 + 2 * dim] * field, dim)
        total = total + rim.following(stencil[1 + 2 * dim] * field, dim)
    return total


def block_row(blocks, c, values):
    return blocks[c] * values[0] + blocks[3 + c] * values[1] + blocks[6 + c] * values[2]


def system_row(c, values, rim, blocks, trans, trans_before):
    total = block_row(blocks, c, values)
    v = values[c]
    for dim in range(3):
        total = total + trans[dim] * (v - rim.following(v, dim))
        total = total + trans_before[dim] * (v - rim.previous(v, dim))
    return total


def pair_sum_x(value, dup):
    odd = (lane_of(value) // dup) % 2 == 1
    return value + jnp.where(odd, roll(value, dup, 1), roll(value, -dup, 1))


def pair_sum_rows(value, depth, height, scratch):
    half = depth // 2
    parts = [value[2 * a * height : (2 * a + 1) * height] + value[(2 * a + 1) * height : (2 * a + 2) * height] for a in range(half)]
    whole = jnp.concatenate(parts)
    count = half * height // 2
    sums = []
    for at in range(0, whole.shape[1], LANES):
        scratch[: half * height, :] = whole[:, at : at + LANES]
        sums.append(scratch[pl.ds(0, count, stride=2), :] + scratch[pl.ds(1, count, stride=2), :])
    return jnp.concatenate(sums, axis=1)


def spread_rows(value, depth, height, scratch):
    count = depth * height
    tiles = []
    for at in range(0, value.shape[1], LANES):
        scratch[pl.ds(0, count, stride=2), :] = value[:, at : at + LANES]
        scratch[pl.ds(1, count, stride=2), :] = value[:, at : at + LANES]
        wide = scratch[: 2 * count, :]
        tiles.append(jnp.concatenate([wide[2 * height * (a // 2) : 2 * height * (a // 2 + 1)] for a in range(2 * depth)]))
    return jnp.concatenate(tiles, axis=1)


def spread_lines(value, scratch):
    count = value.shape[0]
    scratch[pl.ds(0, count, stride=2), :] = value
    scratch[pl.ds(1, count, stride=2), :] = value
    return scratch[: 2 * count, :]


def fold(value):
    half = value.shape[0] // 2
    return jnp.where(lane_of(value[:half]) % 2 == 0, value[:half], value[half:])


def unfold(value):
    even = lane_of(value) % 2 == 0
    return jnp.concatenate([jnp.where(even, value, roll(value, 1, 1)), jnp.where(even, roll(value, -1, 1), value)])


def beside_of(before, after):
    if before is after:
        return before
    return jnp.where(lane_of(before) < LANES // 2, before, after)


def pack_sides(values, dup):
    total = jnp.zeros_like(values[0])
    lane = lane_of(total)
    for c, value in enumerate(values):
        total = jnp.where((lane >= dup * c) & (lane < dup * (c + 1)), roll(value, dup * c, 1), total)
        high = LANES - dup * c
        total = jnp.where((lane >= high - dup) & (lane < high), roll(value, -dup * c, 1), total)
    return total


def unpack_side(value, c, dup):
    return beside_of(roll(value, -dup * c, 1), roll(value, dup * c, 1))


def pack_column(value):
    tile = jnp.zeros((8, LANES), F32)
    lane = lane_of(tile)
    for k in range(value.shape[0] // 8):
        tile = jnp.where((lane >= 2 * k) & (lane < 2 * k + 2), roll(value[8 * k : 8 * k + 8], 2 * k + 1, 1), tile)
    return tile


def unpack_column(tile, rows):
    return jnp.concatenate([roll(tile, -2 * k - 1, 1) for k in range(rows // 8)])


def column_ends(value, per, last):
    step = per - 1 if last else 1
    turned = pltpu.roll(value, step, 1, stride=per, stride_axis=0)
    lane, row = lane_of(value), lax.broadcasted_iota(jnp.int32, value.shape, 0)
    here = (lane // per == row) & (lane % per >= per - 2 if last else lane % per < 2)
    return jnp.sum(jnp.where(here, turned, 0.0), axis=0, keepdims=True)


def moved(rows, by):
    if isinstance(rows, slice):
        return slice(rows.start + by, rows.stop + by)
    return pl.ds(rows.start + by, rows.size, stride=rows.stride)


def shifts_of(value, inner, outer, line, dup, beside):
    none = jnp.zeros((line, LANES), F32)
    lane = lane_of(value)
    if beside:
        low, high = jnp.where(lane < LANES // 2, outer, inner), jnp.where(lane < LANES // 2, inner, outer)
    else:
        low, high = jnp.where(lane < dup, outer, roll(value, dup, 1)), jnp.where(lane >= LANES - dup, outer, roll(value, -dup, 1))
    return [
        jnp.concatenate([none, value[:-line]]),
        jnp.concatenate([value[line:], none]),
        roll(value, 1, 0),
        roll(value, -1, 0),
        low,
        high,
    ]


def smooth(x, added, couplings, line, dup):
    around, beside, second = x[0] + added[0], x[1] + added[1], x[2] + added[1]
    results = []
    for k, (value, shifts) in enumerate(
        (
            (around, shifts_of(around, None, beside, line, dup, False)),
            (beside, shifts_of(beside, around, second, line, dup, True)),
        )
    ):
        total = x[k] + (1.0 - OMEGA) * value
        for c in range(6):
            total = total - couplings[k](c) * shifts[c]
        results.append(total)
    return results


def one_hot(shape, hit):
    return jnp.where(hit(lax.broadcasted_iota(jnp.int32, shape, 0), lax.broadcasted_iota(jnp.int32, shape, 1)), 1.0, 0.0).astype(F32)


def matmul(values, ones):
    n = values.shape[0]
    extra = -n % 16
    if extra:
        values = jnp.concatenate([values, jnp.zeros((extra, values.shape[1]), F32)])
    parts = []
    for _ in range(3):
        parts.append(values.astype(jnp.bfloat16))
        values = values - parts[-1].astype(F32)
    product = jnp.dot(jnp.concatenate(parts), ones.astype(jnp.bfloat16), preferred_element_type=F32)
    step = n + extra
    return (product[2 * step : 2 * step + n] + product[step : step + n]) + product[:n]


def call(kernel, inputs, outputs, scratch=(), far_inputs=0, far_outputs=0):
    inputs = list(inputs)
    for i in range(far_inputs):
        inputs[i] = pltpu.with_memory_space_constraint(inputs[i], pltpu.HBM)

    def specs(count, far):
        return [pl.BlockSpec(memory_space=pltpu.HBM if i < far else pltpu.VMEM) for i in range(count)]

    return pl.pallas_call(
        kernel,
        out_shape=list(outputs),
        in_specs=specs(len(inputs), far_inputs),
        out_specs=specs(len(outputs), far_outputs),
        scratch_shapes=[pltpu.VMEM(shape, F32) if isinstance(shape, tuple) else shape for shape in scratch],
        compiler_params=pltpu.CompilerParams(vmem_limit_bytes=24 * 2**20),
    )(*inputs)


def local(
    source,
    active_cells,
    diag_blocks,
    frozen_inverses,
    transmissibility,
    pressure_weights,
    stencil_fine,
    coarse_one,
    coarse_two,
    coarse_three,
    pressure_state,
    mobilities,
):
    depth, height, width = active_cells.shape
    low_depth, low_height, low_width = coarse_two.shape[1:]
    last_height, last_width = coarse_three.shape[2:]
    fine = Grid(depth, height, 1)
    mid = Grid(depth // 2, height // 2, 2)
    low = Grid(low_depth, low_height, 4)
    mid_window, low_window = Window(mid, 4), Window(low, 2)
    sizes = [lax.axis_size(name) for name in AXES]
    count = sizes[0] * sizes[1] * sizes[2]
    swaps = len(sends())
    rows = fine.rows
    first_round = Message((fine, 4), (mid, 1), (low, 1))
    second_round = Message((fine, 4))
    third_round = Message((fine, 8), (mid, 6, 2), (low, 6, 2))
    fourth_round = Message((fine, 1), {1: 4 * mid.depth}, {1: 4 * low.depth}, (fine, 6, 2), {2: 2 * depth})
    fifth_round = Message((mid, 2), (fine, 3, 2), {1: 2 * depth}, {2: 2 * depth})
    late_round = Message((fine, 9, 0, 1), {0: 4 * mid_window.line}, {0: 4 * low_window.line}, dims=(0, 1))
    late = len(sends((0, 1)))

    def flat(array):
        return array.reshape(array.shape[:-3] + (rows, width))

    def out(*shape):
        return jax.ShapeDtypeStruct(shape, F32)

    source, active, diag, frozen, trans, weights, stencil, pressure, mobility = (
        flat(a)
        for a in (
            source,
            active_cells,
            diag_blocks,
            frozen_inverses,
            transmissibility,
            pressure_weights,
            stencil_fine,
            pressure_state,
            mobilities,
        )
    )
    pressure = pressure[None]

    def coupling_faces(coefs):
        return [[(loader(coefs, 1 + 2 * dim), loader(coefs, 2 + 2 * dim))] for dim in range(3)]

    def widen(values, dup):
        wide = matmul(values, one_hot((values.shape[1], LANES), lambda i, j: i == j // dup))
        return wide.reshape(7, wide.shape[0] // 7, LANES)

    def start_kernel(source, active, frozen, trans, one, two, rhs_out, it_out, frozen_out, trans_out, one_out, two_out, *rest):
        buffers, (source_in, active_in, one_in, two_in, two_flat, sems) = rest[:-6], rest[-6:]
        order = [k for c in range(3) for k in (c, 3 + c, 6 + c)]
        pairs = [(active, active_in), (source, source_in)] + [(frozen.at[k], frozen_out.at[k]) for k in order]
        pairs += [(trans, trans_out), (one, one_in), (two, two_in)]
        copies = [pltpu.make_async_copy(a, b, sems.at[i]) for i, (a, b) in enumerate(pairs)]
        for copy in copies[-2:] + copies[:-2]:
            copy.start()
        copies[-2].wait()
        copies[-1].wait()
        one_out[...] = widen(one_in[...].reshape(7 * mid.rows, mid.width), mid.dup)
        for c in range(7):
            for a in range(low.depth):
                at = c * low.rows + a * low.height
                two_flat[at : at + low.height, :] = two_in[c, a]
        two_out[...] = widen(two_flat[...], low.dup)
        first_round.emit(1, coupling_faces(one_out), buffers)
        first_round.emit(2, coupling_faces(two_out), buffers)
        copies[0].wait()
        mask = active_in[...].astype(F32)
        copies[1].wait()
        rhs = [source_in[c] * mask for c in range(3)]
        for c in range(3):
            rhs_out[c] = rhs[c]
        for c in range(3):
            for copy in copies[2 + 3 * c : 5 + 3 * c]:
                copy.wait()
            it_out[c] = block_row(frozen_out, c, rhs)
        copies[-3].wait()
        its = [(loader(it_out, c),) * 2 for c in range(3)]
        first_round.emit(0, [its + [(loader(trans_out, dim),) * 2] for dim in range(3)], buffers)

    rhs, iterate, frozen, trans, one, two, *buffers = call(
        start_kernel,
        (source, active, frozen, trans, coarse_one.reshape(7, mid.rows, mid.width), coarse_two),
        [out(3, rows, LANES)] * 2
        + [out(9, rows, LANES), out(3, rows, LANES), out(7, mid.rows, LANES), out(7, low.rows, LANES)]
        + first_round.buffers(),
        [
            (3, rows, LANES),
            pltpu.VMEM((rows, LANES), jnp.int32),
            (7, mid.rows, mid.width),
            (7, low.depth, low.height, low.width),
            (7 * low.rows, low.width),
            pltpu.SemaphoreType.DMA((14,)),
        ],
        far_inputs=6,
    )
    got = swap(buffers)

    def couplings(coefs, rim, result):
        scale = OMEGA / coefs[0]
        for dim in range(3):
            result[2 * dim] = scale * rim.previous(coefs[2 + 2 * dim], dim)
            result[2 * dim + 1] = scale * rim.following(coefs[1 + 2 * dim], dim)

    def coarse_couplings(mobility, one, two, *rest):
        got, outs, mobility_out, scratch = rest[:swaps], rest[swaps : swaps + 2], rest[swaps + 2], rest[swaps + 3 :]
        fetch = pltpu.make_async_copy(mobility, mobility_out, scratch[2])
        fetch.start()
        for part, coefs, result, ends in ((1, one, outs[0], scratch[0]), (2, two, outs[1], scratch[1])):
            couplings(coefs, first_round.halos(part, got, ends)[0], result)
        fetch.wait()

    mid_couplings, low_couplings, mobility_near = call(
        coarse_couplings,
        (mobility, one, two, *got),
        [out(6, mid.rows, LANES), out(6, low.rows, LANES), out(3, rows, LANES)],
        [(1, mid.rows, LANES), (1, low.rows, LANES), pltpu.SemaphoreType.DMA],
        far_inputs=1,
    )

    def sweep_one(rhs, it, frozen, diag, trans, stencil, *rest):
        got, (it_out, before_out), buffers, ends = rest[:swaps], rest[swaps : swaps + 2], rest[swaps + 2 : -1], rest[-1]
        rims = first_round.halos(0, got, ends)
        trans_before = [rims[3].previous(trans[dim], dim) for dim in range(3)]
        values = [it[c] for c in range(3)]
        rest = [rhs[c] - system_row(c, values, rims[c], diag, trans, trans_before) for c in range(3)]
        for c in range(3):
            before_out[c] = trans_before[c]
            it_out[c] = values[c] + block_row(frozen, c, rest)
        channels = [(loader(it_out, c),) * 2 for c in range(3)]
        second_round.emit(0, [channels + faces for faces in coupling_faces(stencil)], buffers)

    iterate, trans_before, *buffers = call(
        sweep_one,
        (rhs, iterate, frozen, diag, trans, stencil, *got),
        [out(3, rows, LANES)] * 2 + second_round.buffers(),
        [(4, rows, LANES)],
    )
    second_got = swap(buffers)

    def same(ref, channels):
        return [(loader(ref, c),) * 2 for c in channels]

    def sweep_two(
        rhs, it, frozen, diag, trans, trans_before, active, weights, mobility, pressure, mid_couplings, low_couplings, *rest
    ):
        got, it_out, buffers, ends = rest[:swaps], rest[swaps], rest[swaps + 1 : -1], rest[-1]
        rims = second_round.halos(0, got, ends, range(3))
        values = [it[c] for c in range(3)]
        rest = [rhs[c] - system_row(c, values, rims[c], diag, trans, trans_before) for c in range(3)]
        for c in range(3):
            it_out[c] = values[c] + block_row(frozen, c, rest)
        factors = [(lambda at, c=c: active[at, :].astype(F32) * weights[c, at, :],) * 2 for c in range(3)]
        states = same(mobility, range(3)) + same(pressure, range(1))
        third_round.emit(0, [same(it_out, range(1)) + factors + states] * 3, buffers)
        third_round.emit(1, [same(mid_couplings, range(6))] * 3, buffers)
        third_round.emit(2, [same(low_couplings, range(6))] * 3, buffers)

    iterate, *buffers = call(
        sweep_two,
        (rhs, iterate, frozen, diag, trans, trans_before, active, weights, mobility_near, pressure)
        + (mid_couplings, low_couplings, *second_got),
        [out(3, rows, LANES)] + third_round.buffers(),
        [(3, rows, LANES)],
    )
    third_got = swap(buffers)

    def fine_kernel(stencil, *rest):
        got, (result, sides, ends) = rest[:swaps], rest[swaps:]
        couplings(stencil, second_round.halos(0, got, ends, [3])[0], result)
        sides[...] = fourth_round.packed(3, same(result, range(6)))

    coupling_sides = out(8 * fine.tiles(6), LANES)
    fine_couplings, coupling_sides = call(
        fine_kernel, (stencil, *second_got), [out(6, rows, LANES), coupling_sides], [(1, rows, LANES)]
    )

    def products(coefs, field):
        return [[(product(coefs, 1 + 2 * dim, field), product(coefs, 2 + 2 * dim, field))] for dim in range(3)]

    def pressure_kernel(rhs, it, diag, trans, trans_before, stencil, coupling_sides, mid_couplings, low_couplings, *rest):
        got, (b_out, x_out, mid_side, low_side), buffers = rest[:swaps], rest[swaps : swaps + 4], rest[swaps + 4 : -1]
        (rim,) = third_round.halos(0, got, rest[-1], [0])
        b = rhs[0] - system_row(0, [it[c] for c in range(3)], rim, diag, trans, trans_before)
        b_out[...] = b
        x_out[...] = b * (OMEGA / stencil[0])
        fourth_round.emit(0, products(stencil, x_out), buffers)
        fourth_round.put_rows(3, 2, coupling_sides[...], coupling_sides[...], buffers)
        for part, grid, values, side in ((1, mid, mid_couplings, mid_side), (2, low, low_couplings, low_side)):
            side[...] = pack_sides([beside_of(*faces[2]) for faces in third_round.faces(part, got)], grid.dup)
            ends = []
            for y in (0, grid.height - 1):
                lines = pl.ds(y, grid.depth, stride=grid.height)
                parts = [fold(jnp.concatenate([values[c, lines, :], values[c + 1, lines, :]])) for c in (0, 2, 4)]
                ends.append(jnp.concatenate(parts + [side[lines, :]]))
            fourth_round.put_rows(part, 1, *ends, buffers)

    b_fine, x_fine, mid_side, low_side, *buffers = call(
        pressure_kernel,
        (rhs, iterate, diag, trans, trans_before, stencil, coupling_sides, mid_couplings, low_couplings, *third_got),
        [out(rows, LANES)] * 2 + [out(mid.rows, LANES), out(low.rows, LANES)] + fourth_round.buffers(),
        [(1, rows, LANES)],
    )
    fourth_got = swap(buffers)

    def residual_kernel(b, x, stencil, one, it, active, weights, *rest):
        got, (x_out, adj_out, factor_out), buffers = rest[:swaps], rest[swaps : swaps + 3], rest[swaps + 3 : -2]
        ends, temp = rest[-2:]
        (rim,) = fourth_round.halos(0, got, ends, [0])
        off = off_apply(stencil, x[...], rim)
        residual = (1.0 - OMEGA) * b[...] - off
        q = (1.0 - OMEGA) * x[...] + (b[...] - off) * (OMEGA / stencil[0])
        mask = active[...].astype(F32)
        for c in range(3):
            factor = mask * weights[c]
            factor_out[c] = factor
            adj_out[c] = mask * it[c] + factor * q
        coarse = pair_sum_rows(pair_sum_x(residual, 1), depth, height, temp)
        x_out[...] = coarse * (OMEGA / one[0])
        near = (lambda at: x_out[at, :],) * 2
        channels = []
        for step in (mid.height, 1):
            channels.append([near, (lambda at, s=step: x_out[moved(at, s), :], lambda at, s=step: x_out[moved(at, -s), :])])
        channels.append([near, (lambda at: roll(x_out[at, :], -mid.dup, 1), lambda at: roll(x_out[at, :], mid.dup, 1))])
        fifth_round.emit(0, channels, buffers)
        fifth_round.emit(1, [same(adj_out, range(3))] * 3, buffers)

    x_mid, adj_known, adj_factor, *buffers = call(
        residual_kernel,
        (b_fine, x_fine, stencil, one, iterate, active, weights, *fourth_got),
        [out(mid.rows, LANES), out(3, rows, LANES), out(3, rows, LANES)] + fifth_round.buffers(),
        [(1, rows, LANES), (rows // 2, LANES)],
    )
    fifth_got = swap(buffers)

    def lines_kernel(mid_own, mid_side, low_own, low_side, *rest):
        got, windows = rest[:swaps], rest[swaps:]
        for part, window, own, side, ours, theirs in (
            (1, mid_window, mid_own, mid_side, windows[0], windows[1]),
            (2, low_window, low_own, low_side, windows[2], windows[3]),
        ):
            grid, line = window.grid, window.line
            halves = []
            for half in fourth_round.rows(part, 1, got):
                pairs = [unfold(half[k * grid.depth : (k + 1) * grid.depth]) for k in range(3)]
                halves.append(jnp.concatenate(pairs + [half[3 * grid.depth :]]))
            ours[...] = jnp.zeros(ours.shape, F32)
            theirs[...] = jnp.zeros(theirs.shape, F32)
            pairs = [(ours.at[c], own.at[c], c) for c in range(6)] + [(theirs, side, 6)]
            for ref, source, c in pairs:
                for a in range(grid.depth):
                    at = a * line + window.rim
                    ref[at : at + grid.height, :] = source[a * grid.height : (a + 1) * grid.height, :]
                for y, half in zip((-1, grid.height), halves):
                    ref[pl.ds(window.rim + y, grid.depth, stride=line), :] = half[c * grid.depth : (c + 1) * grid.depth]

    mid_lines, low_lines = (mid.depth * mid_window.line, LANES), (low.depth * low_window.line, LANES)
    mid_around, mid_beside, low_around, low_beside = call(
        lines_kernel,
        (mid_couplings, mid_side, low_couplings, low_side, *fourth_got),
        [out(6, *mid_lines), out(*mid_lines), out(6, *low_lines), out(*low_lines)],
    )

    def device(*steps):
        at = [lax.axis_index(name) for name in AXES]
        inside, flat = True, 0
        for position, size, step in zip(at, sizes, steps):
            inside = inside & (position + step >= 0) & (position + step < size)
        for position, size, step in zip(at, sizes, steps):
            flat = flat * size + jnp.where(inside, position + step, position)
        return flat

    last_groups = LANES // last_width
    last = jnp.concatenate([OMEGA / coarse_three[:1], coarse_three[1:]]).reshape(7, last_height, last_width)
    last = jnp.pad(last, ((0, 2 * last_groups - 7), (0, 0), (0, 0)))
    last = last.reshape(2, last_groups, last_height, last_width).transpose(0, 2, 1, 3).reshape(2 * last_height, LANES)
    keep = low.rows // low.dup
    own_at = keep + 2 * last_height
    block = own_at + 2
    signs = (-1, 1)

    def columns(near, far, sign):
        if sign < 0:
            parts = near, roll(far, 2, 1), roll(near, 2, 1)
        else:
            parts = roll(near, 2, 1), roll(far, 4, 1), roll(near, 8, 1)
        lane = lane_of(near)
        return jnp.where(lane < 2, parts[0], jnp.where(lane < 4, parts[1], jnp.where(lane < 6, parts[2], 0.0)))

    def low_kernel(x, one, mid_couplings, two, last, *rest):
        got, (sent, mark, ends, temp) = rest[:swaps], rest[swaps:]
        (rim,) = fifth_round.halos(0, got, ends, [0])
        value = x[...]
        total = (1.0 - OMEGA) * value
        for dim in range(3):
            total = total - mid_couplings[2 * dim] * rim.previous(value, dim)
            total = total - mid_couplings[2 * dim + 1] * rim.following(value, dim)
        residual = total * (one[0] * (1.0 / OMEGA))
        b = pair_sum_rows(pair_sum_x(residual, mid.dup), mid.depth, mid.height, temp.at[0])
        field = b * (OMEGA / two[0])
        to_next = [two[2 + 2 * dim] * field for dim in range(3)]
        to_previous = [two[1 + 2 * dim] * field for dim in range(3)]
        closed = Closed(low.height, low.dup)
        inner = (1.0 - OMEGA) * b
        for dim in range(3):
            inner = inner - closed.previous(to_next[dim], dim) - closed.following(to_previous[dim], dim)
        row, lane = lax.broadcasted_iota(jnp.int32, field.shape, 0), lane_of(field)
        layer, y = row // low.height, row % low.height
        outer = [
            jnp.where(layer == 0, -to_previous[0], 0.0),
            jnp.where(layer == low.depth - 1, -to_next[0], 0.0),
            jnp.where(y == 0, -to_previous[1], jnp.where(y == low.height - 1, -to_next[1], 0.0)),
            jnp.where(lane < low.dup, -to_previous[2], jnp.where(lane >= LANES - low.dup, -to_next[2], 0.0)),
        ]
        parts = [inner] + outer
        parts = [pair_sum_rows(pair_sum_x(v, low.dup), low.depth, low.height, temp.at[1 + k]) for k, v in enumerate(parts)]
        parts = matmul(jnp.concatenate(parts), one_hot((LANES, LANES), lambda i, j: i == 2 * low.dup * j))
        parts = [parts[k * last_height : (k + 1) * last_height] for k in range(5)]
        upper = last[:last_height] + roll(parts[0], 7 * last_width, 1)
        lower = last[last_height:]
        for k in range(4):
            lower = lower + roll(parts[1 + k], k * last_width, 1)
        packed = jnp.zeros((keep, LANES), F32)
        phase = lane_of(packed) % low.dup
        for k in range(low.dup):
            packed = jnp.where(phase == k, field[k * keep : (k + 1) * keep], packed)
        filled = jnp.concatenate([packed, upper, lower, jnp.zeros((2, LANES), F32)])
        sent[...] = jnp.broadcast_to(filled[None], (count, block, LANES))
        mark[...] = filled

        def near(sign, size):
            return 0 if sign < 0 else size - 1

        def line(a, y):
            return x[a * mid.height + y : a * mid.height + y + 1, :]

        def across(a):
            return x[a * mid.height : (a + 1) * mid.height, :]

        def along(y):
            return x[pl.ds(y, mid.depth, stride=mid.height), :]

        def folded(value):
            return sum(roll(value[2 * k : 2 * k + 2], 6 * k, 1) for k in range(value.shape[0] // 2))

        for sz in signs:
            a = near(sz, mid.depth)
            for sy in signs:
                y = near(sy, mid.height)
                pair = fold(jnp.concatenate([line(a, y), line(a - sz, y)]))
                sent[device(0, sy, sz), own_at : own_at + 2, :] = jnp.concatenate([pair, line(a, y - sy)])
                for sx in signs:
                    corner = columns(line(a, y), line(a, y), sx)
                    sent[device(sx, sy, sz), own_at : own_at + 1, :] = corner
            for sx in signs:
                sent[device(sx, 0, sz), own_at : own_at + 2, :] = folded(columns(across(a), across(a - sz), sx))
        for sy in signs:
            y = near(sy, mid.height)
            for sx in signs:
                sent[device(sx, sy, 0), own_at : own_at + 2, :] = folded(columns(along(y), along(y - sy), sx))

    sent, mark = call(
        low_kernel,
        (x_mid, one, mid_couplings, two, last, *fifth_got),
        [out(count, block, LANES), out(block, LANES)],
        [(1, mid.rows, LANES), (6, mid.rows // 2, LANES)],
    )
    everyone = lax.all_to_all(sent, AXES, 0, 0)

    def late_kernel(mark, adj, couplings, mid_around, mid_beside, low_around, low_beside, *buffers):
        late_round.emit(0, [same(couplings, range(6)) + same(adj, range(3))] * 3, buffers)
        for part, window, ours, theirs in ((1, mid_window, mid_around, mid_beside), (2, low_window, low_around, low_beside)):
            ends = []
            for a in (0, window.grid.depth - 1):
                lines = slice(a * window.line, (a + 1) * window.line)
                parts = [fold(jnp.concatenate([ours[c, lines, :], ours[c + 1, lines, :]])) for c in (0, 2, 4)]
                ends.append(jnp.concatenate(parts + [theirs[lines, :]]))
            late_round.put_rows(part, 0, *ends, buffers)

    buffers = call(
        late_kernel,
        (mark, adj_known, fine_couplings, mid_around, mid_beside, low_around, low_beside),
        late_round.buffers(),
    )
    late_got = swap(buffers, (0, 1))

    def window_kernel(mark, x, *rest):
        got, (x_out,) = rest[:swaps], rest[swaps:]
        x_out[...] = jnp.zeros(x_out.shape, F32)
        near, far = fifth_round.faces(0, got)
        mid_window.fill(x_out.at[0], x[...])
        mid_window.fill(x_out.at[1], beside_of(*near[2]))
        mid_window.fill(x_out.at[2], beside_of(*far[2]))
        for faces, step in ((near, 0), (far, 1)):
            for layer, value in zip((-1 - step, mid.depth + step), faces[0]):
                x_out[0, mid_window.layer(layer), :] = value
            for y, value in zip((-1 - step, mid.height + step), faces[1]):
                x_out[0, mid_window.row(y), :] = value

    (x_windows,) = call(window_kernel, (mark, x_mid, *fifth_got), [out(3, mid_window.rows, LANES)])

    last_rows, last_line = sizes[2] * sizes[1] * last_height, sizes[1] * last_height
    last_base = -(-(last_line + low_window.rim) // 8) * 8

    def solve_last(everyone, temp):
        channels = [[] for _ in range(2 * last_groups)]
        for first in range(0, sizes[0], last_groups):
            here = range(min(last_groups, sizes[0] - first))
            for g in here:
                for y in range(sizes[1]):
                    for z in range(sizes[2]):
                        sender = ((first + g) * sizes[1] + y) * sizes[2] + z
                        for half in range(2):
                            at = half * last_rows + z * last_line + y * last_height
                            start = keep + half * last_height
                            temp[g, at : at + last_height, :] = everyone[sender, start : start + last_height, :]
            parts = [temp[g] for g in here]
            group = lane_of(parts[0]) // last_width
            for q in range(last_groups):
                value = jnp.zeros_like(parts[0])
                for g in here:
                    value = jnp.where(group == g, roll(parts[g], last_width * (g - q), 1), value)
                channels[q].append(value[:last_rows])
                channels[last_groups + q].append(value[last_rows:])
        parts = [jnp.concatenate(tiles, axis=1) for tiles in channels[: last_groups + 4]]
        stencil, (inner, back, on, beside_y, beside_x) = parts[:7], parts[7:]
        y, x = row_y(inner, last_line), lane_of(inner)
        none = jnp.zeros((last_line, inner.shape[1]), F32)
        b = inner + jnp.concatenate([back[last_line:], none]) + jnp.concatenate([none, on[:-last_line]])
        b = b + jnp.where((y % last_height == 0) & (y > 0), roll(beside_y, 1, 0), 0.0)
        b = b + jnp.where((y % last_height == last_height - 1) & (y < last_line - 1), roll(beside_y, -1, 0), 0.0)
        b = b + jnp.where((x % last_width == 0) & (x > 0), roll(beside_x, 1, 1), 0.0)
        b = b + jnp.where((x % last_width == last_width - 1) & (x < inner.shape[1] - 1), roll(beside_x, -1, 1), 0.0)
        closed = Closed(last_line, 1)
        field = start = b * stencil[0]
        for sweep in range(COARSE_SWEEPS - 1):
            field = start + (1.0 - OMEGA) * field - off_apply(stencil, field, closed) * stencil[0]
        return field

    def spread_last(field, temp):
        gx, gy, gz = (lax.axis_index(name) for name in AXES)
        half, reach = low_window.line // 2, low_window.rim // 2
        layers = low.depth // 2 + 2
        dup = 2 * low.dup

        def taken(i, j):
            own = (j < LANES) & (i == gx * last_width + j // dup)
            before = (j >= LANES) & (j < LANES + low.dup) & (i == gx * last_width - 1)
            after = (j >= 2 * LANES - low.dup) & (i == (gx + 1) * last_width)
            return own | before | after

        at = last_base + (gz * (low.depth // 2) - 1) * last_line + gy * last_height - reach
        tiles = []
        for tile in range(0, field.shape[1], LANES):
            temp[12] = jnp.zeros(temp.shape[1:], F32)
            temp[12, last_base : last_base + last_rows, :] = field[:, tile : tile + LANES]
            tiles.append(jnp.concatenate([temp[12, pl.ds(at + k * last_line, half), :] for k in range(layers)]))
        both = matmul(jnp.concatenate(tiles, axis=1), one_hot((field.shape[1], 2 * LANES), taken))
        return [spread_rows(both[:, k * LANES : (k + 1) * LANES], layers, half, temp.at[13 + k]) for k in range(2)]

    def low_windows(everyone, temp, result):
        around = [(sy, sz) for sz in (-1, 0, 1) for sy in (-1, 0, 1)]
        per = -(-len(around) * keep // 8) * 8
        for k, sx in enumerate((0, -1, 1)):
            for i, (sy, sz) in enumerate(around):
                temp[k * per + keep * i : k * per + keep * (i + 1), :] = everyone[device(sx, sy, sz), 0:keep, :]
        packed = temp[: 3 * per, :]
        lane = lane_of(packed)
        turned = {by: roll(packed, by, 1) for by in range(1 - low.dup, low.dup)}
        for k in range(low.dup):
            value = turned[-k]
            for m in range(1, low.dup):
                value = jnp.where(lane % low.dup == m, turned[m - k], value)
            own, before, after = (value[i * per : (i + 1) * per] for i in range(3))
            forms = [own]
            for cells in (1, 2):
                forms.append(beside_of(roll(before, low.dup * cells, 1), roll(after, -low.dup * cells, 1)))
            for i, (sy, sz) in enumerate(around):
                for j in range(keep):
                    a, y = divmod(k * keep + j, low.height)
                    a, y = a + sz * low.depth, y + sy * low.height
                    if -2 <= a < low.depth + 2 and -low_window.rim <= y < low.height + low_window.rim:
                        at = low_window.at(a, y)
                        for form, source in enumerate(forms):
                            result[form, at : at + 1, :] = source[keep * i + j : keep * i + j + 1]
        return [result[form] for form in range(3)]

    def mid_edges(everyone, x):
        def lines(*steps):
            return everyone[device(*steps), own_at : own_at + 2, :]

        def unfolded(value, n):
            return jnp.concatenate([roll(value, -6 * k, 1) for k in range(n // 2)])

        def sides(values, k):
            return beside_of(roll(values[0], -2 * k, 1), roll(values[1], -2 * k - 2, 1))

        for sz in signs:
            a = -1 if sz < 0 else mid.depth
            for sy in signs:
                y = -1 if sy < 0 else mid.height
                got = lines(0, sy, sz)
                pair = unfold(got[:1])
                for layer, at, value in ((a, y, pair[:1]), (a + sz, y, pair[1:]), (a, y + sy, got[1:])):
                    row = mid_window.at(layer, at)
                    x[0, row : row + 1, :] = value
                row = mid_window.at(a, y)
                x[1, row : row + 1, :] = sides([lines(sx, sy, sz)[:1] for sx in signs], 0)
            got = [unfolded(lines(sx, 0, sz), mid.height) for sx in signs]
            x[1, mid_window.layer(a), :] = sides(got, 0)
            x[1, mid_window.layer(a + sz), :] = sides(got, 1)
            x[2, mid_window.layer(a), :] = sides(got, 2)
        for sy in signs:
            y = -1 if sy < 0 else mid.height
            got = [unfolded(lines(sx, sy, 0), mid.depth) for sx in signs]
            x[1, mid_window.row(y), :] = sides(got, 0)
            x[1, mid_window.row(y + sy), :] = sides(got, 1)
            x[2, mid_window.row(y), :] = sides(got, 2)

    def full(part, window, lines, side_lines, got):
        line, none = window.line, jnp.zeros((window.line, LANES), F32)
        ends = late_round.rows(part, 0, got)
        packed = jnp.concatenate([none, ends[0][3 * line :], side_lines[...], ends[1][3 * line :], none])

        def around(c):
            pair = slice(c // 2 * line, (c // 2 + 1) * line)
            own = slice(c % 2 * line, (c % 2 + 1) * line)
            return jnp.concatenate([none, unfold(ends[0][pair])[own], lines[c], unfold(ends[1][pair])[own], none])

        return around, lambda c: unpack_side(packed, c, window.grid.dup)

    def gradient_factors(mobility, pressure, trans, trans_before, *rest):
        got, (inner, layer_out, line_out, side_out, ends) = rest[:swaps], rest[swaps:]
        faces = third_round.faces(0, got, range(4, 8))
        rims = [Rim(fine, f, ends, c) for c, f in enumerate(faces)]
        lines = pl.ds(0, depth, stride=height)
        drops = []
        for dim in range(3):
            drops.append(0.25 * trans[dim] * (pressure[0] - rims[3].following(pressure[0], dim)))
        side_drop = 0.25 * trans_before[2] * (faces[3][2][0] - pressure[0])
        sides = []
        for c in range(3):
            value = mobility[c]
            for dim in range(3):
                inner[3 * dim + c] = drops[dim] * (value + rims[c].following(value, dim))
            drop = 0.25 * trans_before[0, :height, :] * (faces[3][0][0] - pressure[0, :height, :])
            layer_out[c] = drop * (faces[c][0][0] + mobility[c, :height, :])
            drop = 0.25 * trans_before[1, lines, :] * (faces[3][1][0] - pressure[0, lines, :])
            line_out[c] = drop * (faces[c][1][0] + mobility[c, lines, :])
            sides.append(side_drop * (faces[c][2][0] + value))
        side_out[...] = pack_sides(sides, 1)

    gradient_inputs = call(
        gradient_factors,
        (mobility, pressure, trans, trans_before, *third_got),
        [out(9, rows, LANES), out(3, height, LANES), out(3, depth, LANES), out(rows, LANES)],
        [(4, rows, LANES)],
    )

    def final_kernel(
        everyone,
        x_windows,
        mid_around,
        mid_beside,
        low_around,
        low_beside,
        adj_known,
        adj_factor,
        couplings,
        terms,
        layer_terms,
        line_terms,
        side_terms,
        *rest,
    ):
        late_got, third_got, fourth_got, fifth_got = (rest[max(0, k * swaps + late - swaps) : k * swaps + late] for k in range(4))
        rest = rest[3 * swaps + late :]
        adj_out, grad_out = rest[:2]
        last_temp, low_x, low_temp, x, temp, ends, around, beside, value_ref, adj, grad, sems = rest[2:]
        x[...] = x_windows[...]
        mid_edges(everyone, x)
        low_values = low_windows(everyone, low_temp, low_x)
        added = spread_last(solve_last(everyone, last_temp), temp)
        pair = full(2, low_window, low_around, low_beside, late_got)
        results = smooth(low_values, added, pair, low_window.line, low.dup)
        inner = slice(low_window.line, (low.depth + 3) * low_window.line)
        added = [spread_rows(v[inner], low.depth + 2, low_window.line, temp.at[10 + k]) for k, v in enumerate(results)]
        pair = full(1, mid_window, mid_around, mid_beside, late_got)
        beyond = late_round.faces(0, late_got)
        columns = fourth_round.columns(3, fourth_got) + third_round.columns(0, third_got, range(1, 4))
        columns += fifth_round.columns(1, fifth_got)
        factors = third_round.faces(0, third_got, range(1, 4))
        around[...], beside[...] = smooth([x[k] for k in range(3)], added, pair, mid_window.line, mid.dup)

        def own(ref, slot):
            lines = [ref[mid_window.layer(a), :] for a in range(mid.depth)]
            return spread_rows(jnp.concatenate(lines), mid.depth, mid.height, temp.at[slot])

        def layer(ref, a, slot):
            return spread_lines(ref[mid_window.layer(a), :], temp.at[slot])

        def lines(ref, y, slot):
            return spread_lines(ref[mid_window.row(y), :], temp.at[slot])

        def one_row(a, y):
            at = mid_window.at(a, y)
            return around[at : at + 1, :]

        value, side = own(around, 0), own(beside, 1)
        value_ref[...] = value
        layers = [(a, layer(around, a, k), layer(beside, a, k + 1)) for k, a in ((2, -1), (4, mid.depth))]
        rows_y = [(y, lines(around, y, k), lines(beside, y, k + 1)) for k, y in ((6, -1), (8, mid.height))]
        rim = Rim(fine, [[v[1] for v in layers], [v[1] for v in rows_y], (side, side)], ends, 0)

        def gain(value, shifts, coupling):
            total = (1.0 - OMEGA) * value
            for k in range(6):
                total = total - coupling(k) * shifts[k]
            return total

        shifts = [shift(value, dim) for dim in range(3) for shift in (rim.previous, rim.following)]
        own_gain = gain(value, shifts, lambda k: couplings[k])
        for c in range(3):
            adj[c] = adj_known[c] + adj_factor[c] * own_gain
        copies = [pltpu.make_async_copy(adj, adj_out, sems.at[3])]
        copies[0].start()

        def along_x(value, side):
            lane = lane_of(value)
            return [jnp.where(lane < 1, side, roll(value, 1, 1)), jnp.where(lane >= LANES - 1, side, roll(value, -1, 1))]

        def ended(value, low, high):
            row = lax.broadcasted_iota(jnp.int32, value.shape, 0)
            n = value.shape[0]
            return [jnp.where(row == 0, low, roll(value, 1, 0)), jnp.where(row == n - 1, high, roll(value, -1, 0))]

        layer_gains, line_gains = [], []
        for k, (a, here, there) in enumerate(layers):
            shifts = [here, value[:height]] if k == 0 else [value[rows - height :], here]
            shifts += ended(here, one_row(a, -1), one_row(a, mid.height)) + along_x(here, there)
            layer_gains.append(gain(here, shifts, lambda c: beyond[c][0][k]))
        for k, (y, here, there) in enumerate(rows_y):
            inside = value_ref[pl.ds(0 if k == 0 else height - 1, depth, stride=height), :]
            shifts = ended(here, one_row(-1, y), one_row(mid.depth, y))
            shifts += ([here, inside] if k == 0 else [inside, here]) + along_x(here, there)
            line_gains.append(gain(here, shifts, lambda c: beyond[c][1][k]))
        per = height // 4
        beside_column, own_column = pack_column(side), pack_column(value)
        lane, row = lane_of(own_column), lax.broadcasted_iota(jnp.int32, (8, LANES), 0)
        ends_z = [pack_column(v[2]) for v in layers]
        top = 2 * fine.groups - per
        shifts = [
            jnp.where(lane < per, ends_z[0], roll(beside_column, per, 1)),
            jnp.where(lane >= top, roll(ends_z[1], top, 1), roll(beside_column, -per, 1)),
        ]
        up, down = roll(beside_column, 1, 0), roll(beside_column, -1, 0)
        ends_y = [column_ends(rows_y[k][2], per, k == 1) for k in range(2)]
        shifts += [
            jnp.where(row > 0, up, jnp.where(lane % per < 2, ends_y[0], roll(up, 2, 1))),
            jnp.where(row < 7, down, jnp.where(lane % per >= per - 2, ends_y[1], roll(down, -2, 1))),
            jnp.where(lane % 2 == 1, beside_column, own_column),
            jnp.where(lane % 2 == 1, own_column, beside_column),
        ]
        side_gain = gain(beside_column, shifts, lambda c: columns[c])
        adj_rims = []
        for c in range(3):
            known, factor = beyond[6 + c], factors[c]
            faces = [[known[dim][k] + factor[dim][k] * gains[k] for k in range(2)] for dim, gains in enumerate((layer_gains, line_gains))]
            faces.append((unpack_column(columns[9 + c] + columns[6 + c] * side_gain, rows),) * 2)
            adj_rims.append(Rim(fine, faces, ends, 2 + c))
        values = [adj[c] for c in range(3)]
        lines = pl.ds(0, depth, stride=height)
        parts = []
        for c in range(3):
            layer, line, side = (adj_rims[c].faces[dim][0] for dim in range(3))
            parts.append(
                (
                    layer_terms[c] * (layer - values[c][:height]),
                    line_terms[c] * (line - adj[c, lines, :]),
                    unpack_side(side_terms[...], c, 1) * (side - values[c]),
                )
            )
        below = Rim(fine, [(sum(p[dim] for p in parts),) * 2 for dim in range(3)], ends, 5)
        for dim in range(3):
            here = 0.0
            for c in range(3):
                here = here + terms[3 * dim + c] * (values[c] - adj_rims[c].following(values[c], dim))
            grad[dim] = here + below.previous(here, dim)
            copies.append(pltpu.make_async_copy(grad.at[dim], grad_out.at[dim], sems.at[dim]))
            copies[-1].start()
        for copy in copies:
            copy.wait()

    adjoint, gradient = call(
        final_kernel,
        (everyone, x_windows, mid_around, mid_beside, low_around, low_beside)
        + (adj_known, adj_factor, fine_couplings, *gradient_inputs, *late_got, *third_got, *fourth_got, *fifth_got),
        [out(3, rows, LANES)] * 2,
        [
            (min(sizes[0], last_groups), 2 * last_rows, LANES),
            (3, low_window.rows, LANES),
            (max(low_window.rows, 96, 2 * last_base + last_rows), LANES),
            (3, mid_window.rows, LANES),
            (15, max(mid_window.rows, 2 * last_base + last_rows), LANES),
            (6, rows, LANES),
            (mid_window.rows, LANES),
            (mid_window.rows, LANES),
            (rows, LANES),
            (3, rows, LANES),
            (3, rows, LANES),
            pltpu.SemaphoreType.DMA((4,)),
        ],
        far_outputs=2,
    )
    shape = (3, depth, height, width)
    return adjoint.reshape(shape), gradient.reshape(shape)


def solution(mesh):
    cells = P("layer", "gy", "gx")
    fields = P(None, "layer", "gy", "gx")
    return jax.shard_map(
        local,
        mesh=mesh,
        in_specs=(
            fields,
            cells,
            fields,
            fields,
            fields,
            fields,
            fields,
            fields,
            fields,
            fields,
            cells,
            fields,
        ),
        out_specs=(fields, fields),
        check_vma=False,
    )
```
